32 devices in a mesh: grp: 4 (over z), tile: 8 (over y, x, core).
Axes of the slice: x: 2, y: 2, z: 4, core: 2. Of those that a mesh axis runs over, the one named last changes fastest.
Arguments:
- speed: float32 [32, 2, 32, 128], P('tile'), may hold values from 0.15 to 0.4
- density: float32 [32, 2, 32, 128], P('tile'), may hold values from 1 to 3
- fwd_state: bfloat16 [32, 4, 8, 32, 128], P(('grp', 'tile')), may hold values from -6 to 6
- adj_state: bfloat16 [32, 4, 8, 32, 128], P(('grp', 'tile')), may hold values from -6 to 6
- aperture: int32 [32, 4], P(('grp', 'tile')), may hold values from 0 to 31, as said below
- src_pos: int32 [32, 3], P(('grp', 'tile')), may hold values from 0 to 127, as said below
- wavelet: float32 [32, 4], P(('grp', 'tile')), may hold values from -15 to 15
- rec_pos: int32 [32, 8, 2], P(('grp', 'tile')), may hold values from 0 to 127, as said below
- residual: float32 [32, 4, 8], P(('grp', 'tile')), may hold values from -6 to 6
Outputs:
- grad_speed: float32 [32, 2, 32, 128], P('tile')
- grad_density: float32 [32, 2, 32, 128], P('tile')
The draws below stay inside these ranges and needn't reach their ends.
Inputs may be any that keep to these rules, and one draw needn't show every extreme that they name: `aperture`: row s is (c + j) * 4 + e for j = 0 .. 3, with one c in 0 .. 4 and one e in 0 .. 3 for each shot, so a shot takes exactly one tile from each of 4 owners. `src_pos`: columns are x in 0 .. 7, y in 0 .. 31, z in 0 .. 127. `rec_pos`: columns are y in 0 .. 31 and z in 0 .. 127.
All inputs are finite; a program needn't handle non-finite values.
Results may differ from the reference program's by a relative error of at most 0.0003.
Values sent between devices are 32-bit elements; how exact they have to be, the bound alone decides.
No kernel may reach another device: no remote copies, remote signals or barrier semaphores. Data moves between devices by JAX's collectives and lax.ppermute only.
A program may use at most 64 MiB of HBM per device.

```python
import math
import jax
import jax.numpy as jnp
from jax import lax

TX = 2
TY = 32
NZ = 128
TPD = 4
STEPS = 4
AX = 4
APX = 8
APY = 32
NREC = 8
NTILES = 32
SHOTS = 32
N_TILE = 8


def draw_aperture(key, part):
    corner_key, depth_key = jax.random.split(jax.random.fold_in(key, 11))
    corner = jax.random.randint(corner_key, (SHOTS, 1), 0, N_TILE - AX + 1)
    column = jax.random.randint(depth_key, (SHOTS, 1), 0, TPD)
    stripes = corner + jnp.arange(AX, dtype=jnp.int32)[None, :]
    return (stripes * TPD + column).astype(jnp.int32)


def draw_src_pos(key, part):
    upper = jnp.array([APX, APY, NZ], dtype=jnp.int32)
    return jax.random.randint(jax.random.fold_in(key, 23), (SHOTS, 3), 0, upper[None, :]).astype(jnp.int32)


def draw_rec_pos(key, part):
    upper = jnp.array([APY, NZ], dtype=jnp.int32)
    return jax.random.randint(jax.random.fold_in(key, 37), (SHOTS, NREC, 2), 0, upper[None, None, :]).astype(jnp.int32)


def block_scale(stream_key, dims, cuts, low, largest):
    loudness, own = 1.0, jax.random.fold_in(stream_key, 6)
    for position, blocks in cuts:
        draws = jnp.exp(jax.random.uniform(jax.random.fold_in(own, position), (blocks,), jnp.float32, low / len(cuts), largest / len(cuts)))
        loudness = loudness * jnp.repeat(draws, dims[position] // blocks).reshape([-1 if axis == position else 1 for axis in range(len(dims))])
    return loudness


def bell_draw(rng, shape, deviation, bound, cuts=(), kind=jnp.bfloat16):
    values = deviation * jax.random.normal(rng, shape, jnp.float32)
    if cuts:
        values = values * block_scale(rng, shape, cuts, -0.22, 0.18)
    return jnp.clip(values, -bound, bound).astype(kind)


def setup_inputs(seed: int = 0) -> dict:
    splits = jax.random.split(jax.random.key(seed), 10)
    return {
        "speed": jnp.clip(0.15 + 0.25 * jax.random.uniform(splits[0], (NTILES, TX, TY, NZ), jnp.float32) ** block_scale(splits[0], (NTILES, TX, TY, NZ), ((0, 8),), -0.2, 0.2), 0.15, 0.4),
        "density": jnp.clip(1.0 + 2.0 * jax.random.uniform(splits[1], (NTILES, TX, TY, NZ), jnp.float32) ** block_scale(splits[1], (NTILES, TX, TY, NZ), ((0, 8),), -0.2, 0.2), 1.0, 3.0),
        "fwd_state": bell_draw(splits[2], (SHOTS, 4, APX, APY, NZ), 1.0, 6.0, ((0, 32),)),
        "adj_state": bell_draw(splits[3], (SHOTS, 4, APX, APY, NZ), 1.0, 6.0, ((0, 32),)),
        "aperture": draw_aperture(jax.random.fold_in(splits[9], 71), 0),
        "src_pos": draw_src_pos(jax.random.fold_in(splits[9], 71), 0),
        "wavelet": bell_draw(splits[6], (SHOTS, STEPS), 3.0, 15.0, ((0, 32),), jnp.float32),
        "rec_pos": draw_rec_pos(jax.random.fold_in(splits[9], 71), 0),
        "residual": bell_draw(splits[8], (SHOTS, STEPS, NREC), 1.0, 6.0, ((0, 32),), jnp.float32),
    }


COEF = (1225.0 / 1024.0, -245.0 / 3072.0, 49.0 / 5120.0, -5.0 / 7168.0)

def padded_along(values, which_dim):
    widths = [(0, 0), (0, 0), (0, 0)]
    widths[which_dim] = (4, 4)
    return jnp.pad(values, widths)

def forward_diff(values, which_dim):
    length = values.shape[which_dim]
    padded = padded_along(values, which_dim)
    total = jnp.zeros_like(values)
    for order in range(1, 5):
        upper = lax.slice_in_dim(padded, 4 + order, 4 + order + length, axis=which_dim)
        lower = lax.slice_in_dim(padded, 5 - order, 5 - order + length, axis=which_dim)
        total = total + COEF[order - 1] * (upper - lower)
    return total

def backward_diff(values, which_dim):
    length = values.shape[which_dim]
    padded = padded_along(values, which_dim)
    total = jnp.zeros_like(values)
    for order in range(1, 5):
        upper = lax.slice_in_dim(padded, 3 + order, 3 + order + length, axis=which_dim)
        lower = lax.slice_in_dim(padded, 4 - order, 4 - order + length, axis=which_dim)
        total = total + COEF[order - 1] * (upper - lower)
    return total

def advance(pressure, velocity, bulk, buoyancy, source):
    moved = tuple((velocity[which_dim] + buoyancy * forward_diff(pressure, which_dim) for which_dim in range(3)))
    divergence = backward_diff(moved[0], 0) + backward_diff(moved[1], 1) + backward_diff(moved[2], 2)
    return (pressure + bulk * divergence + source, moved)

def evolve(speed_ap, density_ap, fwd_state, adj_state, src_pos, wavelet, rec_pos, residual):
    bulk = density_ap * speed_ap * speed_ap
    buoyancy = 1.0 / density_ap
    xs_cells = jnp.arange(speed_ap.shape[0], dtype=jnp.int32)
    ys_cells = jnp.arange(speed_ap.shape[1], dtype=jnp.int32)
    zs_cells = jnp.arange(speed_ap.shape[2], dtype=jnp.int32)
    src_mask = ((xs_cells == src_pos[0])[:, None, None] & (ys_cells == src_pos[1])[None, :, None] & (zs_cells == src_pos[2])[None, None, :]).astype(jnp.float32)
    rec_mask = ((ys_cells[None, :, None] == rec_pos[:, 0][:, None, None]) & (zs_cells[None, None, :] == rec_pos[:, 1][:, None, None])).astype(jnp.float32)
    state = fwd_state.astype(jnp.float32)
    pressure = state[0]
    velocity = (state[1], state[2], state[3])
    changes = []
    steps_count = wavelet.shape[0]
    for step_index in range(steps_count):
        new_pressure, new_velocity = advance(pressure, velocity, bulk, buoyancy, wavelet[step_index] * src_mask)
        changes.append((new_pressure - pressure, tuple((new_velocity[d] - velocity[d] for d in range(3)))))
        pressure, velocity = (new_pressure, new_velocity)
    adjoint = adj_state.astype(jnp.float32)
    adj_pressure = adjoint[0]
    adj_velocity = (adjoint[1], adjoint[2], adjoint[3])
    bulk_image = jnp.zeros_like(bulk)
    buoy_image = jnp.zeros_like(bulk)
    for step_index in reversed(range(steps_count)):
        adj_pressure, adj_velocity = advance(adj_pressure, adj_velocity, bulk, buoyancy, residual[step_index][:, None, None] * rec_mask)
        bulk_image = bulk_image + changes[step_index][0] * adj_pressure
        dvel = changes[step_index][1]
        buoy_image = buoy_image + dvel[0] * adj_velocity[0] + dvel[1] * adj_velocity[1] + dvel[2] * adj_velocity[2]
    return (bulk_image, buoy_image)

def reference(speed, density, fwd_state, adj_state, aperture, src_pos, wavelet, rec_pos, residual):

    def one_shot(carry, inputs):
        fwd_one, adj_one, tiles_one, src_one, wave_one, recs_one, resid_one = inputs
        speed_ap = speed[tiles_one].reshape(AX * TX, TY, NZ)
        density_ap = density[tiles_one].reshape(AX * TX, TY, NZ)
        bulk_image, buoy_image = evolve(speed_ap, density_ap, fwd_one, adj_one, src_one, wave_one, recs_one, resid_one)
        bulk_acc = carry[0].at[tiles_one].add(bulk_image.reshape(AX, TX, TY, NZ))
        buoy_acc = carry[1].at[tiles_one].add(buoy_image.reshape(AX, TX, TY, NZ))
        return ((bulk_acc, buoy_acc), None)
    zeros = jnp.zeros(speed.shape, jnp.float32)
    (bulk_sum, buoy_sum), _ = lax.scan(one_shot, (zeros, zeros), (fwd_state, adj_state, aperture, src_pos, wavelet, rec_pos, residual))
    scale = 1.0 / math.sqrt(SHOTS)
    grad_speed = scale * (bulk_sum * (2.0 * density * speed))
    grad_density = scale * (bulk_sum * (speed * speed) - buoy_sum / (density * density))
    return (grad_speed, grad_density)
```

```python
import math

import jax
import jax.numpy as jnp
from jax import lax
from jax.sharding import PartitionSpec as P

COEF = (1225.0 / 1024.0, -245.0 / 3072.0, 49.0 / 5120.0, -5.0 / 7168.0)


def padded_along(values, which_dim):
    widths = [(0, 0), (0, 0), (0, 0)]
    widths[which_dim] = (4, 4)
    return jnp.pad(values, widths)


def forward_diff(values, which_dim):
    length = values.shape[which_dim]
    padded = padded_along(values, which_dim)
    total = jnp.zeros_like(values)
    for order in range(1, 5):
        upper = lax.slice_in_dim(padded, 4 + order, 4 + order + length, axis=which_dim)
        lower = lax.slice_in_dim(padded, 5 - order, 5 - order + length, axis=which_dim)
        total = total + COEF[order - 1] * (upper - lower)
    return total


def backward_diff(values, which_dim):
    length = values.shape[which_dim]
    padded = padded_along(values, which_dim)
    total = jnp.zeros_like(values)
    for order in range(1, 5):
        upper = lax.slice_in_dim(padded, 3 + order, 3 + order + length, axis=which_dim)
        lower = lax.slice_in_dim(padded, 4 - order, 4 - order + length, axis=which_dim)
        total = total + COEF[order - 1] * (upper - lower)
    return total


def advance(pressure, velocity, bulk, buoyancy, source):
    moved = tuple(
        (
            velocity[which_dim] + buoyancy * forward_diff(pressure, which_dim)
            for which_dim in range(3)
        )
    )
    divergence = (
        backward_diff(moved[0], 0) + backward_diff(moved[1], 1) + backward_diff(moved[2], 2)
    )
    return (pressure + bulk * divergence + source, moved)


def evolve(speed_ap, density_ap, fwd_state, adj_state, src_pos, wavelet, rec_pos, residual):
    bulk = density_ap * speed_ap * speed_ap
    buoyancy = 1.0 / density_ap
    xs_cells = jnp.arange(speed_ap.shape[0], dtype=jnp.int32)
    ys_cells = jnp.arange(speed_ap.shape[1], dtype=jnp.int32)
    zs_cells = jnp.arange(speed_ap.shape[2], dtype=jnp.int32)
    src_mask = (
        (xs_cells == src_pos[0])[:, None, None]
        & (ys_cells == src_pos[1])[None, :, None]
        & (zs_cells == src_pos[2])[None, None, :]
    ).astype(jnp.float32)
    rec_mask = (
        (ys_cells[None, :, None] == rec_pos[:, 0][:, None, None])
        & (zs_cells[None, None, :] == rec_pos[:, 1][:, None, None])
    ).astype(jnp.float32)
    state = fwd_state.astype(jnp.float32)
    pressure = state[0]
    velocity = (state[1], state[2], state[3])
    changes = []
    steps_count = wavelet.shape[0]
    for step_index in range(steps_count):
        new_pressure, new_velocity = advance(
            pressure, velocity, bulk, buoyancy, wavelet[step_index] * src_mask
        )
        changes.append(
            (new_pressure - pressure, tuple((new_velocity[d] - velocity[d] for d in range(3))))
        )
        pressure, velocity = (new_pressure, new_velocity)
    adjoint = adj_state.astype(jnp.float32)
    adj_pressure = adjoint[0]
    adj_velocity = (adjoint[1], adjoint[2], adjoint[3])
    bulk_image = jnp.zeros_like(bulk)
    buoy_image = jnp.zeros_like(bulk)
    for step_index in reversed(range(steps_count)):
        adj_pressure, adj_velocity = advance(
            adj_pressure,
            adj_velocity,
            bulk,
            buoyancy,
            residual[step_index][:, None, None] * rec_mask,
        )
        bulk_image = bulk_image + changes[step_index][0] * adj_pressure
        dvel = changes[step_index][1]
        buoy_image = (
            buoy_image
            + dvel[0] * adj_velocity[0]
            + dvel[1] * adj_velocity[1]
            + dvel[2] * adj_velocity[2]
        )
    return (bulk_image, buoy_image)


def per_device(speed, density, fwd_state, adj_state, aperture, src_pos, wavelet, rec_pos, residual):
    owners = lax.axis_size("tile")
    groups = lax.axis_size("grp")
    myself = lax.axis_index("tile")
    my_group = lax.axis_index("grp")
    held = speed.shape[0]
    tile_x, tile_y, depth = (speed.shape[1], speed.shape[2], speed.shape[3])
    stripes = aperture.shape[1]
    mine = aperture[0]
    lists = lax.all_gather(aperture, "tile", axis=0, tiled=True)
    column = lists[:, 0] % held
    first = lists[:, 0] // held
    wanted = (first <= myself) & (myself < first + stripes)
    model = jnp.stack([speed, density], axis=1)
    out_tiles = jnp.take(model, column, axis=0)
    came = lax.all_to_all(out_tiles, "tile", split_axis=0, concat_axis=0, tiled=True)
    corner = mine[0] // held
    aper = lax.dynamic_slice_in_dim(came, corner, stripes, axis=0)
    speed_ap = aper[:, 0].reshape(stripes * tile_x, tile_y, depth)
    density_ap = aper[:, 1].reshape(stripes * tile_x, tile_y, depth)
    bulk_image, buoy_image = evolve(
        speed_ap,
        density_ap,
        fwd_state[0],
        adj_state[0],
        src_pos[0],
        wavelet[0],
        rec_pos[0],
        residual[0],
    )
    images = jnp.stack(
        [
            bulk_image.reshape(stripes, tile_x, tile_y, depth),
            buoy_image.reshape(stripes, tile_x, tile_y, depth),
        ],
        axis=1,
    )
    back = lax.dynamic_update_slice_in_dim(
        jnp.zeros((owners, 2, tile_x, tile_y, depth), jnp.float32), images, corner, axis=0
    )
    got = lax.all_to_all(back, "tile", split_axis=0, concat_axis=0, tiled=True)
    picked = (
        wanted[None, :] & (column[None, :] == jnp.arange(held, dtype=jnp.int32)[:, None])
    )
    own = jnp.sum(
        jnp.where(picked[:, :, None, None, None, None], got[None], 0.0), axis=1
    )
    rows = held * tile_x * tile_y
    part = rows // groups
    chunks = own.transpose(1, 0, 2, 3, 4).reshape(2, groups, part, depth)

    def chunk_of(values, index):
        return lax.dynamic_index_in_dim(values, index % groups, axis=values.ndim - 3, keepdims=False)

    total = chunk_of(chunks, my_group)
    for hop in range(1, groups):
        pairs = [(g, (g + hop) % groups) for g in range(groups)]
        total = total + lax.ppermute(chunk_of(chunks, my_group + hop), "grp", pairs)
    my_speed = chunk_of(speed.reshape(groups, part, depth), my_group)
    my_density = chunk_of(density.reshape(groups, part, depth), my_group)
    scale = 1.0 / math.sqrt(groups * owners)
    grads = jnp.stack(
        [
            scale * (total[0] * (2.0 * my_density * my_speed)),
            scale * (total[0] * (my_speed * my_speed) - total[1] / (my_density * my_density)),
        ]
    )
    whole = jnp.zeros((2, groups, part, depth), jnp.float32)
    whole = lax.dynamic_update_slice_in_dim(whole, grads[:, None], my_group, axis=1)
    for hop in range(1, groups):
        pairs = [(g, (g + hop) % groups) for g in range(groups)]
        came_grads = lax.ppermute(grads, "grp", pairs)
        whole = lax.dynamic_update_slice_in_dim(
            whole, came_grads[:, None], (my_group - hop) % groups, axis=1
        )
    return (whole[0].reshape(speed.shape), whole[1].reshape(speed.shape))


def solution(mesh):
    return jax.shard_map(
        per_device,
        mesh=mesh,
        in_specs=(
            P("tile", None, None, None),
            P("tile", None, None, None),
            P(("grp", "tile"), None, None, None, None),
            P(("grp", "tile"), None, None, None, None),
            P(("grp", "tile"), None),
            P(("grp", "tile"), None),
            P(("grp", "tile"), None),
            P(("grp", "tile"), None, None),
            P(("grp", "tile"), None, None),
        ),
        out_specs=(P("tile", None, None, None), P("tile", None, None, None)),
        check_vma=False,
    )
```

```python
import functools
import math

import jax
import jax.numpy as jnp
from jax import lax
from jax.experimental import pallas as pl
from jax.experimental.pallas import tpu as pltpu
from jax.sharding import PartitionSpec as P

COEF = (1225.0 / 1024.0, -245.0 / 3072.0, 49.0 / 5120.0, -5.0 / 7168.0)
REACH = 4
EDGE = 8

VMEM = pl.BlockSpec(memory_space=pltpu.VMEM)
SMEM = pl.BlockSpec(memory_space=pltpu.SMEM)
PARAMS = pltpu.CompilerParams(vmem_limit_bytes=40 * 1024 * 1024)


def corner_and_column(list_ref, held):
    entry = list_ref[0, 0]
    return lax.div(entry, held), lax.rem(entry, held)


def pick_kernel(stripes, speed_ref, density_ref, far_speed_ref, far_density_ref, *refs):
    lists, pieces, rows = refs[:stripes], refs[stripes : 2 * stripes], refs[2 * stripes]
    held = speed_ref.shape[0]
    me = lax.axis_index("tile")
    residue, half = lax.rem(me, stripes), lax.div(me, stripes)
    for hop in range(stripes):
        corner, column = corner_and_column(lists[hop], held)
        here = (residue >= corner) == (half == 0)
        piece = pieces[hop]
        rows[hop, 0] = corner
        rows[hop, 1] = column

        @pl.when(here)
        def _():
            piece[0] = speed_ref[column]
            piece[1] = density_ref[column]

        @pl.when(jnp.logical_not(here))
        def _():
            piece[0] = far_speed_ref[column]
            piece[1] = far_density_ref[column]


def combine(ahead, behind):
    total = None
    for order in range(1, 5):
        term = COEF[order - 1] * (ahead(order) - behind(order))
        total = term if total is None else total + term
    return total


def shifted_z(values, lane, by):
    if by == 0:
        return values
    depth = values.shape[-1]
    rolled = pltpu.roll(values, (-by) % depth, axis=values.ndim - 1)
    inside = lane < depth - by if by > 0 else lane >= -by
    return jnp.where(inside, rolled, 0.0)


def wave_kernel(stripes, steps, held, *refs):
    pieces = refs[:stripes]
    (fwd_ref, adj_ref, list_ref, src_ref, wave_ref, rec_ref, res_ref) = refs[stripes : stripes + 7]
    owners = 2 * stripes
    outs = refs[stripes + 7 : stripes + 7 + owners]
    (bulk, buoy, p, v0, v1, v2, dp, dv, marks, bulk_img, buoy_img) = refs[stripes + 7 + owners :]
    tile_x = pieces[0].shape[1]
    xs, ys, zs = bulk.shape
    me = lax.axis_index("tile")
    residue = lax.rem(me, stripes)
    corner, _ = corner_and_column(list_ref, held)
    for hop in range(stripes):
        place = lax.rem((residue ^ hop) - corner + stripes, stripes)
        cells = pl.ds(place * tile_x, tile_x)
        speed, density = pieces[hop][0], pieces[hop][1]
        bulk[cells] = density * speed * speed
        buoy[cells] = 1.0 / density

    row = lax.broadcasted_iota(jnp.int32, (ys, zs), 0)
    lane = lax.broadcasted_iota(jnp.int32, (ys, zs), 1)
    src_mark = ((row == src_ref[0, 1]) & (lane == src_ref[0, 2])).astype(jnp.float32)
    for x in range(xs):
        marks[x] = ((row == rec_ref[0, x, 0]) & (lane == rec_ref[0, x, 1])).astype(jnp.float32)

    edge = jnp.zeros((REACH, ys + 2 * EDGE, zs), jnp.float32)
    p[:REACH] = edge
    p[REACH + xs :] = edge
    side = jnp.zeros((xs, EDGE, zs), jnp.float32)
    p[REACH : REACH + xs, :EDGE] = side
    p[REACH : REACH + xs, EDGE + ys :] = side
    v1[:, :EDGE] = side
    v1[:, EDGE + ys :] = side
    v0[:REACH] = edge[:, :ys]
    v0[REACH + xs :] = edge[:, :ys]
    middle = pl.ds(EDGE, ys)

    def load(state):
        for x in range(xs):
            p[REACH + x, EDGE : EDGE + ys] = state[0, 0, x].astype(jnp.float32)
            v0[REACH + x] = state[0, 1, x].astype(jnp.float32)
            v1[x, EDGE : EDGE + ys] = state[0, 2, x].astype(jnp.float32)
            v2[x] = state[0, 3, x].astype(jnp.float32)

    def slopes(x):
        centre = p[REACH + x, middle]
        along_x = combine(
            lambda k: p[REACH + x + k, middle], lambda k: p[REACH + x + 1 - k, middle]
        )
        along_y = combine(
            lambda k: p[REACH + x, pl.ds(EDGE + k, ys)],
            lambda k: p[REACH + x, pl.ds(EDGE + 1 - k, ys)],
        )
        along_z = combine(
            lambda k: shifted_z(centre, lane, k), lambda k: shifted_z(centre, lane, 1 - k)
        )
        light = buoy[x]
        return light * along_x, light * along_y, light * along_z

    def push(x):
        change = slopes(x)
        moved = (
            v0[REACH + x] + change[0],
            v1[x, middle] + change[1],
            v2[x] + change[2],
        )
        v0[REACH + x] = moved[0]
        v1[x, middle] = moved[1]
        v2[x] = moved[2]
        return change, moved

    def spread(x):
        along_x = combine(lambda k: v0[REACH + x + k - 1], lambda k: v0[REACH + x - k])
        along_y = combine(
            lambda k: v1[x, pl.ds(EDGE + k - 1, ys)], lambda k: v1[x, pl.ds(EDGE - k, ys)]
        )
        centre = v2[x]
        along_z = combine(
            lambda k: shifted_z(centre, lane, k - 1), lambda k: shifted_z(centre, lane, -k)
        )
        return bulk[x] * (along_x + along_y + along_z)

    def planes(body):
        lax.fori_loop(0, xs, lambda x, _: (body(x), 0)[1], 0, unroll=2)

    load(fwd_ref)
    for step in range(steps):

        def fwd_push(x, step=step):
            change, _ = push(x)
            for d in range(3):
                dv[step, d, x] = change[d]

        def fwd_spread(x, step=step):
            amplitude = jnp.where(x == src_ref[0, 0], wave_ref[0, step], 0.0)
            change = spread(x) + amplitude * src_mark
            dp[step, x] = change
            p[REACH + x, middle] = p[REACH + x, middle] + change

        planes(fwd_push)
        planes(fwd_spread)

    load(adj_ref)
    for step in reversed(range(steps)):
        last = step == steps - 1

        def adj_push(x, step=step, last=last):
            _, moved = push(x)
            image = dv[step, 0, x] * moved[0]
            image = image + dv[step, 1, x] * moved[1]
            image = image + dv[step, 2, x] * moved[2]
            buoy_img[x] = image if last else buoy_img[x] + image

        def adj_spread(x, step=step, last=last):
            moved = p[REACH + x, middle] + spread(x) + res_ref[0, step, x] * marks[x]
            p[REACH + x, middle] = moved
            image = dp[step, x] * moved
            bulk_img[x] = image if last else bulk_img[x] + image

        planes(adj_push)
        planes(adj_spread)

    for hop in range(owners):
        place = jnp.clip((me ^ hop) - corner, 0, stripes - 1)
        cells = pl.ds(place * tile_x, tile_x)
        outs[hop][0] = bulk_img[cells]
        outs[hop][1] = buoy_img[cells]


def gather_kernel(stripes, groups, near_ref, far_ref, *refs):
    owners = 2 * stripes
    came, parts, total = refs[:owners], refs[owners : owners + groups], refs[owners + groups]
    me, group = lax.axis_index("tile"), lax.axis_index("grp")
    tile_rows = came[0].shape[1]
    part = parts[0].shape[1]
    total[...] = jnp.zeros_like(total)
    for hop in range(owners):
        lists = near_ref if hop < stripes else far_ref
        corner, column = lists[hop % stripes, 0], lists[hop % stripes, 1]

        @pl.when((corner <= me) & (me < corner + stripes))
        def _():
            rows = pl.ds(pl.multiple_of(column * tile_rows, tile_rows), tile_rows)
            for field in range(2):
                total[field, rows] = total[field, rows] + came[hop][field]

    for hop in range(groups):
        first = pl.multiple_of(lax.rem(group + hop, groups) * part, part)
        for field in range(2):
            parts[hop][field] = total[field, pl.ds(first, part)]


def grads_kernel(scale, groups, *refs):
    parts, speed_ref, density_ref, grads = refs[:groups], *refs[groups:]
    part = parts[0].shape[1]
    rows = pl.ds(pl.multiple_of(lax.axis_index("grp") * part, part), part)
    speed, density = speed_ref[rows], density_ref[rows]
    bulk_sum, buoy_sum = parts[0][0], parts[0][1]
    for other in parts[1:]:
        bulk_sum = bulk_sum + other[0]
        buoy_sum = buoy_sum + other[1]
    grads[0] = scale * (bulk_sum * (2.0 * density * speed))
    grads[1] = scale * (bulk_sum * (speed * speed) - buoy_sum / (density * density))


def per_device(speed, density, fwd_state, adj_state, aperture, src_pos, wavelet, rec_pos, residual):
    owners = lax.axis_size("tile")
    groups = lax.axis_size("grp")
    my_group = lax.axis_index("grp")
    held, tile_x, tile_y, depth = speed.shape
    stripes = aperture.shape[1]
    steps = wavelet.shape[1]
    xs = stripes * tile_x
    f32 = jnp.float32

    def across(values, hop):
        return lax.ppermute(values, "tile", [(t, t ^ hop) for t in range(owners)])

    lists = [aperture] + [across(aperture, hop) for hop in range(1, stripes)]
    far_speed = across(speed, stripes)
    far_density = across(density, stripes)
    piece = jax.ShapeDtypeStruct((2, tile_x, tile_y, depth), f32)
    picked = pl.pallas_call(
        functools.partial(pick_kernel, stripes),
        out_shape=[piece] * stripes + [jax.ShapeDtypeStruct((stripes, 2), jnp.int32)],
        in_specs=[VMEM] * 4 + [SMEM] * stripes,
        out_specs=[VMEM] * stripes + [SMEM],
        compiler_params=PARAMS,
        name="pick_tiles",
    )(speed, density, far_speed, far_density, *lists)
    near = picked[-1]
    pieces = [picked[0]] + [across(picked[hop], hop) for hop in range(1, stripes)]
    far = across(near, stripes)

    cells = (xs, tile_y, depth)
    images = pl.pallas_call(
        functools.partial(wave_kernel, stripes, steps, held),
        out_shape=[piece] * owners,
        in_specs=[VMEM] * (stripes + 2) + [SMEM] * 5,
        out_specs=[VMEM] * owners,
        scratch_shapes=[
            pltpu.VMEM(cells, f32),
            pltpu.VMEM(cells, f32),
            pltpu.VMEM((xs + 2 * REACH, tile_y + 2 * EDGE, depth), f32),
            pltpu.VMEM((xs + 2 * REACH, tile_y, depth), f32),
            pltpu.VMEM((xs, tile_y + 2 * EDGE, depth), f32),
            pltpu.VMEM(cells, f32),
            pltpu.VMEM((steps,) + cells, f32),
            pltpu.VMEM((steps, 3) + cells, f32),
            pltpu.VMEM(cells, f32),
            pltpu.VMEM(cells, f32),
            pltpu.VMEM(cells, f32),
        ],
        compiler_params=PARAMS,
        name="replay_and_adjoint",
    )(*pieces, fwd_state, adj_state, aperture, src_pos, wavelet, rec_pos, residual)

    tile_rows = tile_x * tile_y
    rows = held * tile_rows
    part = rows // groups
    came = [images[0]] + [across(images[hop], hop) for hop in range(1, owners)]
    came = [values.reshape(2, tile_rows, depth) for values in came]
    part_shape = jax.ShapeDtypeStruct((2, part, depth), f32)
    parts = pl.pallas_call(
        functools.partial(gather_kernel, stripes, groups),
        out_shape=[part_shape] * groups,
        in_specs=[SMEM] * 2 + [VMEM] * owners,
        out_specs=[VMEM] * groups,
        scratch_shapes=[pltpu.VMEM((2, rows, depth), f32)],
        compiler_params=PARAMS,
        name="add_stripes",
    )(near, far, *came)

    def along(values, hop):
        return lax.ppermute(values, "grp", [(g, (g + hop) % groups) for g in range(groups)])

    parts = [parts[0]] + [along(parts[hop], hop) for hop in range(1, groups)]
    grads = pl.pallas_call(
        functools.partial(grads_kernel, 1.0 / math.sqrt(groups * owners), groups),
        out_shape=part_shape,
        in_specs=[VMEM] * (groups + 2),
        out_specs=VMEM,
        compiler_params=PARAMS,
        name="gradients",
    )(*parts, speed.reshape(rows, depth), density.reshape(rows, depth))

    whole = jnp.zeros((2, groups, part, depth), f32)
    for hop in range(groups):
        values = grads if hop == 0 else along(grads, hop)
        place = lax.rem(my_group - hop + groups, groups)
        whole = lax.dynamic_update_slice_in_dim(whole, values[:, None], place, axis=1)
    return (whole[0].reshape(speed.shape), whole[1].reshape(speed.shape))


def solution(mesh):
    return jax.shard_map(
        per_device,
        mesh=mesh,
        in_specs=(
            P("tile", None, None, None),
            P("tile", None, None, None),
            P(("grp", "tile"), None, None, None, None),
            P(("grp", "tile"), None, None, None, None),
            P(("grp", "tile"), None),
            P(("grp", "tile"), None),
            P(("grp", "tile"), None),
            P(("grp", "tile"), None, None),
            P(("grp", "tile"), None, None),
        ),
        out_specs=(P("tile", None, None, None), P("tile", None, None, None)),
        check_vma=False,
    )
```

```python
import functools
import math

import jax
import jax.numpy as jnp
from jax import lax
from jax.experimental import pallas as pl
from jax.experimental.pallas import tpu as pltpu
from jax.sharding import PartitionSpec as P

COEF = (1225.0 / 1024.0, -245.0 / 3072.0, 49.0 / 5120.0, -5.0 / 7168.0)
REACH = 4
EDGE = 8
ROWS = 8
SPAN = 8

VMEM = pl.BlockSpec(memory_space=pltpu.VMEM)
SMEM = pl.BlockSpec(memory_space=pltpu.SMEM)
PARAMS = pltpu.CompilerParams(vmem_limit_bytes=36 * 1024 * 1024)


def entry_of(list_ref):
    return jnp.max(list_ref[0:1, 0:1].astype(jnp.float32)).astype(jnp.int32)


def combine(ahead, behind):
    total = None
    for order in range(1, 5):
        upper, lower, weight = ahead(order), behind(order), COEF[order - 1]
        if upper is None and lower is None:
            continue
        if lower is None:
            term = weight * upper
        elif upper is None:
            term = -weight * lower
        else:
            term = weight * (upper - lower)
        total = term if total is None else total + term
    return total


def along_z(values, first):
    depth = values.shape[-1]
    lane = lax.broadcasted_iota(jnp.int32, values.shape, values.ndim - 1)

    def at(by):
        if by == 0:
            return values
        rolled = pltpu.roll(values, (-by) % depth, axis=values.ndim - 1)
        return jnp.where(lane < depth - by if by > 0 else lane >= -by, rolled, 0.0)

    return combine(lambda k: at(first + k - 1), lambda k: at(first - k))


def clear_edges(xs, ys, p, v0=None, v1=None):
    def zeros(ref):
        ref[...] = jnp.zeros(ref.shape, jnp.float32)

    for ref in (p, v0):
        if ref is not None and xs > SPAN:
            zeros(ref.at[:REACH])
            zeros(ref.at[REACH + xs :])
    for ref, inner in ((p, pl.ds(REACH, xs)), (v1, slice(None))):
        if ref is not None:
            zeros(ref.at[inner, :EDGE])
            zeros(ref.at[inner, EDGE + ys :])


def blocks(xs, ys, body):
    if xs <= SPAN:
        for y0 in range(0, ys, ROWS):
            body(0, xs, y0)
        return

    def span(index, _):
        for y0 in range(0, ys, ROWS):
            body(index * SPAN, SPAN, y0)
        return 0

    lax.fori_loop(0, xs // SPAN, span, 0)


def window(xs, x0, load):
    kept = {}

    def at(offset):
        if xs <= SPAN and not 0 <= offset < xs:
            return None
        if offset not in kept:
            kept[offset] = load(x0 + offset)
        return kept[offset]

    return at


def slopes(xs, p, x0, y0, plane, offset):
    centre = plane(offset)
    here = x0 + offset + REACH
    return (
        combine(lambda k: plane(offset + k), lambda k: plane(offset + 1 - k)),
        combine(
            lambda k: p[here, pl.ds(EDGE + y0 + k, ROWS)],
            lambda k: centre if k == 1 else p[here, pl.ds(EDGE + y0 + 1 - k, ROWS)],
        ),
        along_z(centre, 1),
    )


def prepare_kernel(
    steps, speed, density, fwd, adj, ap, src, wave, rec, res,
    near_speed, near_density, fwd_slope, adj_slope, fwd_source, adj_source, entry, p, q,
):
    xs, ys, zs = fwd_slope.shape[1:]
    near_speed[...] = speed[...]
    near_density[...] = density[...]
    entry[...] = jnp.full(entry.shape, ap[0, 0], jnp.int32)
    row = lax.broadcasted_iota(jnp.int32, (ys, zs), 0)
    lane = lax.broadcasted_iota(jnp.int32, (ys, zs), 1)

    for field, state, slope in ((p, fwd, fwd_slope), (q, adj, adj_slope)):
        clear_edges(xs, ys, field)
        for x in range(xs):
            field[REACH + x, EDGE : EDGE + ys] = state[0, 0, x].astype(jnp.float32)

        def block(x0, count, y0, field=field, slope=slope):
            plane = window(xs, x0, lambda x: field[REACH + x, pl.ds(EDGE + y0, ROWS)])
            for offset in range(count):
                three = slopes(xs, field, x0, y0, plane, offset)
                for d in range(3):
                    slope[d, x0 + offset, pl.ds(y0, ROWS)] = three[d]

        blocks(xs, ys, block)

    src_mark = (row == src[0, 1]) & (lane == src[0, 2])
    for x in range(xs):
        rec_mark = (row == rec[0, x, 0]) & (lane == rec[0, x, 1])
        for step in range(steps):
            amplitude = jnp.where(x == src[0, 0], wave[0, step], 0.0)
            fwd_source[step, x] = jnp.where(src_mark, amplitude, 0.0)
            adj_source[step, x] = jnp.where(rec_mark, res[0, step, x], 0.0)


def pick_kernel(chips, near_speed, near_density, far_speed, far_density, *refs):
    stripes = 2 * chips
    lists, outs = refs[:stripes], refs[stripes:]
    held = near_speed.shape[0]
    me = lax.axis_index("tile")
    residue, half = lax.rem(me, stripes), lax.div(me, stripes)
    for hop in range(stripes):
        entry = entry_of(lists[hop])
        corner, column = lax.div(entry, held), lax.rem(entry, held)
        here = (residue >= corner) == (half == 0)
        piece = outs[hop] if hop < 2 else outs[1 + hop // 2].at[hop % 2]

        @pl.when(here)
        def _():
            piece[0] = near_speed[column]
            piece[1] = near_density[column]

        @pl.when(jnp.logical_not(here))
        def _():
            piece[0] = far_speed[column]
            piece[1] = far_density[column]


def wave_kernel(chips, steps, held, *refs):
    stripes = 2 * chips
    own, beside, pairs, passed = refs[0], refs[1], refs[2 : chips + 1], refs[chips + 1 : stripes]
    fwd, adj, fwd_slope, adj_slope, fwd_source, adj_source, entry_ref = refs[stripes : stripes + 7]
    kept, traded = refs[stripes + 7 : stripes + 9]
    bulk, buoy, p, v0, v1, v2, q, w0, w1, w2, dp, dv, bulk_img, buoy_img = refs[stripes + 9 :]
    tile_x, tile_y = own.shape[1:3]
    xs, ys, zs = bulk.shape
    residue = lax.rem(lax.axis_index("tile"), stripes)
    entry = entry_of(entry_ref)
    corner = lax.div(entry, held)

    def place_of(hop):
        return lax.rem((residue ^ hop) - corner + stripes, stripes) * tile_x

    for hop in range(stripes):
        if hop < 2:
            piece = (own, beside)[hop]
        else:
            piece = pairs[hop // 2 - 1].at[0] if hop % 2 == 0 else passed[hop // 2 - 1]
        cells = pl.ds(place_of(hop), tile_x)
        speed, density = piece[0], piece[1]
        bulk[cells] = density * speed * speed
        buoy[cells] = 1.0 / density

    for state, fields in ((fwd, (p, v0, v1, v2)), (adj, (q, w0, w1, w2))):
        clear_edges(xs, ys, *fields[:3])
        for x in range(xs):
            fields[0][REACH + x, EDGE : EDGE + ys] = state[0, 0, x].astype(jnp.float32)
            fields[1][REACH + x] = state[0, 1, x].astype(jnp.float32)
            fields[2][x, EDGE : EDGE + ys] = state[0, 2, x].astype(jnp.float32)
            fields[3][x] = state[0, 3, x].astype(jnp.float32)

    def push(fields, first, note):
        p, v0, v1, v2 = fields

        def block(x0, count, y0):
            rows, inner = pl.ds(y0, ROWS), pl.ds(EDGE + y0, ROWS)
            plane = window(xs, x0, lambda x: p[REACH + x, inner])
            for offset in range(count):
                x = x0 + offset
                if first is None:
                    three = slopes(xs, p, x0, y0, plane, offset)
                else:
                    three = tuple(first[d, x, rows] for d in range(3))
                light = buoy[x, rows]
                change = tuple(light * slope for slope in three)
                moved = (
                    v0[REACH + x, rows] + change[0],
                    v1[x, inner] + change[1],
                    v2[x, rows] + change[2],
                )
                v0[REACH + x, rows] = moved[0]
                v1[x, inner] = moved[1]
                v2[x, rows] = moved[2]
                note(x, rows, change, moved)

        blocks(xs, ys, block)

    def spread(fields, source, step, note):
        p, v0, v1, v2 = fields

        def block(x0, count, y0):
            rows, inner = pl.ds(y0, ROWS), pl.ds(EDGE + y0, ROWS)
            plane = window(xs, x0, lambda x: v0[REACH + x, rows])
            for offset in range(count):
                x = x0 + offset
                along_x = combine(lambda k: plane(offset + k - 1), lambda k: plane(offset - k))
                along_y = combine(
                    lambda k: v1[x, pl.ds(EDGE + y0 + k - 1, ROWS)],
                    lambda k: v1[x, pl.ds(EDGE + y0 - k, ROWS)],
                )
                total = along_x + along_y + along_z(v2[x, rows], 0)
                change = bulk[x, rows] * total + source[step, x, rows]
                moved = p[REACH + x, inner] + change
                p[REACH + x, inner] = moved
                note(x, rows, change, moved)

        blocks(xs, ys, block)

    fields = (p, v0, v1, v2)
    for step in range(steps):

        def keep_dv(x, rows, change, moved, step=step):
            for d in range(3):
                dv[step, d, x, rows] = change[d]

        def keep_dp(x, rows, change, moved, step=step):
            dp[step, x, rows] = change

        push(fields, fwd_slope if step == 0 else None, keep_dv)
        spread(fields, fwd_source, step, keep_dp)

    fields = (q, w0, w1, w2)
    for step in reversed(range(steps)):
        last = step == steps - 1

        def add_buoy(x, rows, change, moved, step=step, last=last):
            image = dv[step, 0, x, rows] * moved[0]
            image = image + dv[step, 1, x, rows] * moved[1]
            image = image + dv[step, 2, x, rows] * moved[2]
            buoy_img[x, rows] = image if last else buoy_img[x, rows] + image

        def add_bulk(x, rows, change, moved, step=step, last=last):
            image = dp[step, x, rows] * moved
            bulk_img[x, rows] = image if last else bulk_img[x, rows] + image

        push(fields, adj_slope if last else None, add_buoy)
        spread(fields, adj_source, step, add_bulk)

    tile_rows = tile_x * tile_y
    for chip in range(chips):
        for ref, hop in ((kept, 2 * chip), (traded, 2 * chip + 1)):
            cells = pl.ds(place_of(hop), tile_x)
            ref[chip, :tile_rows] = bulk_img[cells].reshape(tile_rows, zs)
            ref[chip, tile_rows : 2 * tile_rows] = buoy_img[cells].reshape(tile_rows, zs)
            ref[chip, 2 * tile_rows :] = jnp.full((8, zs), entry).astype(jnp.float32)


def merge_kernel(chips, kept, came, *outs):
    for chip in range(chips):
        outs[chip][0] = kept[chip]
        outs[chip][1] = came[chip]


def add_kernel(chips, groups, held, *refs):
    came, parts, total = refs[: 2 * chips], refs[2 * chips : 2 * chips + groups], refs[-1]
    stripes = 2 * chips
    me, group = lax.axis_index("tile"), lax.axis_index("grp")
    tile_rows = total.shape[1] // (held + 1)
    part = parts[0].shape[1]
    total[...] = jnp.zeros_like(total)
    for pair in came:
        for shot in range(2):
            entry = jnp.max(pair[shot, 2 * tile_rows :]).astype(jnp.int32)
            corner, column = lax.div(entry, held), lax.rem(entry, held)
            mine = (corner <= me) & (me < corner + stripes)
            slot = jnp.where(mine, column, held)
            rows = pl.ds(pl.multiple_of(slot * tile_rows, tile_rows), tile_rows)
            for field in range(2):
                sent = pair[shot, field * tile_rows : (field + 1) * tile_rows]
                total[field, rows] = total[field, rows] + sent
    for hop in range(groups):
        first = pl.multiple_of(lax.rem(group + hop, groups) * part, part)
        for field in range(2):
            parts[hop][field] = total[field, pl.ds(first, part)]


def grads_kernel(scale, groups, *refs):
    parts, speed_ref, density_ref, grads = refs[:groups], *refs[groups:]
    part = parts[0].shape[1]
    rows = pl.ds(pl.multiple_of(lax.axis_index("grp") * part, part), part)
    speed, density = speed_ref[rows], density_ref[rows]
    bulk_sum, buoy_sum = parts[0][0], parts[0][1]
    for other in parts[1:]:
        bulk_sum = bulk_sum + other[0]
        buoy_sum = buoy_sum + other[1]
    grads[0] = scale * (bulk_sum * (2.0 * density * speed))
    grads[1] = scale * (bulk_sum * (speed * speed) - buoy_sum / (density * density))


def per_device(speed, density, fwd_state, adj_state, aperture, src_pos, wavelet, rec_pos, residual):
    owners = lax.axis_size("tile")
    groups = lax.axis_size("grp")
    my_group = lax.axis_index("grp")
    held, tile_x, tile_y, depth = speed.shape
    stripes = aperture.shape[1]
    chips = stripes // 2
    steps = wavelet.shape[1]
    xs = stripes * tile_x
    f32 = jnp.float32
    cells = (xs, tile_y, depth)

    def shape(*dims):
        return jax.ShapeDtypeStruct(dims, f32)

    def across(values, hop):
        return lax.ppermute(values, "tile", [(t, t ^ hop) for t in range(owners)])

    far_speed = across(speed, stripes)
    far_density = across(density, stripes)
    lists = {hop: across(aperture, hop) for hop in reversed(range(1, stripes))}
    padded = pltpu.VMEM((xs + 2 * REACH, tile_y + 2 * EDGE, depth), f32)
    near_speed, near_density, *prepared = pl.pallas_call(
        functools.partial(prepare_kernel, steps),
        out_shape=[
            shape(*speed.shape),
            shape(*speed.shape),
            shape(3, *cells),
            shape(3, *cells),
            shape(steps, *cells),
            shape(steps, *cells),
            jax.ShapeDtypeStruct((8, depth), jnp.int32),
        ],
        in_specs=[VMEM] * 4 + [SMEM] * 5,
        out_specs=[VMEM] * 7,
        scratch_shapes=[padded, padded],
        compiler_params=PARAMS,
        cost_estimate=pl.CostEstimate(flops=4_000_000, bytes_accessed=6_000_000, transcendentals=0),
        name="prepare",
    )(speed, density, fwd_state, adj_state, aperture, src_pos, wavelet, rec_pos, residual)
    entry = prepared[-1]

    piece = shape(2, tile_x, tile_y, depth)
    pair = shape(2, 2, tile_x, tile_y, depth)
    own, beside, *pairs = pl.pallas_call(
        functools.partial(pick_kernel, chips),
        out_shape=[piece, piece] + [pair] * (chips - 1),
        in_specs=[VMEM] * (4 + stripes),
        out_specs=[VMEM] * (chips + 1),
        compiler_params=PARAMS,
        name="pick_tiles",
    )(near_speed, near_density, far_speed, far_density, entry, *[lists[h] for h in range(1, stripes)])
    pairs = [across(values, 2 * chip) for chip, values in enumerate(pairs, 1)]
    beside = across(beside, 1)
    passed = [across(values[1], 1) for values in pairs]

    tile_rows = tile_x * tile_y
    sent = shape(chips, 2 * tile_rows + 8, depth)
    four = [
        padded,
        pltpu.VMEM((xs + 2 * REACH, tile_y, depth), f32),
        pltpu.VMEM((xs, tile_y + 2 * EDGE, depth), f32),
        pltpu.VMEM(cells, f32),
    ]
    kept, traded = pl.pallas_call(
        functools.partial(wave_kernel, chips, steps, held),
        out_shape=[sent, sent],
        in_specs=[VMEM] * (stripes + 7),
        out_specs=[VMEM] * 2,
        scratch_shapes=[pltpu.VMEM(cells, f32)] * 2
        + four
        + four
        + [
            pltpu.VMEM((steps,) + cells, f32),
            pltpu.VMEM((steps, 3) + cells, f32),
            pltpu.VMEM(cells, f32),
            pltpu.VMEM(cells, f32),
        ],
        compiler_params=PARAMS,
        name="replay_and_adjoint",
    )(own, beside, *pairs, *passed, fwd_state, adj_state, *prepared)

    both = shape(2, 2 * tile_rows + 8, depth)
    stacks = pl.pallas_call(
        functools.partial(merge_kernel, chips),
        out_shape=[both] * chips,
        in_specs=[VMEM] * 2,
        out_specs=[VMEM] * chips,
        compiler_params=PARAMS,
        name="merge_pair",
    )(kept, across(traded, 1))
    came = [
        across(stacks[chip], 2 * chip + stripes * half)
        for half in range(2)
        for chip in range(chips)
        if chip or half
    ]

    rows = held * tile_rows
    part = rows // groups
    part_shape = shape(2, part, depth)
    parts = pl.pallas_call(
        functools.partial(add_kernel, chips, groups, held),
        out_shape=[part_shape] * groups,
        in_specs=[VMEM] * stripes,
        out_specs=[VMEM] * groups,
        scratch_shapes=[pltpu.VMEM((2, rows + tile_rows, depth), f32)],
        compiler_params=PARAMS,
        name="add_stripes",
    )(stacks[0], *came)

    def along(values, hop):
        return lax.ppermute(values, "grp", [(g, (g + hop) % groups) for g in range(groups)])

    parts = [parts[0]] + [along(parts[hop], hop) for hop in range(1, groups)]
    grads = pl.pallas_call(
        functools.partial(grads_kernel, 1.0 / math.sqrt(groups * owners), groups),
        out_shape=part_shape,
        in_specs=[VMEM] * (groups + 2),
        out_specs=VMEM,
        compiler_params=PARAMS,
        name="gradients",
    )(*parts, near_speed.reshape(rows, depth), near_density.reshape(rows, depth))

    whole = jnp.zeros((2, groups, part, depth), f32)
    for hop in range(groups):
        values = grads if hop == 0 else along(grads, hop)
        place = lax.rem(my_group - hop + groups, groups)
        whole = lax.dynamic_update_slice_in_dim(whole, values[:, None], place, axis=1)
    return (whole[0].reshape(speed.shape), whole[1].reshape(speed.shape))


def solution(mesh):
    return jax.shard_map(
        per_device,
        mesh=mesh,
        in_specs=(
            P("tile", None, None, None),
            P("tile", None, None, None),
            P(("grp", "tile"), None, None, None, None),
            P(("grp", "tile"), None, None, None, None),
            P(("grp", "tile"), None),
            P(("grp", "tile"), None),
            P(("grp", "tile"), None),
            P(("grp", "tile"), None, None),
            P(("grp", "tile"), None, None),
        ),
        out_specs=(P("tile", None, None, None), P("tile", None, None, None)),
        check_vma=False,
    )
```

```python
import functools
import math

import jax
import jax.numpy as jnp
from jax import lax
from jax.experimental import pallas as pl
from jax.experimental.pallas import tpu as pltpu
from jax.sharding import PartitionSpec as P

COEF = (1225.0 / 1024.0, -245.0 / 3072.0, 49.0 / 5120.0, -5.0 / 7168.0)
REACH = 4
EDGE = 8
ROWS = 8
SPAN = 8

SMEM = pl.BlockSpec(memory_space=pltpu.SMEM)
VMEM = pl.BlockSpec(memory_space=pltpu.VMEM)
PARAMS = pltpu.CompilerParams(vmem_limit_bytes=36 * 1024 * 1024)


def entry_of(list_ref):
    return jnp.max(list_ref[0:1, 0:1].astype(jnp.float32)).astype(jnp.int32)


def combine(ahead, behind):
    total = None
    for order in range(1, 5):
        upper, lower, weight = ahead(order), behind(order), COEF[order - 1]
        if upper is None and lower is None:
            continue
        if lower is None:
            term = weight * upper
        elif upper is None:
            term = -weight * lower
        else:
            term = weight * (upper - lower)
        total = term if total is None else total + term
    return total


def along_z(values, first):
    depth = values.shape[-1]
    lane = lax.broadcasted_iota(jnp.int32, values.shape, values.ndim - 1)

    def at(by):
        if by == 0:
            return values
        rolled = pltpu.roll(values, (-by) % depth, axis=values.ndim - 1)
        return jnp.where(lane < depth - by if by > 0 else lane >= -by, rolled, 0.0)

    return combine(lambda k: at(first + k - 1), lambda k: at(first - k))


def blocks(xs, ys, body):
    if xs <= SPAN:
        for y0 in range(0, ys, ROWS):
            body(0, xs, y0)
        return

    def span(index, _):
        for y0 in range(0, ys, ROWS):
            body(index * SPAN, SPAN, y0)
        return 0

    lax.fori_loop(0, xs // SPAN, span, 0)


def window(xs, x0, load):
    kept = {}

    def at(offset):
        if xs <= SPAN and not 0 <= offset < xs:
            return None
        if offset not in kept:
            kept[offset] = load(x0 + offset)
        return kept[offset]

    return at


def slopes(xs, p, x0, y0, plane, offset):
    centre = plane(offset)
    here = x0 + offset + REACH
    return (
        combine(lambda k: plane(offset + k), lambda k: plane(offset + 1 - k)),
        combine(
            lambda k: p[here, pl.ds(EDGE + y0 + k, ROWS)],
            lambda k: centre if k == 1 else p[here, pl.ds(EDGE + y0 + 1 - k, ROWS)],
        ),
        along_z(centre, 1),
    )


def prepare_kernel(
    steps, fwd, adj, src, wave, rec, res, _piece,
    fwd_slope, adj_slope, fwd_source, adj_source, *fields,
):
    xs, ys, zs = fwd_slope.shape[1:]

    def clear(ref):
        ref[...] = jnp.zeros(ref.shape, jnp.float32)

    for state, (p, v0, v1, v2), slope in (
        (fwd, fields[:4], fwd_slope),
        (adj, fields[4:], adj_slope),
    ):
        for ref in (p, v0):
            clear(ref.at[:REACH])
            clear(ref.at[REACH + xs :])
        for ref in (p.at[pl.ds(REACH, xs)], v1):
            clear(ref.at[:, :EDGE])
            clear(ref.at[:, EDGE + ys :])
        for x in range(xs):
            p[REACH + x, EDGE : EDGE + ys] = state[0, 0, x].astype(jnp.float32)
            v0[REACH + x] = state[0, 1, x].astype(jnp.float32)
            v1[x, EDGE : EDGE + ys] = state[0, 2, x].astype(jnp.float32)
            v2[x] = state[0, 3, x].astype(jnp.float32)

        def block(x0, count, y0, p=p, slope=slope):
            plane = window(xs, x0, lambda x: p[REACH + x, pl.ds(EDGE + y0, ROWS)])
            for offset in range(count):
                three = slopes(xs, p, x0, y0, plane, offset)
                for d in range(3):
                    slope[d, x0 + offset, pl.ds(y0, ROWS)] = three[d]

        blocks(xs, ys, block)

    row = lax.broadcasted_iota(jnp.int32, (ys, zs), 0)
    lane = lax.broadcasted_iota(jnp.int32, (ys, zs), 1)
    src_mark = (row == src[0, 1]) & (lane == src[0, 2])
    for x in range(xs):
        rec_mark = (row == rec[0, 0, x]) & (lane == rec[0, 1, x])
        for step in range(steps):
            amplitude = jnp.where(x == src[0, 0], wave[0, step], 0.0)
            fwd_source[step, x] = jnp.where(src_mark, amplitude, 0.0)
            adj_source[step, x] = jnp.where(rec_mark, res[0, step, x], 0.0)


def near_kernel(speed, density, aperture, near_speed, near_density, entry):
    near_speed[...] = speed[...]
    near_density[...] = density[...]
    entry[...] = jnp.full(entry.shape, entry_of(aperture), jnp.int32)


def pick_kernel(chips, near_speed, near_density, far_speed, far_density, *refs):
    stripes = 2 * chips
    lists, outs = refs[:stripes], refs[stripes:]
    held = near_speed.shape[0]
    me = lax.axis_index("tile")
    residue, half = lax.rem(me, stripes), lax.div(me, stripes)
    for hop in range(stripes):
        entry = entry_of(lists[hop])
        corner, column = lax.div(entry, held), lax.rem(entry, held)
        here = (residue >= corner) == (half == 0)
        piece = outs[hop]

        @pl.when(here)
        def _():
            piece[0] = near_speed[column]
            piece[1] = near_density[column]

        @pl.when(jnp.logical_not(here))
        def _():
            piece[0] = far_speed[column]
            piece[1] = far_density[column]


def wave_kernel(chips, steps, held, *refs):
    stripes = 2 * chips
    pieces, refs = refs[:stripes], refs[stripes:]
    fwd_slope, adj_slope, fwd_source, adj_source, entry_ref = refs[:5]
    kept, traded, p, v0, v1, v2, q, w0, w1, w2 = refs[13:23]
    bulk, buoy, dp, dv, bulk_img, buoy_img = refs[23:]
    tile_x, tile_y = pieces[0].shape[1:3]
    xs, ys, zs = bulk.shape
    residue = lax.rem(lax.axis_index("tile"), stripes)
    entry = entry_of(entry_ref)
    corner = lax.div(entry, held)

    def place_of(hop):
        return lax.rem((residue ^ hop) - corner + stripes, stripes) * tile_x

    for hop in range(stripes):
        cells = pl.ds(place_of(hop), tile_x)
        speed, density = pieces[hop][0], pieces[hop][1]
        bulk[cells] = density * speed * speed
        buoy[cells] = 1.0 / density

    def push(fields, first, note):
        p, v0, v1, v2 = fields

        def block(x0, count, y0):
            rows, inner = pl.ds(y0, ROWS), pl.ds(EDGE + y0, ROWS)
            plane = window(xs, x0, lambda x: p[REACH + x, inner])
            for offset in range(count):
                x = x0 + offset
                if first is None:
                    three = slopes(xs, p, x0, y0, plane, offset)
                else:
                    three = tuple(first[d, x, rows] for d in range(3))
                light = buoy[x, rows]
                change = tuple(light * slope for slope in three)
                moved = (
                    v0[REACH + x, rows] + change[0],
                    v1[x, inner] + change[1],
                    v2[x, rows] + change[2],
                )
                v0[REACH + x, rows] = moved[0]
                v1[x, inner] = moved[1]
                v2[x, rows] = moved[2]
                note(x, rows, change, moved)

        blocks(xs, ys, block)

    def spread(fields, source, step, note):
        p, v0, v1, v2 = fields

        def block(x0, count, y0):
            rows, inner = pl.ds(y0, ROWS), pl.ds(EDGE + y0, ROWS)
            plane = window(xs, x0, lambda x: v0[REACH + x, rows])
            for offset in range(count):
                x = x0 + offset
                along_x = combine(lambda k: plane(offset + k - 1), lambda k: plane(offset - k))
                along_y = combine(
                    lambda k: v1[x, pl.ds(EDGE + y0 + k - 1, ROWS)],
                    lambda k: v1[x, pl.ds(EDGE + y0 - k, ROWS)],
                )
                total = along_x + along_y + along_z(v2[x, rows], 0)
                change = bulk[x, rows] * total + source[step, x, rows]
                moved = p[REACH + x, inner] + change
                p[REACH + x, inner] = moved
                note(x, rows, change, moved)

        blocks(xs, ys, block)

    fields = (p, v0, v1, v2)
    for step in range(steps):

        def keep_dv(x, rows, change, moved, step=step):
            for d in range(3):
                dv[step, d, x, rows] = change[d]

        def keep_dp(x, rows, change, moved, step=step):
            dp[step, x, rows] = change

        push(fields, fwd_slope if step == 0 else None, keep_dv)
        spread(fields, fwd_source, step, keep_dp)

    fields = (q, w0, w1, w2)
    for step in reversed(range(steps)):
        last = step == steps - 1

        def add_buoy(x, rows, change, moved, step=step, last=last):
            image = dv[step, 0, x, rows] * moved[0]
            image = image + dv[step, 1, x, rows] * moved[1]
            image = image + dv[step, 2, x, rows] * moved[2]
            buoy_img[x, rows] = image if last else buoy_img[x, rows] + image

        def add_bulk(x, rows, change, moved, step=step, last=last):
            image = dp[step, x, rows] * moved
            bulk_img[x, rows] = image if last else bulk_img[x, rows] + image

        push(fields, adj_slope if last else None, add_buoy)
        spread(fields, adj_source, step, add_bulk)

    tile_rows = tile_x * tile_y
    for chip in range(chips):
        for ref, hop in ((kept, 2 * chip), (traded, 2 * chip + 1)):
            cells = pl.ds(place_of(hop), tile_x)
            ref[chip, :tile_rows] = bulk_img[cells].reshape(tile_rows, zs)
            ref[chip, tile_rows : 2 * tile_rows] = buoy_img[cells].reshape(tile_rows, zs)
            ref[chip, 2 * tile_rows :] = jnp.full((8, zs), entry).astype(jnp.float32)


def merge_kernel(chips, kept, came, *outs):
    for chip in range(chips):
        outs[chip][0] = kept[chip]
        outs[chip][1] = came[chip]


def add_kernel(chips, groups, held, *refs):
    came, parts, total = refs[: 2 * chips], refs[2 * chips : 2 * chips + groups], refs[-1]
    stripes = 2 * chips
    me, group = lax.axis_index("tile"), lax.axis_index("grp")
    tile_rows = total.shape[1] // (held + 1)
    part = parts[0].shape[1]
    total[...] = jnp.zeros_like(total)
    for pair in came:
        for shot in range(2):
            entry = jnp.max(pair[shot, 2 * tile_rows :]).astype(jnp.int32)
            corner, column = lax.div(entry, held), lax.rem(entry, held)
            mine = (corner <= me) & (me < corner + stripes)
            slot = jnp.where(mine, column, held)
            rows = pl.ds(pl.multiple_of(slot * tile_rows, tile_rows), tile_rows)
            for field in range(2):
                sent = pair[shot, field * tile_rows : (field + 1) * tile_rows]
                total[field, rows] = total[field, rows] + sent
    for hop in range(groups):
        first = pl.multiple_of((group ^ hop) * part, part)
        for field in range(2):
            parts[hop][field] = total[field, pl.ds(first, part)]


def grads_kernel(scale, groups, *refs):
    parts, speed_ref, density_ref, grads = refs[:groups], *refs[groups:]
    part = parts[0].shape[1]
    rows = pl.ds(pl.multiple_of(lax.axis_index("grp") * part, part), part)
    speed, density = speed_ref[rows], density_ref[rows]
    bulk_sum, buoy_sum = parts[0][0], parts[0][1]
    for other in parts[1:]:
        bulk_sum = bulk_sum + other[0]
        buoy_sum = buoy_sum + other[1]
    grads[0] = scale * (bulk_sum * (2.0 * density * speed))
    grads[1] = scale * (bulk_sum * (speed * speed) - buoy_sum / (density * density))


def per_device(speed, density, fwd_state, adj_state, aperture, src_pos, wavelet, rec_pos, residual):
    owners = lax.axis_size("tile")
    groups = lax.axis_size("grp")
    my_group = lax.axis_index("grp")
    held, tile_x, tile_y, depth = speed.shape
    stripes = aperture.shape[1]
    chips = stripes // 2
    steps = wavelet.shape[1]
    xs = stripes * tile_x
    f32 = jnp.float32
    cells = (xs, tile_y, depth)

    def shape(*dims):
        return jax.ShapeDtypeStruct(dims, f32)

    def across(values, hop):
        return lax.ppermute(values, "tile", [(t, t ^ hop) for t in range(owners)])

    far_speed = across(speed, stripes)
    far_density = across(density, stripes)
    far_first = [hop for hop in range(stripes - 1, 0, -1)]
    lists = {hop: across(aperture, hop) for hop in far_first}
    four = [
        (xs + 2 * REACH, tile_y + 2 * EDGE, depth),
        (xs + 2 * REACH, tile_y, depth),
        (xs, tile_y + 2 * EDGE, depth),
        cells,
    ]
    near_speed, near_density, entry = pl.pallas_call(
        near_kernel,
        out_shape=[
            shape(*speed.shape),
            shape(*speed.shape),
            jax.ShapeDtypeStruct((8, depth), jnp.int32),
        ],
        in_specs=[VMEM] * 3,
        out_specs=[VMEM] * 3,
        compiler_params=PARAMS,
        cost_estimate=pl.CostEstimate(flops=4_000_000, bytes_accessed=6_000_000, transcendentals=0),
        name="hold_near_tiles",
    )(speed, density, aperture)
    pieces = pl.pallas_call(
        functools.partial(pick_kernel, chips),
        out_shape=[shape(2, tile_x, tile_y, depth)] * stripes,
        in_specs=[VMEM] * (4 + stripes),
        out_specs=[VMEM] * stripes,
        compiler_params=PARAMS,
        name="pick_tiles",
    )(near_speed, near_density, far_speed, far_density, entry, *[lists[h] for h in range(1, stripes)])
    moved = {hop: across(pieces[hop], hop) for hop in far_first}

    prepared = pl.pallas_call(
        functools.partial(prepare_kernel, steps),
        out_shape=[shape(3, *cells)] * 2
        + [shape(steps, *cells)] * 2
        + [shape(*dims) for dims in four + four],
        in_specs=[VMEM] * 2 + [SMEM] * 4 + [VMEM],
        out_specs=[VMEM] * 12,
        compiler_params=PARAMS,
        cost_estimate=pl.CostEstimate(flops=4_000_000, bytes_accessed=6_000_000, transcendentals=0),
        name="prepare",
    )(fwd_state, adj_state, src_pos, wavelet, jnp.swapaxes(rec_pos, 1, 2), residual, pieces[0])
    prepared, fields = prepared[:4], prepared[4:]
    pieces = [pieces[0]] + [moved[hop] for hop in range(1, stripes)]

    tile_rows = tile_x * tile_y
    sent = shape(chips, 2 * tile_rows + 8, depth)
    kept, traded, *_ = pl.pallas_call(
        functools.partial(wave_kernel, chips, steps, held),
        out_shape=[sent, sent] + [shape(*dims) for dims in four + four],
        in_specs=[VMEM] * (stripes + 13),
        out_specs=[VMEM] * 10,
        scratch_shapes=[
            pltpu.VMEM(cells, f32),
            pltpu.VMEM(cells, f32),
            pltpu.VMEM((steps,) + cells, f32),
            pltpu.VMEM((steps, 3) + cells, f32),
            pltpu.VMEM(cells, f32),
            pltpu.VMEM(cells, f32),
        ],
        input_output_aliases={stripes + 5 + index: 2 + index for index in range(8)},
        compiler_params=PARAMS,
        name="replay_and_adjoint",
    )(*pieces, *prepared, entry, *fields)

    both = shape(2, 2 * tile_rows + 8, depth)
    stacks = pl.pallas_call(
        functools.partial(merge_kernel, chips),
        out_shape=[both] * chips,
        in_specs=[VMEM] * 2,
        out_specs=[VMEM] * chips,
        compiler_params=PARAMS,
        name="merge_pair",
    )(kept, across(traded, 1))
    came = [
        across(stacks[chip], 2 * chip + stripes * half)
        for half in range(2)
        for chip in range(chips)
        if chip or half
    ]

    rows = held * tile_rows
    part = rows // groups
    part_shape = shape(2, part, depth)
    parts = pl.pallas_call(
        functools.partial(add_kernel, chips, groups, held),
        out_shape=[part_shape] * groups,
        in_specs=[VMEM] * stripes,
        out_specs=[VMEM] * groups,
        scratch_shapes=[pltpu.VMEM((2, rows + tile_rows, depth), f32)],
        compiler_params=PARAMS,
        name="add_stripes",
    )(stacks[0], *came)

    def along(values, hop):
        return lax.ppermute(values, "grp", [(g, g ^ hop) for g in range(groups)])

    parts = [parts[0]] + [along(parts[hop], hop) for hop in range(groups - 1, 0, -1)]
    grads = pl.pallas_call(
        functools.partial(grads_kernel, 1.0 / math.sqrt(groups * owners), groups),
        out_shape=part_shape,
        in_specs=[VMEM] * (groups + 2),
        out_specs=VMEM,
        compiler_params=PARAMS,
        name="gradients",
    )(*parts, near_speed.reshape(rows, depth), near_density.reshape(rows, depth))

    whole = jnp.zeros((2, groups, part, depth), f32)
    for hop in [0] + list(range(groups - 1, 0, -1)):
        values = grads if hop == 0 else along(grads, hop)
        place = my_group ^ hop
        whole = lax.dynamic_update_slice_in_dim(whole, values[:, None], place, axis=1)
    return (whole[0].reshape(speed.shape), whole[1].reshape(speed.shape))


def solution(mesh):
    return jax.shard_map(
        per_device,
        mesh=mesh,
        in_specs=(
            P("tile", None, None, None),
            P("tile", None, None, None),
            P(("grp", "tile"), None, None, None, None),
            P(("grp", "tile"), None, None, None, None),
            P(("grp", "tile"), None),
            P(("grp", "tile"), None),
            P(("grp", "tile"), None),
            P(("grp", "tile"), None, None),
            P(("grp", "tile"), None, None),
        ),
        out_specs=(P("tile", None, None, None), P("tile", None, None, None)),
        check_vma=False,
    )
```

```python
import functools
import math

import jax
import jax.numpy as jnp
from jax import lax
from jax.experimental import pallas as pl
from jax.experimental.pallas import tpu as pltpu
from jax.sharding import PartitionSpec as P

COEF = (1225.0 / 1024.0, -245.0 / 3072.0, 49.0 / 5120.0, -5.0 / 7168.0)
REACH = 4
EDGE = 8
ROWS = 8
SPAN = 8

SMEM = pl.BlockSpec(memory_space=pltpu.SMEM)
VMEM = pl.BlockSpec(memory_space=pltpu.VMEM)
PARAMS = pltpu.CompilerParams(vmem_limit_bytes=36 * 1024 * 1024)


def entry_of(list_ref):
    return jnp.max(list_ref[0:1, 0:1].astype(jnp.float32)).astype(jnp.int32)


def combine(ahead, behind):
    total = None
    for order in range(1, 5):
        upper, lower, weight = ahead(order), behind(order), COEF[order - 1]
        if upper is None and lower is None:
            continue
        if lower is None:
            term = weight * upper
        elif upper is None:
            term = -weight * lower
        else:
            term = weight * (upper - lower)
        total = term if total is None else total + term
    return total


def along_z(values, first):
    depth = values.shape[-1]
    lane = lax.broadcasted_iota(jnp.int32, values.shape, values.ndim - 1)

    def at(by):
        if by == 0:
            return values
        rolled = pltpu.roll(values, (-by) % depth, axis=values.ndim - 1)
        return jnp.where(lane < depth - by if by > 0 else lane >= -by, rolled, 0.0)

    return combine(lambda k: at(first + k - 1), lambda k: at(first - k))


def blocks(xs, ys, body):
    if xs <= SPAN:
        for y0 in range(0, ys, ROWS):
            body(0, xs, y0)
        return

    def span(index, _):
        for y0 in range(0, ys, ROWS):
            body(index * SPAN, SPAN, y0)
        return 0

    lax.fori_loop(0, xs // SPAN, span, 0)


def window(xs, x0, load):
    kept = {}

    def at(offset):
        if xs <= SPAN and not 0 <= offset < xs:
            return None
        if offset not in kept:
            kept[offset] = load(x0 + offset)
        return kept[offset]

    return at


def slopes(xs, p, x0, y0, plane, offset):
    centre = plane(offset)
    here = x0 + offset + REACH
    return (
        combine(lambda k: plane(offset + k), lambda k: plane(offset + 1 - k)),
        combine(
            lambda k: p[here, pl.ds(EDGE + y0 + k, ROWS)],
            lambda k: centre if k == 1 else p[here, pl.ds(EDGE + y0 + 1 - k, ROWS)],
        ),
        along_z(centre, 1),
    )


def prepare_kernel(
    steps, fwd, adj, src, wave, rec, res, _piece,
    fwd_slope, adj_slope, fwd_source, adj_source, *fields,
):
    xs, ys, zs = fwd_slope.shape[1:]

    def clear(ref):
        ref[...] = jnp.zeros(ref.shape, jnp.float32)

    for state, (p, v0, v1, v2), slope in (
        (fwd, fields[:4], fwd_slope),
        (adj, fields[4:], adj_slope),
    ):
        for ref in (p, v0):
            clear(ref.at[:REACH])
            clear(ref.at[REACH + xs :])
        for ref in (p.at[pl.ds(REACH, xs)], v1):
            clear(ref.at[:, :EDGE])
            clear(ref.at[:, EDGE + ys :])
        for x in range(xs):
            p[REACH + x, EDGE : EDGE + ys] = state[0, 0, x].astype(jnp.float32)
            v0[REACH + x] = state[0, 1, x].astype(jnp.float32)
            v1[x, EDGE : EDGE + ys] = state[0, 2, x].astype(jnp.float32)
            v2[x] = state[0, 3, x].astype(jnp.float32)

        def block(x0, count, y0, p=p, slope=slope):
            plane = window(xs, x0, lambda x: p[REACH + x, pl.ds(EDGE + y0, ROWS)])
            for offset in range(count):
                three = slopes(xs, p, x0, y0, plane, offset)
                for d in range(3):
                    slope[d, x0 + offset, pl.ds(y0, ROWS)] = three[d]

        blocks(xs, ys, block)

    row = lax.broadcasted_iota(jnp.int32, (ys, zs), 0)
    lane = lax.broadcasted_iota(jnp.int32, (ys, zs), 1)
    src_mark = (row == src[0, 1]) & (lane == src[0, 2])
    for x in range(xs):
        rec_mark = (row == rec[0, 0, x]) & (lane == rec[0, 1, x])
        for step in range(steps):
            amplitude = jnp.where(x == src[0, 0], wave[0, step], 0.0)
            fwd_source[step, x] = jnp.where(src_mark, amplitude, 0.0)
            adj_source[step, x] = jnp.where(rec_mark, res[0, step, x], 0.0)


def near_kernel(speed, density, aperture, near_speed, near_density, entry):
    near_speed[...] = speed[...]
    near_density[...] = density[...]
    entry[...] = jnp.full(entry.shape, entry_of(aperture), jnp.int32)


def table_kernel(*refs):
    lists, table = refs[:-1], refs[-1]
    for hop, entry in enumerate(lists):
        table[hop : hop + 1] = jnp.full((1, table.shape[1]), entry_of(entry), jnp.int32)


def pick_kernel(stripes, near_speed, near_density, far_speed, far_density, table, _far, *outs):
    held = near_speed.shape[0]
    me = lax.axis_index("tile")
    residue, half = lax.rem(me, stripes), lax.div(me, stripes)
    for hop in range(stripes):
        entry = entry_of(table.at[hop : hop + 1])
        corner, column = lax.div(entry, held), lax.rem(entry, held)
        here = (residue >= corner) == (half == 0)
        piece = outs[hop]

        @pl.when(here)
        def _():
            piece[0] = near_speed[column]
            piece[1] = near_density[column]

        @pl.when(jnp.logical_not(here))
        def _():
            piece[0] = far_speed[column]
            piece[1] = far_density[column]


def wave_kernel(stripes, steps, held, *refs):
    pieces, refs = refs[:stripes], refs[stripes:]
    fwd_slope, adj_slope, fwd_source, adj_source, entry_ref = refs[:5]
    images = refs[13 : 13 + stripes]
    p, v0, v1, v2, q, w0, w1, w2, bulk, buoy, dp, dv, bulk_img, buoy_img = refs[13 + stripes :]
    tile_x, tile_y = pieces[0].shape[1:3]
    xs, ys, zs = bulk.shape
    residue = lax.rem(lax.axis_index("tile"), stripes)
    entry = entry_of(entry_ref)
    corner = lax.div(entry, held)

    def place_of(hop):
        return lax.rem((residue ^ hop) - corner + stripes, stripes) * tile_x

    for hop in range(stripes):
        cells = pl.ds(place_of(hop), tile_x)
        speed, density = pieces[hop][0], pieces[hop][1]
        bulk[cells] = density * speed * speed
        buoy[cells] = 1.0 / density

    def push(fields, first, note):
        p, v0, v1, v2 = fields

        def block(x0, count, y0):
            rows, inner = pl.ds(y0, ROWS), pl.ds(EDGE + y0, ROWS)
            plane = window(xs, x0, lambda x: p[REACH + x, inner])
            for offset in range(count):
                x = x0 + offset
                if first is None:
                    three = slopes(xs, p, x0, y0, plane, offset)
                else:
                    three = tuple(first[d, x, rows] for d in range(3))
                light = buoy[x, rows]
                change = tuple(light * slope for slope in three)
                moved = (
                    v0[REACH + x, rows] + change[0],
                    v1[x, inner] + change[1],
                    v2[x, rows] + change[2],
                )
                v0[REACH + x, rows] = moved[0]
                v1[x, inner] = moved[1]
                v2[x, rows] = moved[2]
                note(x, rows, change, moved)

        blocks(xs, ys, block)

    def spread(fields, source, step, note):
        p, v0, v1, v2 = fields

        def block(x0, count, y0):
            rows, inner = pl.ds(y0, ROWS), pl.ds(EDGE + y0, ROWS)
            plane = window(xs, x0, lambda x: v0[REACH + x, rows])
            for offset in range(count):
                x = x0 + offset
                along_x = combine(lambda k: plane(offset + k - 1), lambda k: plane(offset - k))
                along_y = combine(
                    lambda k: v1[x, pl.ds(EDGE + y0 + k - 1, ROWS)],
                    lambda k: v1[x, pl.ds(EDGE + y0 - k, ROWS)],
                )
                total = along_x + along_y + along_z(v2[x, rows], 0)
                change = bulk[x, rows] * total + source[step, x, rows]
                moved = p[REACH + x, inner] + change
                p[REACH + x, inner] = moved
                note(x, rows, change, moved)

        blocks(xs, ys, block)

    fields = (p, v0, v1, v2)
    for step in range(steps):

        def keep_dv(x, rows, change, moved, step=step):
            for d in range(3):
                dv[step, d, x, rows] = change[d]

        def keep_dp(x, rows, change, moved, step=step):
            dp[step, x, rows] = change

        push(fields, fwd_slope if step == 0 else None, keep_dv)
        spread(fields, fwd_source, step, keep_dp)

    fields = (q, w0, w1, w2)
    for step in reversed(range(steps)):
        last = step == steps - 1

        def add_buoy(x, rows, change, moved, step=step, last=last):
            image = dv[step, 0, x, rows] * moved[0]
            image = image + dv[step, 1, x, rows] * moved[1]
            image = image + dv[step, 2, x, rows] * moved[2]
            buoy_img[x, rows] = image if last else buoy_img[x, rows] + image

        def add_bulk(x, rows, change, moved, step=step, last=last):
            image = dp[step, x, rows] * moved
            bulk_img[x, rows] = image if last else bulk_img[x, rows] + image

        push(fields, adj_slope if last else None, add_buoy)
        spread(fields, adj_source, step, add_bulk)

    tile_rows = tile_x * tile_y
    for hop in range(stripes):
        cells = pl.ds(place_of(hop), tile_x)
        images[hop][:tile_rows] = bulk_img[cells].reshape(tile_rows, zs)
        images[hop][tile_rows:] = buoy_img[cells].reshape(tile_rows, zs)


def add_kernel(stripes, groups, held, near, far, *refs):
    came, parts, total = refs[: 2 * stripes], refs[2 * stripes : 2 * stripes + groups], refs[-1]
    me, group = lax.axis_index("tile"), lax.axis_index("grp")
    tile_rows = total.shape[1] // (held + 1)
    part = parts[0].shape[1]
    total[...] = jnp.zeros_like(total)
    for hop, sent in enumerate(came):
        row = hop % stripes
        entry = entry_of((near if hop < stripes else far).at[row : row + 1])
        corner, column = lax.div(entry, held), lax.rem(entry, held)
        mine = (corner <= me) & (me < corner + stripes)
        slot = jnp.where(mine, column, held)
        rows = pl.ds(pl.multiple_of(slot * tile_rows, tile_rows), tile_rows)
        for field in range(2):
            stripe = sent[field * tile_rows : (field + 1) * tile_rows]
            total[field, rows] = total[field, rows] + stripe
    for hop in range(groups):
        first = pl.multiple_of((group ^ hop) * part, part)
        for field in range(2):
            parts[hop][field] = total[field, pl.ds(first, part)]


def grads_kernel(scale, groups, *refs):
    parts, speed_ref, density_ref, grads = refs[:groups], *refs[groups:]
    part = parts[0].shape[1]
    rows = pl.ds(pl.multiple_of(lax.axis_index("grp") * part, part), part)
    speed, density = speed_ref[rows], density_ref[rows]
    bulk_sum, buoy_sum = parts[0][0], parts[0][1]
    for other in parts[1:]:
        bulk_sum = bulk_sum + other[0]
        buoy_sum = buoy_sum + other[1]
    grads[0] = scale * (bulk_sum * (2.0 * density * speed))
    grads[1] = scale * (bulk_sum * (speed * speed) - buoy_sum / (density * density))


def place_kernel(hops, *refs):
    parts, outs, sems = refs[: len(hops)], refs[-3:-1], refs[-1]
    part = parts[0].shape[1]
    copies = []
    for index, hop in enumerate(hops):
        rows = pl.ds(pl.multiple_of((lax.axis_index("grp") ^ hop) * part, part), part)
        for field in range(2):
            copies.append(
                pltpu.make_async_copy(
                    parts[index].at[field], outs[field].at[rows], sems.at[index, field]
                )
            )
    for copy in copies:
        copy.start()
    for copy in copies:
        copy.wait()


def per_device(speed, density, fwd_state, adj_state, aperture, src_pos, wavelet, rec_pos, residual):
    owners = lax.axis_size("tile")
    groups = lax.axis_size("grp")
    held, tile_x, tile_y, depth = speed.shape
    stripes = aperture.shape[1]
    steps = wavelet.shape[1]
    xs = stripes * tile_x
    f32 = jnp.float32
    cells = (xs, tile_y, depth)

    def shape(*dims):
        return jax.ShapeDtypeStruct(dims, f32)

    def across(values, hop):
        return lax.ppermute(values, "tile", [(t, t ^ hop) for t in range(owners)])

    far_speed = across(speed, stripes)
    far_density = across(density, stripes)
    far_first = [hop for hop in range(stripes - 1, 0, -1)]
    lists = {hop: across(aperture, hop) for hop in far_first}
    four = [
        (xs + 2 * REACH, tile_y + 2 * EDGE, depth),
        (xs + 2 * REACH, tile_y, depth),
        (xs, tile_y + 2 * EDGE, depth),
        cells,
    ]
    near_speed, near_density, entry = pl.pallas_call(
        near_kernel,
        out_shape=[
            shape(*speed.shape),
            shape(*speed.shape),
            jax.ShapeDtypeStruct((8, depth), jnp.int32),
        ],
        in_specs=[VMEM] * 3,
        out_specs=[VMEM] * 3,
        compiler_params=PARAMS,
        cost_estimate=pl.CostEstimate(flops=4_000_000, bytes_accessed=6_000_000, transcendentals=0),
        name="hold_near_tiles",
    )(speed, density, aperture)
    table = pl.pallas_call(
        table_kernel,
        out_shape=jax.ShapeDtypeStruct((stripes, depth), jnp.int32),
        in_specs=[VMEM] * stripes,
        out_specs=VMEM,
        compiler_params=PARAMS,
        name="list_table",
    )(entry, *[lists[hop] for hop in range(1, stripes)])
    far_table = across(table, stripes)
    pieces = pl.pallas_call(
        functools.partial(pick_kernel, stripes),
        out_shape=[shape(2, tile_x, tile_y, depth)] * stripes,
        in_specs=[VMEM] * 6,
        out_specs=[VMEM] * stripes,
        compiler_params=PARAMS,
        name="pick_tiles",
    )(near_speed, near_density, far_speed, far_density, table, far_table)
    moved = {hop: across(pieces[hop], hop) for hop in far_first}

    prepared = pl.pallas_call(
        functools.partial(prepare_kernel, steps),
        out_shape=[shape(3, *cells)] * 2
        + [shape(steps, *cells)] * 2
        + [shape(*dims) for dims in four + four],
        in_specs=[VMEM] * 2 + [SMEM] * 4 + [VMEM],
        out_specs=[VMEM] * 12,
        compiler_params=PARAMS,
        cost_estimate=pl.CostEstimate(flops=4_000_000, bytes_accessed=6_000_000, transcendentals=0),
        name="prepare",
    )(fwd_state, adj_state, src_pos, wavelet, jnp.swapaxes(rec_pos, 1, 2), residual, pieces[0])
    prepared, fields = prepared[:4], prepared[4:]
    pieces = [pieces[0]] + [moved[hop] for hop in range(1, stripes)]

    tile_rows = tile_x * tile_y
    image = shape(2 * tile_rows, depth)
    images = pl.pallas_call(
        functools.partial(wave_kernel, stripes, steps, held),
        out_shape=[image] * stripes + [shape(*dims) for dims in four + four],
        in_specs=[VMEM] * (stripes + 13),
        out_specs=[VMEM] * (stripes + 8),
        scratch_shapes=[
            pltpu.VMEM(cells, f32),
            pltpu.VMEM(cells, f32),
            pltpu.VMEM((steps,) + cells, f32),
            pltpu.VMEM((steps, 3) + cells, f32),
            pltpu.VMEM(cells, f32),
            pltpu.VMEM(cells, f32),
        ],
        input_output_aliases={stripes + 5 + index: stripes + index for index in range(8)},
        compiler_params=PARAMS,
        name="replay_and_adjoint",
    )(*pieces, *prepared, entry, *fields)

    came = {hop: across(images[hop % stripes], hop) for hop in range(owners - 1, 0, -1)}
    came = [images[0]] + [came[hop] for hop in range(1, owners)]

    rows = held * tile_rows
    part = rows // groups
    part_shape = shape(2, part, depth)
    parts = pl.pallas_call(
        functools.partial(add_kernel, stripes, groups, held),
        out_shape=[part_shape] * groups,
        in_specs=[VMEM] * (owners + 2),
        out_specs=[VMEM] * groups,
        scratch_shapes=[pltpu.VMEM((2, rows + tile_rows, depth), f32)],
        compiler_params=PARAMS,
        name="add_stripes",
    )(table, far_table, *came)

    def along(values, hop):
        return lax.ppermute(values, "grp", [(g, g ^ hop) for g in range(groups)])

    parts = [parts[0]] + [along(parts[hop], hop) for hop in range(groups - 1, 0, -1)]
    grads = pl.pallas_call(
        functools.partial(grads_kernel, 1.0 / math.sqrt(groups * owners), groups),
        out_shape=part_shape,
        in_specs=[VMEM] * (groups + 2),
        out_specs=VMEM,
        compiler_params=PARAMS,
        name="gradients",
    )(*parts, near_speed.reshape(rows, depth), near_density.reshape(rows, depth))

    order = list(range(groups - 1, 0, -1))
    sent = {hop: along(grads, hop) for hop in order}
    sent[0] = grads
    outs = ()
    for hops in ([0] + order[:-1], order[-1:]):
        outs = pl.pallas_call(
            functools.partial(place_kernel, hops),
            out_shape=[shape(rows, depth)] * 2,
            in_specs=[VMEM] * len(hops) + [pl.BlockSpec(memory_space=pl.ANY)] * len(outs),
            out_specs=[pl.BlockSpec(memory_space=pl.ANY)] * 2,
            scratch_shapes=[pltpu.SemaphoreType.DMA((len(hops), 2))],
            input_output_aliases={len(hops) + field: field for field in range(len(outs))},
            compiler_params=PARAMS,
            name="place_gradients",
        )(*[sent[hop] for hop in hops], *outs)
    return tuple(values.reshape(speed.shape) for values in outs)


def solution(mesh):
    return jax.shard_map(
        per_device,
        mesh=mesh,
        in_specs=(
            P("tile", None, None, None),
            P("tile", None, None, None),
            P(("grp", "tile"), None, None, None, None),
            P(("grp", "tile"), None, None, None, None),
            P(("grp", "tile"), None),
            P(("grp", "tile"), None),
            P(("grp", "tile"), None),
            P(("grp", "tile"), None, None),
            P(("grp", "tile"), None, None),
        ),
        out_specs=(P("tile", None, None, None), P("tile", None, None, None)),
        check_vma=False,
    )
```

```python
import functools
import math

import jax
import jax.numpy as jnp
from jax import lax
from jax.experimental import pallas as pl
from jax.experimental.pallas import tpu as pltpu
from jax.sharding import PartitionSpec as P

COEF = (1225.0 / 1024.0, -245.0 / 3072.0, 49.0 / 5120.0, -5.0 / 7168.0)
REACH = 4
EDGE = 8
ROWS = 8
SPAN = 8

SMEM = pl.BlockSpec(memory_space=pltpu.SMEM)
VMEM = pl.BlockSpec(memory_space=pltpu.VMEM)
PARAMS = pltpu.CompilerParams(vmem_limit_bytes=36 * 1024 * 1024)


def entry_of(list_ref):
    return jnp.max(list_ref[0:1, 0:1].astype(jnp.float32)).astype(jnp.int32)


def combine(ahead, behind):
    total = None
    for order in range(1, 5):
        upper, lower, weight = ahead(order), behind(order), COEF[order - 1]
        if upper is None and lower is None:
            continue
        if lower is None:
            term = weight * upper
        elif upper is None:
            term = -weight * lower
        else:
            term = weight * (upper - lower)
        total = term if total is None else total + term
    return total


def along_z(values, first):
    depth = values.shape[-1]
    lane = lax.broadcasted_iota(jnp.int32, values.shape, values.ndim - 1)

    def at(by):
        if by == 0:
            return values
        rolled = pltpu.roll(values, (-by) % depth, axis=values.ndim - 1)
        return jnp.where(lane < depth - by if by > 0 else lane >= -by, rolled, 0.0)

    return combine(lambda k: at(first + k - 1), lambda k: at(first - k))


def blocks(xs, ys, body):
    if xs <= SPAN:
        for y0 in range(0, ys, ROWS):
            body(0, xs, y0)
        return

    def span(index, _):
        for y0 in range(0, ys, ROWS):
            body(index * SPAN, SPAN, y0)
        return 0

    lax.fori_loop(0, xs // SPAN, span, 0)


def window(xs, x0, load):
    kept = {}

    def at(offset):
        if xs <= SPAN and not 0 <= offset < xs:
            return None
        if offset not in kept:
            kept[offset] = load(x0 + offset)
        return kept[offset]

    return at


def slopes(xs, p, x0, y0, plane, offset):
    centre = plane(offset)
    here = x0 + offset + REACH
    return (
        combine(lambda k: plane(offset + k), lambda k: plane(offset + 1 - k)),
        combine(
            lambda k: p[here, pl.ds(EDGE + y0 + k, ROWS)],
            lambda k: centre if k == 1 else p[here, pl.ds(EDGE + y0 + 1 - k, ROWS)],
        ),
        along_z(centre, 1),
    )


def prepare_kernel(
    steps, fwd, adj, src, wave, rec, res, _piece,
    fwd_slope, adj_slope, fwd_source, adj_source, *fields,
):
    xs, ys, zs = fwd_slope.shape[1:]

    def clear(ref):
        ref[...] = jnp.zeros(ref.shape, jnp.float32)

    for state, (p, v0, v1, v2), slope in (
        (fwd, fields[:4], fwd_slope),
        (adj, fields[4:], adj_slope),
    ):
        for ref in (p, v0):
            clear(ref.at[:REACH])
            clear(ref.at[REACH + xs :])
        for ref in (p.at[pl.ds(REACH, xs)], v1):
            clear(ref.at[:, :EDGE])
            clear(ref.at[:, EDGE + ys :])
        for x in range(xs):
            p[REACH + x, EDGE : EDGE + ys] = state[0, 0, x].astype(jnp.float32)
            v0[REACH + x] = state[0, 1, x].astype(jnp.float32)
            v1[x, EDGE : EDGE + ys] = state[0, 2, x].astype(jnp.float32)
            v2[x] = state[0, 3, x].astype(jnp.float32)

        def block(x0, count, y0, p=p, slope=slope):
            plane = window(xs, x0, lambda x: p[REACH + x, pl.ds(EDGE + y0, ROWS)])
            for offset in range(count):
                three = slopes(xs, p, x0, y0, plane, offset)
                for d in range(3):
                    slope[d, x0 + offset, pl.ds(y0, ROWS)] = three[d]

        blocks(xs, ys, block)

    row = lax.broadcasted_iota(jnp.int32, (ys, zs), 0)
    lane = lax.broadcasted_iota(jnp.int32, (ys, zs), 1)
    src_mark = (row == src[0, 1]) & (lane == src[0, 2])
    for x in range(xs):
        rec_mark = (row == rec[0, 0, x]) & (lane == rec[0, 1, x])
        for step in range(steps):
            amplitude = jnp.where(x == src[0, 0], wave[0, step], 0.0)
            fwd_source[step, x] = jnp.where(src_mark, amplitude, 0.0)
            adj_source[step, x] = jnp.where(rec_mark, res[0, step, x], 0.0)


def near_kernel(speed, density, aperture, near_speed, near_density, entry):
    near_speed[...] = speed[...]
    near_density[...] = density[...]
    entry[...] = jnp.full(entry.shape, entry_of(aperture), jnp.int32)


def pick_kernel(chips, near_speed, near_density, far_speed, far_density, *refs):
    stripes = 2 * chips
    lists, outs = refs[:stripes], refs[stripes:]
    held = near_speed.shape[0]
    me = lax.axis_index("tile")
    residue, half = lax.rem(me, stripes), lax.div(me, stripes)
    for hop in range(stripes):
        entry = entry_of(lists[hop])
        corner, column = lax.div(entry, held), lax.rem(entry, held)
        here = (residue >= corner) == (half == 0)
        piece = outs[hop]

        @pl.when(here)
        def _():
            piece[0] = near_speed[column]
            piece[1] = near_density[column]

        @pl.when(jnp.logical_not(here))
        def _():
            piece[0] = far_speed[column]
            piece[1] = far_density[column]


def gather_order(stripes):
    return [0] + list(range(2, stripes)) + [1]


def wave_kernel(chips, steps, held, *refs):
    stripes = 2 * chips
    pieces, refs = refs[:stripes], refs[stripes:]
    fwd_slope, adj_slope, fwd_source, adj_source, entry_ref = refs[:5]
    kept, traded, p, v0, v1, v2, q, w0, w1, w2 = refs[13:23]
    bulk, buoy, dp, dv, bulk_img, buoy_img = refs[23:]
    tile_x, tile_y = pieces[0].shape[1:3]
    xs, ys, zs = bulk.shape
    residue = lax.rem(lax.axis_index("tile"), stripes)
    entry = entry_of(entry_ref)
    corner = lax.div(entry, held)

    def place_of(hop):
        return lax.rem((residue ^ hop) - corner + stripes, stripes) * tile_x

    for hop, piece in zip(gather_order(stripes), pieces):
        cells = pl.ds(place_of(hop), tile_x)
        speed, density = piece[0], piece[1]
        bulk[cells] = density * speed * speed
        buoy[cells] = 1.0 / density

    def push(fields, first, note):
        p, v0, v1, v2 = fields

        def block(x0, count, y0):
            rows, inner = pl.ds(y0, ROWS), pl.ds(EDGE + y0, ROWS)
            plane = window(xs, x0, lambda x: p[REACH + x, inner])
            for offset in range(count):
                x = x0 + offset
                if first is None:
                    three = slopes(xs, p, x0, y0, plane, offset)
                else:
                    three = tuple(first[d, x, rows] for d in range(3))
                light = buoy[x, rows]
                change = tuple(light * slope for slope in three)
                moved = (
                    v0[REACH + x, rows] + change[0],
                    v1[x, inner] + change[1],
                    v2[x, rows] + change[2],
                )
                v0[REACH + x, rows] = moved[0]
                v1[x, inner] = moved[1]
                v2[x, rows] = moved[2]
                note(x, rows, change, moved)

        blocks(xs, ys, block)

    def spread(fields, source, step, note):
        p, v0, v1, v2 = fields

        def block(x0, count, y0):
            rows, inner = pl.ds(y0, ROWS), pl.ds(EDGE + y0, ROWS)
            plane = window(xs, x0, lambda x: v0[REACH + x, rows])
            for offset in range(count):
                x = x0 + offset
                along_x = combine(lambda k: plane(offset + k - 1), lambda k: plane(offset - k))
                along_y = combine(
                    lambda k: v1[x, pl.ds(EDGE + y0 + k - 1, ROWS)],
                    lambda k: v1[x, pl.ds(EDGE + y0 - k, ROWS)],
                )
                total = along_x + along_y + along_z(v2[x, rows], 0)
                change = bulk[x, rows] * total + source[step, x, rows]
                moved = p[REACH + x, inner] + change
                p[REACH + x, inner] = moved
                note(x, rows, change, moved)

        blocks(xs, ys, block)

    fields = (p, v0, v1, v2)
    for step in range(steps):

        def keep_dv(x, rows, change, moved, step=step):
            for d in range(3):
                dv[step, d, x, rows] = change[d]

        def keep_dp(x, rows, change, moved, step=step):
            dp[step, x, rows] = change

        push(fields, fwd_slope if step == 0 else None, keep_dv)
        spread(fields, fwd_source, step, keep_dp)

    fields = (q, w0, w1, w2)
    for step in reversed(range(steps)):
        last = step == steps - 1

        def add_buoy(x, rows, change, moved, step=step, last=last):
            image = dv[step, 0, x, rows] * moved[0]
            image = image + dv[step, 1, x, rows] * moved[1]
            image = image + dv[step, 2, x, rows] * moved[2]
            buoy_img[x, rows] = image if last else buoy_img[x, rows] + image

        def add_bulk(x, rows, change, moved, step=step, last=last):
            image = dp[step, x, rows] * moved
            bulk_img[x, rows] = image if last else bulk_img[x, rows] + image

        push(fields, adj_slope if last else None, add_buoy)
        spread(fields, adj_source, step, add_bulk)

    tile_rows = tile_x * tile_y
    for chip in range(chips):
        for ref, hop in ((kept, 2 * chip), (traded, 2 * chip + 1)):
            cells = pl.ds(place_of(hop), tile_x)
            ref[chip, :tile_rows] = bulk_img[cells].reshape(tile_rows, zs)
            ref[chip, tile_rows : 2 * tile_rows] = buoy_img[cells].reshape(tile_rows, zs)
            ref[chip, 2 * tile_rows :] = jnp.full((8, zs), entry).astype(jnp.float32)


def merge_kernel(chips, kept, came, *outs):
    for index, out in enumerate(outs):
        out[0] = kept[index % chips]
        out[1] = came[index % chips]


def add_kernel(chips, groups, held, *refs):
    came, parts, total = refs[: 2 * chips], refs[2 * chips : 2 * chips + groups], refs[-1]
    stripes = 2 * chips
    me, group = lax.axis_index("tile"), lax.axis_index("grp")
    tile_rows = total.shape[1] // (held + 1)
    part = parts[0].shape[1]
    total[...] = jnp.zeros_like(total)
    for pair in came:
        for shot in range(2):
            entry = jnp.max(pair[shot, 2 * tile_rows :]).astype(jnp.int32)
            corner, column = lax.div(entry, held), lax.rem(entry, held)
            mine = (corner <= me) & (me < corner + stripes)
            slot = jnp.where(mine, column, held)
            rows = pl.ds(pl.multiple_of(slot * tile_rows, tile_rows), tile_rows)
            for field in range(2):
                sent = pair[shot, field * tile_rows : (field + 1) * tile_rows]
                total[field, rows] = total[field, rows] + sent
    for hop in range(groups):
        first = pl.multiple_of((group ^ hop) * part, part)
        for field in range(2):
            parts[hop][field] = total[field, pl.ds(first, part)]


def grads_kernel(scale, groups, *refs):
    parts, speed_ref, density_ref, grads = refs[:groups], *refs[groups:]
    part = parts[0].shape[1]
    rows = pl.ds(pl.multiple_of(lax.axis_index("grp") * part, part), part)
    speed, density = speed_ref[rows], density_ref[rows]
    bulk_sum, buoy_sum = parts[0][0], parts[0][1]
    for other in parts[1:]:
        bulk_sum = bulk_sum + other[0]
        buoy_sum = buoy_sum + other[1]
    grads[0] = scale * (bulk_sum * (2.0 * density * speed))
    grads[1] = scale * (bulk_sum * (speed * speed) - buoy_sum / (density * density))


def per_device(speed, density, fwd_state, adj_state, aperture, src_pos, wavelet, rec_pos, residual):
    owners = lax.axis_size("tile")
    groups = lax.axis_size("grp")
    my_group = lax.axis_index("grp")
    held, tile_x, tile_y, depth = speed.shape
    stripes = aperture.shape[1]
    chips = stripes // 2
    steps = wavelet.shape[1]
    xs = stripes * tile_x
    f32 = jnp.float32
    cells = (xs, tile_y, depth)

    def shape(*dims):
        return jax.ShapeDtypeStruct(dims, f32)

    def across(values, hop):
        return lax.ppermute(values, "tile", [(t, t ^ hop) for t in range(owners)])

    far_speed = across(speed, stripes)
    far_density = across(density, stripes)
    far_first = [hop for hop in range(stripes - 1, 0, -1)]
    lists = {hop: across(aperture, hop) for hop in far_first}
    four = [
        (xs + 2 * REACH, tile_y + 2 * EDGE, depth),
        (xs + 2 * REACH, tile_y, depth),
        (xs, tile_y + 2 * EDGE, depth),
        cells,
    ]
    near_speed, near_density, entry = pl.pallas_call(
        near_kernel,
        out_shape=[
            shape(*speed.shape),
            shape(*speed.shape),
            jax.ShapeDtypeStruct((8, depth), jnp.int32),
        ],
        in_specs=[VMEM] * 3,
        out_specs=[VMEM] * 3,
        compiler_params=PARAMS,
        cost_estimate=pl.CostEstimate(flops=4_000_000, bytes_accessed=6_000_000, transcendentals=0),
        name="hold_near_tiles",
    )(speed, density, aperture)
    pieces = pl.pallas_call(
        functools.partial(pick_kernel, chips),
        out_shape=[shape(2, tile_x, tile_y, depth)] * stripes,
        in_specs=[VMEM] * (4 + stripes),
        out_specs=[VMEM] * stripes,
        compiler_params=PARAMS,
        name="pick_tiles",
    )(near_speed, near_density, far_speed, far_density, entry, *[lists[h] for h in range(1, stripes)])

    prepared = pl.pallas_call(
        functools.partial(prepare_kernel, steps),
        out_shape=[shape(3, *cells)] * 2
        + [shape(steps, *cells)] * 2
        + [shape(*dims) for dims in four + four],
        in_specs=[VMEM] * 2 + [SMEM] * 4 + [VMEM],
        out_specs=[VMEM] * 12,
        compiler_params=PARAMS,
        cost_estimate=pl.CostEstimate(flops=4_000_000, bytes_accessed=6_000_000, transcendentals=0),
        name="prepare",
    )(fwd_state, adj_state, src_pos, wavelet, jnp.swapaxes(rec_pos, 1, 2), residual, pieces[0])
    prepared, fields = prepared[:4], prepared[4:]
    pieces = [across(pieces[hop], hop) if hop else pieces[0] for hop in gather_order(stripes)]

    tile_rows = tile_x * tile_y
    sent = shape(chips, 2 * tile_rows + 8, depth)
    kept, traded, *_ = pl.pallas_call(
        functools.partial(wave_kernel, chips, steps, held),
        out_shape=[sent, sent] + [shape(*dims) for dims in four + four],
        in_specs=[VMEM] * (stripes + 13),
        out_specs=[VMEM] * 10,
        scratch_shapes=[
            pltpu.VMEM(cells, f32),
            pltpu.VMEM(cells, f32),
            pltpu.VMEM((steps,) + cells, f32),
            pltpu.VMEM((steps, 3) + cells, f32),
            pltpu.VMEM(cells, f32),
            pltpu.VMEM(cells, f32),
        ],
        input_output_aliases={stripes + 5 + index: 2 + index for index in range(8)},
        compiler_params=PARAMS,
        name="replay_and_adjoint",
    )(*pieces, *prepared, entry, *fields)

    both = shape(2, 2 * tile_rows + 8, depth)
    stacks = pl.pallas_call(
        functools.partial(merge_kernel, chips),
        out_shape=[both] * stripes,
        in_specs=[VMEM] * 2,
        out_specs=[VMEM] * stripes,
        compiler_params=PARAMS,
        name="merge_pair",
    )(kept, across(traded, 1))
    came = [across(stacks[chip], 2 * chip) for chip in [1] + list(range(stripes - 1, 1, -1))]

    rows = held * tile_rows
    part = rows // groups
    part_shape = shape(2, part, depth)
    parts = pl.pallas_call(
        functools.partial(add_kernel, chips, groups, held),
        out_shape=[part_shape] * groups,
        in_specs=[VMEM] * stripes,
        out_specs=[VMEM] * groups,
        scratch_shapes=[pltpu.VMEM((2, rows + tile_rows, depth), f32)],
        compiler_params=PARAMS,
        name="add_stripes",
    )(stacks[0], *came)

    def along(values, hop):
        return lax.ppermute(values, "grp", [(g, g ^ hop) for g in range(groups)])

    parts = [parts[0]] + [along(parts[hop], hop) for hop in range(groups - 1, 0, -1)]
    grads = pl.pallas_call(
        functools.partial(grads_kernel, 1.0 / math.sqrt(groups * owners), groups),
        out_shape=part_shape,
        in_specs=[VMEM] * (groups + 2),
        out_specs=VMEM,
        compiler_params=PARAMS,
        name="gradients",
    )(*parts, near_speed.reshape(rows, depth), near_density.reshape(rows, depth))

    whole = jnp.zeros((2, groups, part, depth), f32)
    for hop in [0] + list(range(groups - 1, 0, -1)):
        values = grads if hop == 0 else along(grads, hop)
        place = my_group ^ hop
        whole = lax.dynamic_update_slice_in_dim(whole, values[:, None], place, axis=1)
    return (whole[0].reshape(speed.shape), whole[1].reshape(speed.shape))


def solution(mesh):
    return jax.shard_map(
        per_device,
        mesh=mesh,
        in_specs=(
            P("tile", None, None, None),
            P("tile", None, None, None),
            P(("grp", "tile"), None, None, None, None),
            P(("grp", "tile"), None, None, None, None),
            P(("grp", "tile"), None),
            P(("grp", "tile"), None),
            P(("grp", "tile"), None),
            P(("grp", "tile"), None, None),
            P(("grp", "tile"), None, None),
        ),
        out_specs=(P("tile", None, None, None), P("tile", None, None, None)),
        check_vma=False,
    )
```

```python
import functools
import math

import jax
import jax.numpy as jnp
from jax import lax
from jax.experimental import pallas as pl
from jax.experimental.pallas import tpu as pltpu
from jax.sharding import PartitionSpec as P

COEF = (1225.0 / 1024.0, -245.0 / 3072.0, 49.0 / 5120.0, -5.0 / 7168.0)
REACH = 4
EDGE = 8
ROWS = 8
SPAN = 8

SMEM = pl.BlockSpec(memory_space=pltpu.SMEM)
VMEM = pl.BlockSpec(memory_space=pltpu.VMEM)
PARAMS = pltpu.CompilerParams(vmem_limit_bytes=36 * 1024 * 1024)


def entry_of(list_ref):
    return jnp.max(list_ref[0:1, 0:1].astype(jnp.float32)).astype(jnp.int32)


def combine(ahead, behind):
    total = None
    for order in range(1, 5):
        upper, lower = ahead(order), behind(order)
        if upper is None and lower is None:
            continue
        if lower is None:
            term = upper
        elif upper is None:
            term = -lower
        else:
            term = upper - lower
        if order > 1:
            term = (COEF[order - 1] / COEF[0]) * term
        total = term if total is None else total + term
    return total


def along_z(values, first):
    depth = values.shape[-1]
    lane = lax.broadcasted_iota(jnp.int32, values.shape, values.ndim - 1)
    total = None
    for order in range(1, 5):
        for by, sign in ((first + order - 1, 1.0), (first - order, -1.0)):
            weight = sign * COEF[order - 1] / COEF[0]
            if by == 0:
                term = values if weight == 1.0 else -values if weight == -1.0 else weight * values
            else:
                inside = lane < depth - by if by > 0 else lane >= -by
                masked = jnp.where(inside, weight, 0.0)
                term = masked * pltpu.roll(values, (-by) % depth, axis=values.ndim - 1)
            total = term if total is None else total + term
    return total


def blocks(xs, ys, body):
    if xs <= SPAN:
        for y0 in range(0, ys, ROWS):
            body(0, xs, y0)
        return

    def span(index, _):
        for y0 in range(0, ys, ROWS):
            body(index * SPAN, SPAN, y0)
        return 0

    lax.fori_loop(0, xs // SPAN, span, 0)


def window(xs, x0, load):
    kept = {}

    def at(offset):
        if xs <= SPAN and not 0 <= offset < xs:
            return None
        if offset not in kept:
            kept[offset] = load(x0 + offset)
        return kept[offset]

    return at


def slopes(xs, p, x0, y0, plane, offset):
    centre = plane(offset)
    here = x0 + offset + REACH
    return (
        combine(lambda k: plane(offset + k), lambda k: plane(offset + 1 - k)),
        combine(
            lambda k: p[here, pl.ds(EDGE + y0 + k, ROWS)],
            lambda k: centre if k == 1 else p[here, pl.ds(EDGE + y0 + 1 - k, ROWS)],
        ),
        along_z(centre, 1),
    )


def prepare_kernel(
    steps, fwd, adj, src, wave, rec, res, _piece,
    fwd_slope, adj_slope, fwd_source, adj_source, *fields,
):
    xs, ys, zs = fwd_slope.shape[1:]

    def clear(ref):
        ref[...] = jnp.zeros(ref.shape, jnp.float32)

    for state, (p, v0, v1, v2), slope in (
        (fwd, fields[:4], fwd_slope),
        (adj, fields[4:], adj_slope),
    ):
        for ref in (p, v0):
            clear(ref.at[:REACH])
            clear(ref.at[REACH + xs :])
        for ref in (p.at[pl.ds(REACH, xs)], v1):
            clear(ref.at[:, :EDGE])
            clear(ref.at[:, EDGE + ys :])
        for x in range(xs):
            p[REACH + x, EDGE : EDGE + ys] = state[0, 0, x].astype(jnp.float32)
            v0[REACH + x] = state[0, 1, x].astype(jnp.float32)
            v1[x, EDGE : EDGE + ys] = state[0, 2, x].astype(jnp.float32)
            v2[x] = state[0, 3, x].astype(jnp.float32)

        def block(x0, count, y0, p=p, slope=slope):
            plane = window(xs, x0, lambda x: p[REACH + x, pl.ds(EDGE + y0, ROWS)])
            for offset in range(count):
                three = slopes(xs, p, x0, y0, plane, offset)
                for d in range(3):
                    slope[d, x0 + offset, pl.ds(y0, ROWS)] = three[d]

        blocks(xs, ys, block)

    row = lax.broadcasted_iota(jnp.int32, (ys, zs), 0)
    lane = lax.broadcasted_iota(jnp.int32, (ys, zs), 1)
    src_mark = (row == src[0, 1]) & (lane == src[0, 2])
    for x in range(xs):
        rec_mark = (row == rec[0, 0, x]) & (lane == rec[0, 1, x])
        for step in range(steps):
            amplitude = jnp.where(x == src[0, 0], wave[0, step], 0.0)
            fwd_source[step, x] = jnp.where(src_mark, amplitude, 0.0)
            adj_source[step, x] = jnp.where(rec_mark, res[0, step, x], 0.0)


def near_kernel(speed, density, aperture, near_speed, near_density, entry):
    near_speed[...] = speed[...]
    near_density[...] = density[...]
    entry[...] = jnp.full(entry.shape, entry_of(aperture), jnp.int32)


def pick_kernel(chips, near_speed, near_density, far_speed, far_density, *refs):
    stripes = 2 * chips
    lists, outs = refs[:stripes], refs[stripes:]
    held = near_speed.shape[0]
    me = lax.axis_index("tile")
    residue, half = lax.rem(me, stripes), lax.div(me, stripes)
    for hop in range(stripes):
        entry = entry_of(lists[hop])
        corner, column = lax.div(entry, held), lax.rem(entry, held)
        here = (residue >= corner) == (half == 0)
        piece = outs[hop]

        @pl.when(here)
        def _():
            piece[0] = near_speed[column]
            piece[1] = near_density[column]

        @pl.when(jnp.logical_not(here))
        def _():
            piece[0] = far_speed[column]
            piece[1] = far_density[column]


def wave_kernel(chips, steps, held, *refs):
    stripes = 2 * chips
    pieces, refs = refs[:stripes], refs[stripes:]
    fwd_slope, adj_slope, fwd_source, adj_source, entry_ref = refs[:5]
    kept, traded, p, v0, v1, v2, q, w0, w1, w2 = refs[13:23]
    bulk, buoy, dp, dv, bulk_img, buoy_img = refs[23:]
    tile_x, tile_y = pieces[0].shape[1:3]
    xs, ys, zs = bulk.shape
    residue = lax.rem(lax.axis_index("tile"), stripes)
    entry = entry_of(entry_ref)
    corner = lax.div(entry, held)

    def place_of(hop):
        return lax.rem((residue ^ hop) - corner + stripes, stripes) * tile_x

    for hop in range(stripes):
        cells = pl.ds(place_of(hop), tile_x)
        speed, density = pieces[hop][0], pieces[hop][1]
        bulk[cells] = COEF[0] * (density * speed * speed)
        buoy[cells] = COEF[0] / density

    def push(fields, first, note):
        p, v0, v1, v2 = fields

        def block(x0, count, y0):
            rows, inner = pl.ds(y0, ROWS), pl.ds(EDGE + y0, ROWS)
            plane = window(xs, x0, lambda x: p[REACH + x, inner])
            for offset in range(count):
                x = x0 + offset
                if first is None:
                    three = slopes(xs, p, x0, y0, plane, offset)
                else:
                    three = tuple(first[d, x, rows] for d in range(3))
                light = buoy[x, rows]
                change = tuple(light * slope for slope in three)
                moved = (
                    v0[REACH + x, rows] + change[0],
                    v1[x, inner] + change[1],
                    v2[x, rows] + change[2],
                )
                v0[REACH + x, rows] = moved[0]
                v1[x, inner] = moved[1]
                v2[x, rows] = moved[2]
                note(x, rows, change, moved)

        blocks(xs, ys, block)

    def spread(fields, source, step, note):
        p, v0, v1, v2 = fields

        def block(x0, count, y0):
            rows, inner = pl.ds(y0, ROWS), pl.ds(EDGE + y0, ROWS)
            plane = window(xs, x0, lambda x: v0[REACH + x, rows])
            for offset in range(count):
                x = x0 + offset
                along_x = combine(lambda k: plane(offset + k - 1), lambda k: plane(offset - k))
                along_y = combine(
                    lambda k: v1[x, pl.ds(EDGE + y0 + k - 1, ROWS)],
                    lambda k: v1[x, pl.ds(EDGE + y0 - k, ROWS)],
                )
                total = along_x + along_y + along_z(v2[x, rows], 0)
                change = bulk[x, rows] * total + source[step, x, rows]
                moved = p[REACH + x, inner] + change
                p[REACH + x, inner] = moved
                note(x, rows, change, moved)

        blocks(xs, ys, block)

    fields = (p, v0, v1, v2)
    for step in range(steps):

        def keep_dv(x, rows, change, moved, step=step):
            for d in range(3):
                dv[step, d, x, rows] = change[d]

        def keep_dp(x, rows, change, moved, step=step):
            dp[step, x, rows] = change

        push(fields, fwd_slope if step == 0 else None, keep_dv)
        spread(fields, fwd_source, step, keep_dp)

    fields = (q, w0, w1, w2)
    for step in reversed(range(steps)):
        last = step == steps - 1

        def add_buoy(x, rows, change, moved, step=step, last=last):
            image = dv[step, 0, x, rows] * moved[0]
            image = image + dv[step, 1, x, rows] * moved[1]
            image = image + dv[step, 2, x, rows] * moved[2]
            buoy_img[x, rows] = image if last else buoy_img[x, rows] + image

        def add_bulk(x, rows, change, moved, step=step, last=last):
            image = dp[step, x, rows] * moved
            bulk_img[x, rows] = image if last else bulk_img[x, rows] + image

        push(fields, adj_slope if last else None, add_buoy)
        spread(fields, adj_source, step, add_bulk)

    tile_rows = tile_x * tile_y
    for chip in range(chips):
        for ref, hop in ((kept, 2 * chip), (traded, 2 * chip + 1)):
            cells = pl.ds(place_of(hop), tile_x)
            ref[chip, :tile_rows] = bulk_img[cells].reshape(tile_rows, zs)
            ref[chip, tile_rows : 2 * tile_rows] = buoy_img[cells].reshape(tile_rows, zs)
            ref[chip, 2 * tile_rows :] = jnp.full((8, zs), entry).astype(jnp.float32)


def merge_kernel(chips, kept, came, *outs):
    for chip in range(chips):
        outs[chip][0] = kept[chip]
        outs[chip][1] = came[chip]


def add_kernel(chips, groups, held, *refs):
    came, parts, total = refs[: 2 * chips], refs[2 * chips : 2 * chips + groups], refs[-1]
    stripes = 2 * chips
    me, group = lax.axis_index("tile"), lax.axis_index("grp")
    tile_rows = total.shape[1] // (held + 1)
    part = parts[0].shape[1]
    total[...] = jnp.zeros_like(total)
    for pair in came:
        for shot in range(2):
            entry = jnp.max(pair[shot, 2 * tile_rows :]).astype(jnp.int32)
            corner, column = lax.div(entry, held), lax.rem(entry, held)
            mine = (corner <= me) & (me < corner + stripes)
            slot = jnp.where(mine, column, held)
            rows = pl.ds(pl.multiple_of(slot * tile_rows, tile_rows), tile_rows)
            for field in range(2):
                sent = pair[shot, field * tile_rows : (field + 1) * tile_rows]
                total[field, rows] = total[field, rows] + sent
    odd = lax.rem(me, 2) == 1
    for index, (hop, other) in enumerate(zip([0] + far_first(groups), [0] + near_first(groups))):
        first = pl.multiple_of((group ^ jnp.where(odd, hop, other)) * part, part)
        for field in range(2):
            parts[index][field] = total[field, pl.ds(first, part)]


def far_first(groups):
    return list(range(groups - 1, 0, -1))


def near_first(groups):
    return [1] + list(range(groups - 1, 1, -1))


def grads_kernel(scale, groups, *refs):
    parts, speed_ref, density_ref, grads = refs[:groups], *refs[groups:]
    part = parts[0].shape[1]
    rows = pl.ds(pl.multiple_of(lax.axis_index("grp") * part, part), part)
    speed, density = speed_ref[rows], density_ref[rows]
    bulk_sum, buoy_sum = parts[0][0], parts[0][1]
    for other in parts[1:]:
        bulk_sum = bulk_sum + other[0]
        buoy_sum = buoy_sum + other[1]
    grads[0] = scale * (bulk_sum * (2.0 * density * speed))
    grads[1] = scale * (bulk_sum * (speed * speed) - buoy_sum / (density * density))


def per_device(speed, density, fwd_state, adj_state, aperture, src_pos, wavelet, rec_pos, residual):
    owners = lax.axis_size("tile")
    groups = lax.axis_size("grp")
    my_group = lax.axis_index("grp")
    held, tile_x, tile_y, depth = speed.shape
    stripes = aperture.shape[1]
    chips = stripes // 2
    steps = wavelet.shape[1]
    xs = stripes * tile_x
    f32 = jnp.float32
    cells = (xs, tile_y, depth)

    def shape(*dims):
        return jax.ShapeDtypeStruct(dims, f32)

    def across(values, hop):
        return lax.ppermute(values, "tile", [(t, t ^ hop) for t in range(owners)])

    far_speed = across(speed, stripes)
    far_density = across(density, stripes)
    lists = {hop: across(aperture, hop) for hop in range(stripes - 1, 0, -1)}
    four = [
        (xs + 2 * REACH, tile_y + 2 * EDGE, depth),
        (xs + 2 * REACH, tile_y, depth),
        (xs, tile_y + 2 * EDGE, depth),
        cells,
    ]
    near_speed, near_density, entry = pl.pallas_call(
        near_kernel,
        out_shape=[
            shape(*speed.shape),
            shape(*speed.shape),
            jax.ShapeDtypeStruct((8, depth), jnp.int32),
        ],
        in_specs=[VMEM] * 3,
        out_specs=[VMEM] * 3,
        compiler_params=PARAMS,
        cost_estimate=pl.CostEstimate(flops=4_000_000, bytes_accessed=6_000_000, transcendentals=0),
        name="hold_near_tiles",
    )(speed, density, aperture)
    pieces = pl.pallas_call(
        functools.partial(pick_kernel, chips),
        out_shape=[shape(2, tile_x, tile_y, depth)] * stripes,
        in_specs=[VMEM] * (4 + stripes),
        out_specs=[VMEM] * stripes,
        compiler_params=PARAMS,
        name="pick_tiles",
    )(near_speed, near_density, far_speed, far_density, entry, *[lists[h] for h in range(1, stripes)])
    moved = {hop: across(pieces[hop], hop) for hop in range(stripes - 1, 0, -1)}

    prepared = pl.pallas_call(
        functools.partial(prepare_kernel, steps),
        out_shape=[shape(3, *cells)] * 2
        + [shape(steps, *cells)] * 2
        + [shape(*dims) for dims in four + four],
        in_specs=[VMEM] * 2 + [SMEM] * 4 + [VMEM],
        out_specs=[VMEM] * 12,
        compiler_params=PARAMS,
        cost_estimate=pl.CostEstimate(flops=4_000_000, bytes_accessed=6_000_000, transcendentals=0),
        name="prepare",
    )(fwd_state, adj_state, src_pos, wavelet, jnp.swapaxes(rec_pos, 1, 2), residual, pieces[0])
    prepared, fields = prepared[:4], prepared[4:]
    pieces = [pieces[0]] + [moved[hop] for hop in range(1, stripes)]

    tile_rows = tile_x * tile_y
    sent = shape(chips, 2 * tile_rows + 8, depth)
    kept, traded, *_ = pl.pallas_call(
        functools.partial(wave_kernel, chips, steps, held),
        out_shape=[sent, sent] + [shape(*dims) for dims in four + four],
        in_specs=[VMEM] * (stripes + 13),
        out_specs=[VMEM] * 10,
        scratch_shapes=[
            pltpu.VMEM(cells, f32),
            pltpu.VMEM(cells, f32),
            pltpu.VMEM((steps,) + cells, f32),
            pltpu.VMEM((steps, 3) + cells, f32),
            pltpu.VMEM(cells, f32),
            pltpu.VMEM(cells, f32),
        ],
        input_output_aliases={stripes + 5 + index: 2 + index for index in range(8)},
        compiler_params=PARAMS,
        name="replay_and_adjoint",
    )(*pieces, *prepared, entry, *fields)

    both = shape(2, 2 * tile_rows + 8, depth)
    stacks = pl.pallas_call(
        functools.partial(merge_kernel, chips),
        out_shape=[both] * chips,
        in_specs=[VMEM] * 2,
        out_specs=[VMEM] * chips,
        compiler_params=PARAMS,
        name="merge_pair",
    )(kept, across(traded, 1))
    came = [
        across(stacks[chip], 2 * chip + stripes * half)
        for half in range(2)
        for chip in range(chips)
        if chip or half
    ]

    rows = held * tile_rows
    part = rows // groups
    part_shape = shape(2, part, depth)
    parts = pl.pallas_call(
        functools.partial(add_kernel, chips, groups, held),
        out_shape=[part_shape] * groups,
        in_specs=[VMEM] * stripes,
        out_specs=[VMEM] * groups,
        scratch_shapes=[pltpu.VMEM((2, rows + tile_rows, depth), f32)],
        compiler_params=PARAMS,
        name="add_stripes",
    )(stacks[0], *came)

    def along(values, hop):
        return lax.ppermute(values, "grp", [(g, g ^ hop) for g in range(groups)])

    def by_core(values, odd_hop, even_hop):
        pairs = [
            (g * owners + t, (g ^ (odd_hop if t % 2 else even_hop)) * owners + t)
            for g in range(groups)
            for t in range(owners)
        ]
        return lax.ppermute(values, ("grp", "tile"), pairs)

    hops = zip(parts[1:], far_first(groups), near_first(groups))
    parts = [parts[0]] + [by_core(*each) for each in hops]
    grads = pl.pallas_call(
        functools.partial(grads_kernel, 1.0 / math.sqrt(groups * owners), groups),
        out_shape=part_shape,
        in_specs=[VMEM] * (groups + 2),
        out_specs=VMEM,
        compiler_params=PARAMS,
        name="gradients",
    )(*parts, near_speed.reshape(rows, depth), near_density.reshape(rows, depth))

    whole = jnp.zeros((2, groups, part, depth), f32)
    for hop in [0] + far_first(groups):
        values = grads if hop == 0 else along(grads, hop)
        place = my_group ^ hop
        whole = lax.dynamic_update_slice_in_dim(whole, values[:, None], place, axis=1)
    return (whole[0].reshape(speed.shape), whole[1].reshape(speed.shape))


def solution(mesh):
    return jax.shard_map(
        per_device,
        mesh=mesh,
        in_specs=(
            P("tile", None, None, None),
            P("tile", None, None, None),
            P(("grp", "tile"), None, None, None, None),
            P(("grp", "tile"), None, None, None, None),
            P(("grp", "tile"), None),
            P(("grp", "tile"), None),
            P(("grp", "tile"), None),
            P(("grp", "tile"), None, None),
            P(("grp", "tile"), None, None),
        ),
        out_specs=(P("tile", None, None, None), P("tile", None, None, None)),
        check_vma=False,
    )
```

```python
import functools
import math

import jax
import jax.numpy as jnp
from jax import lax
from jax.experimental import pallas as pl
from jax.experimental.pallas import tpu as pltpu
from jax.sharding import PartitionSpec as P

COEF = (1225.0 / 1024.0, -245.0 / 3072.0, 49.0 / 5120.0, -5.0 / 7168.0)
REACH = 4
EDGE = 8
ROWS = 8
SPAN = 8

SMEM = pl.BlockSpec(memory_space=pltpu.SMEM)
VMEM = pl.BlockSpec(memory_space=pltpu.VMEM)
PARAMS = pltpu.CompilerParams(vmem_limit_bytes=36 * 1024 * 1024)


def entry_of(list_ref):
    return jnp.max(list_ref[0:1, 0:1].astype(jnp.float32)).astype(jnp.int32)


def combine(ahead, behind):
    total = None
    for order in range(1, 5):
        upper, lower = ahead(order), behind(order)
        if upper is None and lower is None:
            continue
        if lower is None:
            term = upper
        elif upper is None:
            term = -lower
        else:
            term = upper - lower
        if order > 1:
            term = (COEF[order - 1] / COEF[0]) * term
        total = term if total is None else total + term
    return total


def band(first, depth):
    source = lax.broadcasted_iota(jnp.int32, (depth, depth), 0)
    target = lax.broadcasted_iota(jnp.int32, (depth, depth), 1)
    total = jnp.zeros((depth, depth), jnp.float32)
    for order in range(1, 5):
        weight = COEF[order - 1] / COEF[0]
        total = total + jnp.where(source == target + (first + order - 1), weight, 0.0)
        total = total - jnp.where(source == target + (first - order), weight, 0.0)
    return jnp.concatenate(halves(total), axis=1)


def halves(values):
    high = values.astype(jnp.bfloat16)
    return high, (values - high.astype(jnp.float32)).astype(jnp.bfloat16)


def along_z(values, matrix):
    xs, ys, zs = values.shape
    pair = jnp.concatenate(halves(values.reshape(xs * ys, zs)), axis=1)
    parts = jnp.dot(pair, matrix, preferred_element_type=jnp.float32)
    return (parts[:, :zs] + parts[:, zs:]).reshape(xs, ys, zs)


def blocks(xs, ys, body):
    if xs <= SPAN:
        for y0 in range(0, ys, ROWS):
            body(0, xs, y0)
        return

    def span(index, _):
        for y0 in range(0, ys, ROWS):
            body(index * SPAN, SPAN, y0)
        return 0

    lax.fori_loop(0, xs // SPAN, span, 0)


def window(xs, x0, load):
    kept = {}

    def at(offset):
        if xs <= SPAN and not 0 <= offset < xs:
            return None
        if offset not in kept:
            kept[offset] = load(x0 + offset)
        return kept[offset]

    return at


def slopes(xs, p, x0, y0, plane, offset):
    centre = plane(offset)
    here = x0 + offset + REACH
    return (
        combine(lambda k: plane(offset + k), lambda k: plane(offset + 1 - k)),
        combine(
            lambda k: p[here, pl.ds(EDGE + y0 + k, ROWS)],
            lambda k: centre if k == 1 else p[here, pl.ds(EDGE + y0 + 1 - k, ROWS)],
        ),
    )


def prepare_kernel(
    steps, fwd, adj, src, wave, rec, res, _piece,
    fwd_slope, adj_slope, fwd_source, adj_source, ahead, behind, *fields,
):
    xs, ys, zs = fwd_slope.shape[1:]
    for ref, first in ((ahead, 1), (behind, 0)):
        one = band(first, zs)
        ref[:zs] = one
        ref[zs:] = one

    def clear(ref):
        ref[...] = jnp.zeros(ref.shape, jnp.float32)

    for state, (p, v0, v1, v2), slope in (
        (fwd, fields[:4], fwd_slope),
        (adj, fields[4:], adj_slope),
    ):
        for ref in (p, v0):
            clear(ref.at[:REACH])
            clear(ref.at[REACH + xs :])
        for ref in (p.at[pl.ds(REACH, xs)], v1):
            clear(ref.at[:, :EDGE])
            clear(ref.at[:, EDGE + ys :])
        for x in range(xs):
            p[REACH + x, EDGE : EDGE + ys] = state[0, 0, x].astype(jnp.float32)
            v0[REACH + x] = state[0, 1, x].astype(jnp.float32)
            v1[x, EDGE : EDGE + ys] = state[0, 2, x].astype(jnp.float32)
            v2[x] = state[0, 3, x].astype(jnp.float32)

        def block(x0, count, y0, p=p, slope=slope):
            plane = window(xs, x0, lambda x: p[REACH + x, pl.ds(EDGE + y0, ROWS)])
            for offset in range(count):
                for d, values in enumerate(slopes(xs, p, x0, y0, plane, offset)):
                    slope[d, x0 + offset, pl.ds(y0, ROWS)] = values

        blocks(xs, ys, block)
        slope[2] = along_z(p[REACH : REACH + xs, EDGE : EDGE + ys], ahead[...])

    row = lax.broadcasted_iota(jnp.int32, (ys, zs), 0)
    lane = lax.broadcasted_iota(jnp.int32, (ys, zs), 1)
    src_mark = (row == src[0, 1]) & (lane == src[0, 2])
    for x in range(xs):
        rec_mark = (row == rec[0, 0, x]) & (lane == rec[0, 1, x])
        for step in range(steps):
            amplitude = jnp.where(x == src[0, 0], wave[0, step], 0.0)
            fwd_source[step, x] = jnp.where(src_mark, amplitude, 0.0)
            adj_source[step, x] = jnp.where(rec_mark, res[0, step, x], 0.0)


def near_kernel(speed, density, aperture, near_speed, near_density, entry):
    near_speed[...] = speed[...]
    near_density[...] = density[...]
    entry[...] = jnp.full(entry.shape, entry_of(aperture), jnp.int32)


def pick_kernel(chips, near_speed, near_density, far_speed, far_density, *refs):
    stripes = 2 * chips
    lists, outs = refs[:stripes], refs[stripes:]
    held = near_speed.shape[0]
    me = lax.axis_index("tile")
    residue, half = lax.rem(me, stripes), lax.div(me, stripes)
    for hop in range(stripes):
        entry = entry_of(lists[hop])
        corner, column = lax.div(entry, held), lax.rem(entry, held)
        here = (residue >= corner) == (half == 0)
        piece = outs[hop]

        @pl.when(here)
        def _():
            piece[0] = near_speed[column]
            piece[1] = near_density[column]

        @pl.when(jnp.logical_not(here))
        def _():
            piece[0] = far_speed[column]
            piece[1] = far_density[column]


def wave_kernel(chips, steps, held, *refs):
    stripes = 2 * chips
    pieces, refs = refs[:stripes], refs[stripes:]
    fwd_slope, adj_slope, fwd_source, adj_source, ahead, behind, entry_ref = refs[:7]
    kept, traded, p, v0, v1, v2, q, w0, w1, w2 = refs[15:25]
    bulk, buoy, dp, dv, bulk_img, buoy_img, across_z, flat = refs[25:]
    tile_x, tile_y = pieces[0].shape[1:3]
    xs, ys, zs = bulk.shape
    residue = lax.rem(lax.axis_index("tile"), stripes)
    entry = entry_of(entry_ref)
    corner = lax.div(entry, held)

    def place_of(hop):
        return lax.rem((residue ^ hop) - corner + stripes, stripes) * tile_x

    for hop in range(stripes):
        cells = pl.ds(place_of(hop), tile_x)
        speed, density = pieces[hop][0], pieces[hop][1]
        bulk[cells] = COEF[0] * (density * speed * speed)
        buoy[cells] = COEF[0] / density

    def push(fields, first, note):
        p, v0, v1, v2 = fields
        if first is None:
            across_z[...] = along_z(p[REACH : REACH + xs, EDGE : EDGE + ys], ahead[...])

        def block(x0, count, y0):
            rows, inner = pl.ds(y0, ROWS), pl.ds(EDGE + y0, ROWS)
            plane = window(xs, x0, lambda x: p[REACH + x, inner])
            for offset in range(count):
                x = x0 + offset
                if first is None:
                    two = slopes(xs, p, x0, y0, plane, offset)
                else:
                    two = (first[0, x, rows], first[1, x, rows])
                places = ((v0, REACH + x, rows), (v1, x, inner))
                for d, (ref, at, span) in enumerate(places):
                    change = buoy[x, rows] * two[d]
                    moved = ref[at, span] + change
                    ref[at, span] = moved
                    note(d, x, rows, change, moved)

        def block_z(x0, count, y0):
            rows = pl.ds(y0, ROWS)
            for x in range(count):
                x = x0 + x
                slope = across_z[x, rows] if first is None else first[2, x, rows]
                change = buoy[x, rows] * slope
                moved = v2[x, rows] + change
                v2[x, rows] = moved
                note(2, x, rows, change, moved)

        blocks(xs, ys, block)
        blocks(xs, ys, block_z)

    def spread(fields, source, step, note):
        p, v0, v1, v2 = fields
        across_z[...] = along_z(v2[...], behind[...])

        def block(x0, count, y0):
            rows = pl.ds(y0, ROWS)
            plane = window(xs, x0, lambda x: v0[REACH + x, rows])
            for offset in range(count):
                x = x0 + offset
                along_x = combine(lambda k: plane(offset + k - 1), lambda k: plane(offset - k))
                along_y = combine(
                    lambda k: v1[x, pl.ds(EDGE + y0 + k - 1, ROWS)],
                    lambda k: v1[x, pl.ds(EDGE + y0 - k, ROWS)],
                )
                flat[x, rows] = along_x + along_y

        def block_z(x0, count, y0):
            rows, inner = pl.ds(y0, ROWS), pl.ds(EDGE + y0, ROWS)
            for x in range(count):
                x = x0 + x
                change = bulk[x, rows] * (flat[x, rows] + across_z[x, rows])
                change = change + source[step, x, rows]
                moved = p[REACH + x, inner] + change
                p[REACH + x, inner] = moved
                note(x, rows, change, moved)

        blocks(xs, ys, block)
        blocks(xs, ys, block_z)

    fields = (p, v0, v1, v2)
    for step in range(steps):

        def keep_dv(d, x, rows, change, moved, step=step):
            dv[step, d, x, rows] = change

        def keep_dp(x, rows, change, moved, step=step):
            dp[step, x, rows] = change

        push(fields, fwd_slope if step == 0 else None, keep_dv)
        spread(fields, fwd_source, step, keep_dp)

    fields = (q, w0, w1, w2)
    for step in reversed(range(steps)):
        last = step == steps - 1

        def add_buoy(d, x, rows, change, moved, step=step, last=last):
            image = dv[step, d, x, rows] * moved
            buoy_img[x, rows] = image if last and d == 0 else buoy_img[x, rows] + image

        def add_bulk(x, rows, change, moved, step=step, last=last):
            image = dp[step, x, rows] * moved
            bulk_img[x, rows] = image if last else bulk_img[x, rows] + image

        push(fields, adj_slope if last else None, add_buoy)
        spread(fields, adj_source, step, add_bulk)

    tile_rows = tile_x * tile_y
    for chip in range(chips):
        for ref, hop in ((kept, 2 * chip), (traded, 2 * chip + 1)):
            cells = pl.ds(place_of(hop), tile_x)
            ref[chip, :tile_rows] = bulk_img[cells].reshape(tile_rows, zs)
            ref[chip, tile_rows : 2 * tile_rows] = buoy_img[cells].reshape(tile_rows, zs)
            ref[chip, 2 * tile_rows :] = jnp.full((8, zs), entry).astype(jnp.float32)


def merge_kernel(chips, kept, came, *outs):
    for chip in range(chips):
        outs[chip][0] = kept[chip]
        outs[chip][1] = came[chip]


def add_kernel(chips, groups, held, *refs):
    came, parts, total = refs[: 2 * chips], refs[2 * chips : 2 * chips + groups], refs[-1]
    stripes = 2 * chips
    me, group = lax.axis_index("tile"), lax.axis_index("grp")
    tile_rows = total.shape[1] // (held + 1)
    part = parts[0].shape[1]
    total[...] = jnp.zeros_like(total)
    for pair in came:
        for shot in range(2):
            entry = jnp.max(pair[shot, 2 * tile_rows :]).astype(jnp.int32)
            corner, column = lax.div(entry, held), lax.rem(entry, held)
            mine = (corner <= me) & (me < corner + stripes)
            slot = jnp.where(mine, column, held)
            rows = pl.ds(pl.multiple_of(slot * tile_rows, tile_rows), tile_rows)
            for field in range(2):
                sent = pair[shot, field * tile_rows : (field + 1) * tile_rows]
                total[field, rows] = total[field, rows] + sent
    for index, hop in enumerate([0] + far_first(groups)):
        first = pl.multiple_of((group ^ hop) * part, part)
        for field in range(2):
            parts[index][field] = total[field, pl.ds(first, part)]


def far_first(groups):
    return list(range(groups - 1, 0, -1))


def grads_kernel(scale, groups, *refs):
    parts, speed_ref, density_ref, grads = refs[:groups], *refs[groups:]
    part = parts[0].shape[1]
    rows = pl.ds(pl.multiple_of(lax.axis_index("grp") * part, part), part)
    speed, density = speed_ref[rows], density_ref[rows]
    bulk_sum, buoy_sum = parts[0][0], parts[0][1]
    for other in parts[1:]:
        bulk_sum = bulk_sum + other[0]
        buoy_sum = buoy_sum + other[1]
    grads[0] = scale * (bulk_sum * (2.0 * density * speed))
    grads[1] = scale * (bulk_sum * (speed * speed) - buoy_sum / (density * density))


def per_device(speed, density, fwd_state, adj_state, aperture, src_pos, wavelet, rec_pos, residual):
    owners = lax.axis_size("tile")
    groups = lax.axis_size("grp")
    my_group = lax.axis_index("grp")
    held, tile_x, tile_y, depth = speed.shape
    stripes = aperture.shape[1]
    chips = stripes // 2
    steps = wavelet.shape[1]
    xs = stripes * tile_x
    f32 = jnp.float32
    cells = (xs, tile_y, depth)

    def shape(*dims):
        return jax.ShapeDtypeStruct(dims, f32)

    def across(values, hop):
        return lax.ppermute(values, "tile", [(t, t ^ hop) for t in range(owners)])

    far_speed = across(speed, stripes)
    far_density = across(density, stripes)
    lists = {hop: across(aperture, hop) for hop in range(stripes - 1, 0, -1)}
    four = [
        (xs + 2 * REACH, tile_y + 2 * EDGE, depth),
        (xs + 2 * REACH, tile_y, depth),
        (xs, tile_y + 2 * EDGE, depth),
        cells,
    ]
    near_speed, near_density, entry = pl.pallas_call(
        near_kernel,
        out_shape=[
            shape(*speed.shape),
            shape(*speed.shape),
            jax.ShapeDtypeStruct((8, depth), jnp.int32),
        ],
        in_specs=[VMEM] * 3,
        out_specs=[VMEM] * 3,
        compiler_params=PARAMS,
        cost_estimate=pl.CostEstimate(flops=4_000_000, bytes_accessed=6_000_000, transcendentals=0),
        name="hold_near_tiles",
    )(speed, density, aperture)
    pieces = pl.pallas_call(
        functools.partial(pick_kernel, chips),
        out_shape=[shape(2, tile_x, tile_y, depth)] * stripes,
        in_specs=[VMEM] * (4 + stripes),
        out_specs=[VMEM] * stripes,
        compiler_params=PARAMS,
        name="pick_tiles",
    )(near_speed, near_density, far_speed, far_density, entry, *[lists[h] for h in range(1, stripes)])
    moved = {hop: across(pieces[hop], hop) for hop in range(stripes - 1, 0, -1)}

    prepared = pl.pallas_call(
        functools.partial(prepare_kernel, steps),
        out_shape=[shape(3, *cells)] * 2
        + [shape(steps, *cells)] * 2
        + [jax.ShapeDtypeStruct((2 * depth, 2 * depth), jnp.bfloat16)] * 2
        + [shape(*dims) for dims in four + four],
        in_specs=[VMEM] * 2 + [SMEM] * 4 + [VMEM],
        out_specs=[VMEM] * 14,
        compiler_params=PARAMS,
        cost_estimate=pl.CostEstimate(flops=4_000_000, bytes_accessed=6_000_000, transcendentals=0),
        name="prepare",
    )(fwd_state, adj_state, src_pos, wavelet, jnp.swapaxes(rec_pos, 1, 2), residual, pieces[0])
    prepared, fields = prepared[:6], prepared[6:]
    pieces = [pieces[0]] + [moved[hop] for hop in range(1, stripes)]

    tile_rows = tile_x * tile_y
    sent = shape(chips, 2 * tile_rows + 8, depth)
    kept, traded, *_ = pl.pallas_call(
        functools.partial(wave_kernel, chips, steps, held),
        out_shape=[sent, sent] + [shape(*dims) for dims in four + four],
        in_specs=[VMEM] * (stripes + 15),
        out_specs=[VMEM] * 10,
        scratch_shapes=[
            pltpu.VMEM(cells, f32),
            pltpu.VMEM(cells, f32),
            pltpu.VMEM((steps,) + cells, f32),
            pltpu.VMEM((steps, 3) + cells, f32),
            pltpu.VMEM(cells, f32),
            pltpu.VMEM(cells, f32),
            pltpu.VMEM(cells, f32),
            pltpu.VMEM(cells, f32),
        ],
        input_output_aliases={stripes + 7 + index: 2 + index for index in range(8)},
        compiler_params=PARAMS,
        name="replay_and_adjoint",
    )(*pieces, *prepared, entry, *fields)

    both = shape(2, 2 * tile_rows + 8, depth)
    stacks = pl.pallas_call(
        functools.partial(merge_kernel, chips),
        out_shape=[both] * chips,
        in_specs=[VMEM] * 2,
        out_specs=[VMEM] * chips,
        compiler_params=PARAMS,
        name="merge_pair",
    )(kept, across(traded, 1))
    came = [
        across(stacks[chip], 2 * chip + stripes * half)
        for half in range(2)
        for chip in range(chips)
        if chip or half
    ]

    rows = held * tile_rows
    part = rows // groups
    part_shape = shape(2, part, depth)
    parts = pl.pallas_call(
        functools.partial(add_kernel, chips, groups, held),
        out_shape=[part_shape] * groups,
        in_specs=[VMEM] * stripes,
        out_specs=[VMEM] * groups,
        scratch_shapes=[pltpu.VMEM((2, rows + tile_rows, depth), f32)],
        compiler_params=PARAMS,
        name="add_stripes",
    )(stacks[0], *came)

    def along(values, hop):
        return lax.ppermute(values, "grp", [(g, g ^ hop) for g in range(groups)])

    parts = [parts[0]] + [along(values, hop) for values, hop in zip(parts[1:], far_first(groups))]
    grads = pl.pallas_call(
        functools.partial(grads_kernel, 1.0 / math.sqrt(groups * owners), groups),
        out_shape=part_shape,
        in_specs=[VMEM] * (groups + 2),
        out_specs=VMEM,
        compiler_params=PARAMS,
        name="gradients",
    )(*parts, near_speed.reshape(rows, depth), near_density.reshape(rows, depth))

    whole = jnp.zeros((2, groups, part, depth), f32)
    for hop in [0] + far_first(groups):
        values = grads if hop == 0 else along(grads, hop)
        place = my_group ^ hop
        whole = lax.dynamic_update_slice_in_dim(whole, values[:, None], place, axis=1)
    return (whole[0].reshape(speed.shape), whole[1].reshape(speed.shape))


def solution(mesh):
    return jax.shard_map(
        per_device,
        mesh=mesh,
        in_specs=(
            P("tile", None, None, None),
            P("tile", None, None, None),
            P(("grp", "tile"), None, None, None, None),
            P(("grp", "tile"), None, None, None, None),
            P(("grp", "tile"), None),
            P(("grp", "tile"), None),
            P(("grp", "tile"), None),
            P(("grp", "tile"), None, None),
            P(("grp", "tile"), None, None),
        ),
        out_specs=(P("tile", None, None, None), P("tile", None, None, None)),
        check_vma=False,
    )
```

```python
import functools
import math

import jax
import jax.numpy as jnp
from jax import lax
from jax.experimental import pallas as pl
from jax.experimental.pallas import tpu as pltpu
from jax.sharding import PartitionSpec as P

COEF = (1225.0 / 1024.0, -245.0 / 3072.0, 49.0 / 5120.0, -5.0 / 7168.0)
REACH = 4
EDGE = 8
ROWS = 8
SPAN = 8

SMEM = pl.BlockSpec(memory_space=pltpu.SMEM)
VMEM = pl.BlockSpec(memory_space=pltpu.VMEM)
PARAMS = pltpu.CompilerParams(vmem_limit_bytes=36 * 1024 * 1024)


def entry_of(list_ref):
    return jnp.max(list_ref[0:1, 0:1].astype(jnp.float32)).astype(jnp.int32)


def combine(ahead, behind):
    total = None
    for order in range(1, 5):
        upper, lower = ahead(order), behind(order)
        if upper is None and lower is None:
            continue
        if lower is None:
            term = upper
        elif upper is None:
            term = -lower
        else:
            term = upper - lower
        if order > 1:
            term = (COEF[order - 1] / COEF[0]) * term
        total = term if total is None else total + term
    return total


def band(first, depth):
    source = lax.broadcasted_iota(jnp.int32, (depth, depth), 0)
    target = lax.broadcasted_iota(jnp.int32, (depth, depth), 1)
    total = jnp.zeros((depth, depth), jnp.float32)
    for order in range(1, 5):
        weight = COEF[order - 1] / COEF[0]
        total = total + jnp.where(source == target + (first + order - 1), weight, 0.0)
        total = total - jnp.where(source == target + (first - order), weight, 0.0)
    return jnp.concatenate(halves(total), axis=1)


def halves(values):
    high = values.astype(jnp.bfloat16)
    return high, (values - high.astype(jnp.float32)).astype(jnp.bfloat16)


def along_z(values, matrix):
    xs, ys, zs = values.shape
    pair = jnp.concatenate(halves(values.reshape(xs * ys, zs)), axis=1)
    parts = jnp.dot(pair, matrix, preferred_element_type=jnp.float32)
    return (parts[:, :zs] + parts[:, zs:]).reshape(xs, ys, zs)


def blocks(xs, ys, body):
    if xs <= SPAN:
        for y0 in range(0, ys, ROWS):
            body(0, xs, y0)
        return

    def span(index, _):
        for y0 in range(0, ys, ROWS):
            body(index * SPAN, SPAN, y0)
        return 0

    lax.fori_loop(0, xs // SPAN, span, 0)


def window(xs, x0, load):
    kept = {}

    def at(offset):
        if xs <= SPAN and not 0 <= offset < xs:
            return None
        if offset not in kept:
            kept[offset] = load(x0 + offset)
        return kept[offset]

    return at


def slopes(xs, p, x0, y0, plane, offset):
    centre = plane(offset)
    here = x0 + offset + REACH
    return (
        combine(lambda k: plane(offset + k), lambda k: plane(offset + 1 - k)),
        combine(
            lambda k: p[here, pl.ds(EDGE + y0 + k, ROWS)],
            lambda k: centre if k == 1 else p[here, pl.ds(EDGE + y0 + 1 - k, ROWS)],
        ),
    )


def prepare_kernel(
    steps, fwd, adj, src, wave, rec, res, _piece,
    fwd_slope, adj_slope, fwd_source, adj_source, ahead, behind, *fields,
):
    xs, ys, zs = fwd_slope.shape[1:]
    for ref, first in ((ahead, 1), (behind, 0)):
        one = band(first, zs)
        ref[:zs] = one
        ref[zs:] = one

    def clear(ref):
        ref[...] = jnp.zeros(ref.shape, jnp.float32)

    for state, (p, v0, v1, v2), slope in (
        (fwd, fields[:4], fwd_slope),
        (adj, fields[4:], adj_slope),
    ):
        for ref in (p, v0):
            clear(ref.at[:REACH])
            clear(ref.at[REACH + xs :])
        for ref in (p.at[pl.ds(REACH, xs)], v1):
            clear(ref.at[:, :EDGE])
            clear(ref.at[:, EDGE + ys :])
        for x in range(xs):
            p[REACH + x, EDGE : EDGE + ys] = state[0, 0, x].astype(jnp.float32)
            v0[REACH + x] = state[0, 1, x].astype(jnp.float32)
            v1[x, EDGE : EDGE + ys] = state[0, 2, x].astype(jnp.float32)
            v2[x] = state[0, 3, x].astype(jnp.float32)

        def block(x0, count, y0, p=p, slope=slope):
            plane = window(xs, x0, lambda x: p[REACH + x, pl.ds(EDGE + y0, ROWS)])
            for offset in range(count):
                for d, values in enumerate(slopes(xs, p, x0, y0, plane, offset)):
                    slope[d, x0 + offset, pl.ds(y0, ROWS)] = values

        blocks(xs, ys, block)
        slope[2] = along_z(p[REACH : REACH + xs, EDGE : EDGE + ys], ahead[...])

    row = lax.broadcasted_iota(jnp.int32, (ys, zs), 0)
    lane = lax.broadcasted_iota(jnp.int32, (ys, zs), 1)
    src_mark = (row == src[0, 1]) & (lane == src[0, 2])
    for x in range(xs):
        rec_mark = (row == rec[0, 0, x]) & (lane == rec[0, 1, x])
        for step in range(steps):
            amplitude = jnp.where(x == src[0, 0], wave[0, step], 0.0)
            fwd_source[step, x] = jnp.where(src_mark, amplitude, 0.0)
            adj_source[step, x] = jnp.where(rec_mark, res[0, step, x], 0.0)


def near_kernel(speed, density, aperture, near_speed, near_density, entry):
    near_speed[...] = speed[...]
    near_density[...] = density[...]
    entry[...] = jnp.full(entry.shape, entry_of(aperture), jnp.int32)


def pick_kernel(chips, near_speed, near_density, far_speed, far_density, *refs):
    stripes = 2 * chips
    lists, outs = refs[:stripes], refs[stripes:]
    held = near_speed.shape[0]
    me = lax.axis_index("tile")
    residue, half = lax.rem(me, stripes), lax.div(me, stripes)
    for hop in range(stripes):
        entry = entry_of(lists[hop])
        corner, column = lax.div(entry, held), lax.rem(entry, held)
        here = (residue >= corner) == (half == 0)
        piece = outs[hop]

        @pl.when(here)
        def _():
            piece[0] = near_speed[column]
            piece[1] = near_density[column]

        @pl.when(jnp.logical_not(here))
        def _():
            piece[0] = far_speed[column]
            piece[1] = far_density[column]


def wave_kernel(chips, steps, held, *refs):
    stripes = 2 * chips
    pieces, refs = refs[:stripes], refs[stripes:]
    fwd_slope, adj_slope, fwd_source, adj_source, ahead, behind, entry_ref = refs[:7]
    kept, traded, p, v0, v1, v2, q, w0, w1, w2 = refs[15:25]
    bulk, buoy, dp, dv, bulk_img, buoy_img, across_z, flat = refs[25:]
    tile_x, tile_y = pieces[0].shape[1:3]
    xs, ys, zs = bulk.shape
    residue = lax.rem(lax.axis_index("tile"), stripes)
    entry = entry_of(entry_ref)
    corner = lax.div(entry, held)

    def place_of(hop):
        return lax.rem((residue ^ hop) - corner + stripes, stripes) * tile_x

    for hop in range(stripes):
        cells = pl.ds(place_of(hop), tile_x)
        speed, density = pieces[hop][0], pieces[hop][1]
        bulk[cells] = COEF[0] * (density * speed * speed)
        buoy[cells] = COEF[0] / density

    def push(fields, first, note):
        p, v0, v1, v2 = fields
        if first is None:
            across_z[...] = along_z(p[REACH : REACH + xs, EDGE : EDGE + ys], ahead[...])

        def block(x0, count, y0):
            rows, inner = pl.ds(y0, ROWS), pl.ds(EDGE + y0, ROWS)
            plane = window(xs, x0, lambda x: p[REACH + x, inner])
            for offset in range(count):
                x = x0 + offset
                if first is None:
                    two = slopes(xs, p, x0, y0, plane, offset)
                else:
                    two = (first[0, x, rows], first[1, x, rows])
                places = ((v0, REACH + x, rows), (v1, x, inner))
                for d, (ref, at, span) in enumerate(places):
                    change = buoy[x, rows] * two[d]
                    moved = ref[at, span] + change
                    ref[at, span] = moved
                    note(d, x, rows, change, moved)

        def block_z(x0, count, y0):
            rows = pl.ds(y0, ROWS)
            for x in range(count):
                x = x0 + x
                slope = across_z[x, rows] if first is None else first[2, x, rows]
                change = buoy[x, rows] * slope
                moved = v2[x, rows] + change
                v2[x, rows] = moved
                note(2, x, rows, change, moved)

        blocks(xs, ys, block)
        blocks(xs, ys, block_z)

    def spread(fields, source, step, note):
        p, v0, v1, v2 = fields
        across_z[...] = along_z(v2[...], behind[...])

        def block(x0, count, y0):
            rows = pl.ds(y0, ROWS)
            plane = window(xs, x0, lambda x: v0[REACH + x, rows])
            for offset in range(count):
                x = x0 + offset
                along_x = combine(lambda k: plane(offset + k - 1), lambda k: plane(offset - k))
                along_y = combine(
                    lambda k: v1[x, pl.ds(EDGE + y0 + k - 1, ROWS)],
                    lambda k: v1[x, pl.ds(EDGE + y0 - k, ROWS)],
                )
                flat[x, rows] = along_x + along_y

        def block_z(x0, count, y0):
            rows, inner = pl.ds(y0, ROWS), pl.ds(EDGE + y0, ROWS)
            for x in range(count):
                x = x0 + x
                change = bulk[x, rows] * (flat[x, rows] + across_z[x, rows])
                change = change + source[step, x, rows]
                moved = p[REACH + x, inner] + change
                p[REACH + x, inner] = moved
                note(x, rows, change, moved)

        blocks(xs, ys, block)
        blocks(xs, ys, block_z)

    fields = (p, v0, v1, v2)
    for step in range(steps):

        def keep_dv(d, x, rows, change, moved, step=step):
            dv[step, d, x, rows] = change

        def keep_dp(x, rows, change, moved, step=step):
            dp[step, x, rows] = change

        push(fields, fwd_slope if step == 0 else None, keep_dv)
        spread(fields, fwd_source, step, keep_dp)

    fields = (q, w0, w1, w2)
    for step in reversed(range(steps)):
        last = step == steps - 1

        def add_buoy(d, x, rows, change, moved, step=step, last=last):
            image = dv[step, d, x, rows] * moved
            buoy_img[x, rows] = image if last and d == 0 else buoy_img[x, rows] + image

        def add_bulk(x, rows, change, moved, step=step, last=last):
            image = dp[step, x, rows] * moved
            bulk_img[x, rows] = image if last else bulk_img[x, rows] + image

        push(fields, adj_slope if last else None, add_buoy)
        spread(fields, adj_source, step, add_bulk)

    tile_rows = tile_x * tile_y
    for chip in range(chips):
        for ref, hop in ((kept, 2 * chip), (traded, 2 * chip + 1)):
            cells = pl.ds(place_of(hop), tile_x)
            ref[chip, :tile_rows] = bulk_img[cells].reshape(tile_rows, zs)
            ref[chip, tile_rows : 2 * tile_rows] = buoy_img[cells].reshape(tile_rows, zs)
            ref[chip, 2 * tile_rows :] = jnp.full((8, zs), entry).astype(jnp.float32)


def merge_kernel(chips, kept, came, *outs):
    tile_rows = (kept.shape[1] - 8) // 2
    half = lax.div(lax.axis_index("tile"), 2 * chips)
    for index, out in enumerate(outs):
        chip, other = index % chips, index // chips
        field = jnp.where(half == other, 0, 1)
        rows = pl.ds(pl.multiple_of(field * tile_rows, tile_rows), tile_rows)
        for shot, source in enumerate((kept, came)):
            out[shot * tile_rows : (shot + 1) * tile_rows] = source[chip, rows]
            first = 2 * tile_rows + 4 * shot
            out[first : first + 4] = source[chip, 2 * tile_rows : 2 * tile_rows + 4]


def add_kernel(stripes, groups, held, *refs):
    came, parts, total = refs[:stripes], refs[stripes:-1], refs[-1]
    me, group = lax.axis_index("tile"), lax.axis_index("grp")
    residue, half = lax.rem(me, stripes), lax.div(me, stripes)
    tile_rows = total.shape[0] // (2 * held)
    part = parts[0].shape[0]
    total[...] = jnp.zeros_like(total)
    for pair in came:
        for shot in range(2):
            first = 2 * tile_rows + 4 * shot
            entry = jnp.max(pair[first : first + 4]).astype(jnp.int32)
            corner, column = lax.div(entry, held), lax.rem(entry, held)
            slot = jnp.where(residue < corner, held, 0) + column
            rows = pl.ds(pl.multiple_of(slot * tile_rows, tile_rows), tile_rows)
            total[rows] = total[rows] + pair[shot * tile_rows : (shot + 1) * tile_rows]
    for out, (hop, flip) in zip(parts, part_order(groups)):
        owner = jnp.where(half == flip, 0, 1)
        first = owner * (held * tile_rows) + (group ^ hop) * part
        out[...] = total[pl.ds(pl.multiple_of(first, part), part)]


def part_order(groups):
    hops = [(hop, flip) for hop in far_first(groups) for flip in range(2)]
    return [(0, 0)] + hops + [(0, 1)]


def far_first(groups):
    return list(range(groups - 1, 0, -1))


def grads_kernel(scale, groups, stripes, *refs):
    parts, speed_ref, density_ref, grads = refs[: 2 * groups], *refs[2 * groups :]
    part = parts[0].shape[0]
    rows = pl.ds(pl.multiple_of(lax.axis_index("grp") * part, part), part)
    speed, density = speed_ref[rows], density_ref[rows]
    sums = [None, None]
    for values, (_, flip) in zip(parts, part_order(groups)):
        sums[flip] = values[...] if sums[flip] is None else sums[flip] + values[...]
    first_half = lax.axis_index("tile") < stripes
    bulk_sum = jnp.where(first_half, sums[0], sums[1])
    buoy_sum = jnp.where(first_half, sums[1], sums[0])
    grads[0] = scale * (bulk_sum * (2.0 * density * speed))
    grads[1] = scale * (bulk_sum * (speed * speed) - buoy_sum / (density * density))


def per_device(speed, density, fwd_state, adj_state, aperture, src_pos, wavelet, rec_pos, residual):
    owners = lax.axis_size("tile")
    groups = lax.axis_size("grp")
    my_group = lax.axis_index("grp")
    held, tile_x, tile_y, depth = speed.shape
    stripes = aperture.shape[1]
    chips = stripes // 2
    steps = wavelet.shape[1]
    xs = stripes * tile_x
    f32 = jnp.float32
    cells = (xs, tile_y, depth)

    def shape(*dims):
        return jax.ShapeDtypeStruct(dims, f32)

    def across(values, hop):
        return lax.ppermute(values, "tile", [(t, t ^ hop) for t in range(owners)])

    far_speed = across(speed, stripes)
    far_density = across(density, stripes)
    lists = {hop: across(aperture, hop) for hop in range(stripes - 1, 0, -1)}
    four = [
        (xs + 2 * REACH, tile_y + 2 * EDGE, depth),
        (xs + 2 * REACH, tile_y, depth),
        (xs, tile_y + 2 * EDGE, depth),
        cells,
    ]
    near_speed, near_density, entry = pl.pallas_call(
        near_kernel,
        out_shape=[
            shape(*speed.shape),
            shape(*speed.shape),
            jax.ShapeDtypeStruct((8, depth), jnp.int32),
        ],
        in_specs=[VMEM] * 3,
        out_specs=[VMEM] * 3,
        compiler_params=PARAMS,
        cost_estimate=pl.CostEstimate(flops=4_000_000, bytes_accessed=6_000_000, transcendentals=0),
        name="hold_near_tiles",
    )(speed, density, aperture)
    pieces = pl.pallas_call(
        functools.partial(pick_kernel, chips),
        out_shape=[shape(2, tile_x, tile_y, depth)] * stripes,
        in_specs=[VMEM] * (4 + stripes),
        out_specs=[VMEM] * stripes,
        compiler_params=PARAMS,
        name="pick_tiles",
    )(near_speed, near_density, far_speed, far_density, entry, *[lists[h] for h in range(1, stripes)])
    moved = {hop: across(pieces[hop], hop) for hop in range(stripes - 1, 0, -1)}

    prepared = pl.pallas_call(
        functools.partial(prepare_kernel, steps),
        out_shape=[shape(3, *cells)] * 2
        + [shape(steps, *cells)] * 2
        + [jax.ShapeDtypeStruct((2 * depth, 2 * depth), jnp.bfloat16)] * 2
        + [shape(*dims) for dims in four + four],
        in_specs=[VMEM] * 2 + [SMEM] * 4 + [VMEM],
        out_specs=[VMEM] * 14,
        compiler_params=PARAMS,
        cost_estimate=pl.CostEstimate(flops=4_000_000, bytes_accessed=6_000_000, transcendentals=0),
        name="prepare",
    )(fwd_state, adj_state, src_pos, wavelet, jnp.swapaxes(rec_pos, 1, 2), residual, pieces[0])
    prepared, fields = prepared[:6], prepared[6:]
    pieces = [pieces[0]] + [moved[hop] for hop in range(1, stripes)]

    tile_rows = tile_x * tile_y
    sent = shape(chips, 2 * tile_rows + 8, depth)
    kept, traded, *_ = pl.pallas_call(
        functools.partial(wave_kernel, chips, steps, held),
        out_shape=[sent, sent] + [shape(*dims) for dims in four + four],
        in_specs=[VMEM] * (stripes + 15),
        out_specs=[VMEM] * 10,
        scratch_shapes=[
            pltpu.VMEM(cells, f32),
            pltpu.VMEM(cells, f32),
            pltpu.VMEM((steps,) + cells, f32),
            pltpu.VMEM((steps, 3) + cells, f32),
            pltpu.VMEM(cells, f32),
            pltpu.VMEM(cells, f32),
            pltpu.VMEM(cells, f32),
            pltpu.VMEM(cells, f32),
        ],
        input_output_aliases={stripes + 7 + index: 2 + index for index in range(8)},
        compiler_params=PARAMS,
        name="replay_and_adjoint",
    )(*pieces, *prepared, entry, *fields)

    stacks = pl.pallas_call(
        functools.partial(merge_kernel, chips),
        out_shape=[shape(2 * tile_rows + 8, depth)] * stripes,
        in_specs=[VMEM] * 2,
        out_specs=[VMEM] * stripes,
        compiler_params=PARAMS,
        name="merge_pair",
    )(kept, across(traded, 1))
    came = [across(stacks[chip], 2 * chip) if chip else stacks[0] for chip in range(stripes)]

    rows = held * tile_rows
    part = rows // groups
    parts = pl.pallas_call(
        functools.partial(add_kernel, stripes, groups, held),
        out_shape=[shape(part, depth)] * (2 * groups),
        in_specs=[VMEM] * stripes,
        out_specs=[VMEM] * (2 * groups),
        scratch_shapes=[pltpu.VMEM((2 * rows, depth), f32)],
        compiler_params=PARAMS,
        name="add_stripes",
    )(*came)

    def along(values, hop, flip=0):
        pairs = [
            (g * owners + t, (g ^ hop) * owners + (t ^ (flip * stripes)))
            for g in range(groups)
            for t in range(owners)
        ]
        return lax.ppermute(values, ("grp", "tile"), pairs)

    parts = [
        along(values, *hops) if any(hops) else values
        for values, hops in zip(parts, part_order(groups))
    ]
    grads = pl.pallas_call(
        functools.partial(grads_kernel, 1.0 / math.sqrt(groups * owners), groups, stripes),
        out_shape=shape(2, part, depth),
        in_specs=[VMEM] * (2 * groups + 2),
        out_specs=VMEM,
        compiler_params=PARAMS,
        name="gradients",
    )(*parts, near_speed.reshape(rows, depth), near_density.reshape(rows, depth))

    whole = jnp.zeros((2, groups, part, depth), f32)
    for hop in [0] + far_first(groups):
        values = grads if hop == 0 else along(grads, hop)
        place = my_group ^ hop
        whole = lax.dynamic_update_slice_in_dim(whole, values[:, None], place, axis=1)
    return (whole[0].reshape(speed.shape), whole[1].reshape(speed.shape))


def solution(mesh):
    return jax.shard_map(
        per_device,
        mesh=mesh,
        in_specs=(
            P("tile", None, None, None),
            P("tile", None, None, None),
            P(("grp", "tile"), None, None, None, None),
            P(("grp", "tile"), None, None, None, None),
            P(("grp", "tile"), None),
            P(("grp", "tile"), None),
            P(("grp", "tile"), None),
            P(("grp", "tile"), None, None),
            P(("grp", "tile"), None, None),
        ),
        out_specs=(P("tile", None, None, None), P("tile", None, None, None)),
        check_vma=False,
    )
```

```python
import functools
import math

import jax
import jax.numpy as jnp
from jax import lax
from jax.experimental import pallas as pl
from jax.experimental.pallas import tpu as pltpu
from jax.sharding import PartitionSpec as P

COEF = (1225.0 / 1024.0, -245.0 / 3072.0, 49.0 / 5120.0, -5.0 / 7168.0)
REACH = 4
EDGE = 8
ROWS = 8
SPAN = 8

SMEM = pl.BlockSpec(memory_space=pltpu.SMEM)
VMEM = pl.BlockSpec(memory_space=pltpu.VMEM)
PARAMS = pltpu.CompilerParams(vmem_limit_bytes=36 * 1024 * 1024)


def entry_of(list_ref):
    return jnp.max(list_ref[0:1, 0:1].astype(jnp.float32)).astype(jnp.int32)


def combine(ahead, behind):
    total = None
    for order in range(1, 5):
        upper, lower = ahead(order), behind(order)
        if upper is None and lower is None:
            continue
        if lower is None:
            term = upper
        elif upper is None:
            term = -lower
        else:
            term = upper - lower
        if order > 1:
            term = (COEF[order - 1] / COEF[0]) * term
        total = term if total is None else total + term
    return total


def band(first, depth):
    source = lax.broadcasted_iota(jnp.int32, (depth, depth), 0)
    target = lax.broadcasted_iota(jnp.int32, (depth, depth), 1)
    total = jnp.zeros((depth, depth), jnp.float32)
    for order in range(1, 5):
        weight = COEF[order - 1] / COEF[0]
        total = total + jnp.where(source == target + (first + order - 1), weight, 0.0)
        total = total - jnp.where(source == target + (first - order), weight, 0.0)
    return jnp.concatenate(halves(total), axis=1)


def halves(values):
    high = values.astype(jnp.bfloat16)
    return high, (values - high.astype(jnp.float32)).astype(jnp.bfloat16)


def along_z(values, matrix):
    xs, ys, zs = values.shape
    pair = jnp.concatenate(halves(values.reshape(xs * ys, zs)), axis=1)
    parts = jnp.dot(pair, matrix, preferred_element_type=jnp.float32)
    return (parts[:, :zs] + parts[:, zs:]).reshape(xs, ys, zs)


def blocks(xs, ys, body):
    if xs <= SPAN:
        for y0 in range(0, ys, ROWS):
            body(0, xs, y0)
        return

    def span(index, _):
        for y0 in range(0, ys, ROWS):
            body(index * SPAN, SPAN, y0)
        return 0

    lax.fori_loop(0, xs // SPAN, span, 0)


def window(xs, x0, load):
    kept = {}

    def at(offset):
        if xs <= SPAN and not 0 <= offset < xs:
            return None
        if offset not in kept:
            kept[offset] = load(x0 + offset)
        return kept[offset]

    return at


def slopes(xs, p, x0, y0, plane, offset):
    centre = plane(offset)
    here = x0 + offset + REACH
    return (
        combine(lambda k: plane(offset + k), lambda k: plane(offset + 1 - k)),
        combine(
            lambda k: p[here, pl.ds(EDGE + y0 + k, ROWS)],
            lambda k: centre if k == 1 else p[here, pl.ds(EDGE + y0 + 1 - k, ROWS)],
        ),
    )


def prepare_kernel(
    steps, fwd, adj, src, wave, rec, res, _piece,
    fwd_slope, adj_slope, fwd_source, adj_source, ahead, behind, *fields,
):
    xs, ys, zs = fwd_slope.shape[1:]
    for ref, first in ((ahead, 1), (behind, 0)):
        one = band(first, zs)
        ref[:zs] = one
        ref[zs:] = one

    def clear(ref):
        ref[...] = jnp.zeros(ref.shape, jnp.float32)

    for state, (p, v0, v1, v2), slope in (
        (fwd, fields[:4], fwd_slope),
        (adj, fields[4:], adj_slope),
    ):
        for ref in (p, v0):
            clear(ref.at[:REACH])
            clear(ref.at[REACH + xs :])
        for ref in (p.at[pl.ds(REACH, xs)], v1):
            clear(ref.at[:, :EDGE])
            clear(ref.at[:, EDGE + ys :])
        for x in range(xs):
            p[REACH + x, EDGE : EDGE + ys] = state[0, 0, x].astype(jnp.float32)
            v0[REACH + x] = state[0, 1, x].astype(jnp.float32)
            v1[x, EDGE : EDGE + ys] = state[0, 2, x].astype(jnp.float32)
            v2[x] = state[0, 3, x].astype(jnp.float32)

        def block(x0, count, y0, p=p, slope=slope):
            plane = window(xs, x0, lambda x: p[REACH + x, pl.ds(EDGE + y0, ROWS)])
            for offset in range(count):
                for d, values in enumerate(slopes(xs, p, x0, y0, plane, offset)):
                    slope[d, x0 + offset, pl.ds(y0, ROWS)] = values

        blocks(xs, ys, block)
        slope[2] = along_z(p[REACH : REACH + xs, EDGE : EDGE + ys], ahead[...])

    row = lax.broadcasted_iota(jnp.int32, (ys, zs), 0)
    lane = lax.broadcasted_iota(jnp.int32, (ys, zs), 1)
    src_mark = (row == src[0, 1]) & (lane == src[0, 2])
    for x in range(xs):
        rec_mark = (row == rec[0, 0, x]) & (lane == rec[0, 1, x])
        for step in range(steps):
            amplitude = jnp.where(x == src[0, 0], wave[0, step], 0.0)
            fwd_source[step, x] = jnp.where(src_mark, amplitude, 0.0)
            adj_source[step, x] = jnp.where(rec_mark, res[0, step, x], 0.0)


def near_kernel(speed, density, aperture, near_speed, near_density, entry):
    near_speed[...] = speed[...]
    near_density[...] = density[...]
    entry[...] = jnp.full(entry.shape, entry_of(aperture), jnp.int32)


def pick_kernel(chips, near_speed, near_density, far_speed, far_density, *refs):
    stripes = 2 * chips
    lists, outs = refs[:stripes], refs[stripes:]
    held = near_speed.shape[0]
    me = lax.axis_index("tile")
    residue, half = lax.rem(me, stripes), lax.div(me, stripes)
    for hop in range(stripes):
        entry = entry_of(lists[hop])
        corner, column = lax.div(entry, held), lax.rem(entry, held)
        here = (residue >= corner) == (half == 0)
        piece = outs[hop]

        @pl.when(here)
        def _():
            piece[0] = near_speed[column]
            piece[1] = near_density[column]

        @pl.when(jnp.logical_not(here))
        def _():
            piece[0] = far_speed[column]
            piece[1] = far_density[column]


def wave_kernel(chips, steps, held, *refs):
    stripes = 2 * chips
    pieces, refs = refs[:stripes], refs[stripes:]
    fwd_slope, adj_slope, fwd_source, adj_source, ahead, behind, entry_ref = refs[:7]
    kept, traded, p, v0, v1, v2, q, w0, w1, w2 = refs[15:25]
    bulk, buoy, dp, dv, bulk_img, buoy_img, across_z, flat = refs[25:]
    tile_x, tile_y = pieces[0].shape[1:3]
    xs, ys, zs = bulk.shape
    residue = lax.rem(lax.axis_index("tile"), stripes)
    entry = entry_of(entry_ref)
    corner = lax.div(entry, held)

    def place_of(hop):
        return lax.rem((residue ^ hop) - corner + stripes, stripes) * tile_x

    for hop in range(stripes):
        cells = pl.ds(place_of(hop), tile_x)
        speed, density = pieces[hop][0], pieces[hop][1]
        bulk[cells] = COEF[0] * (density * speed * speed)
        buoy[cells] = COEF[0] / density

    def push(fields, first, note):
        p, v0, v1, v2 = fields
        if first is None:
            across_z[...] = along_z(p[REACH : REACH + xs, EDGE : EDGE + ys], ahead[...])

        def block(x0, count, y0):
            rows, inner = pl.ds(y0, ROWS), pl.ds(EDGE + y0, ROWS)
            plane = window(xs, x0, lambda x: p[REACH + x, inner])
            for offset in range(count):
                x = x0 + offset
                if first is None:
                    two = slopes(xs, p, x0, y0, plane, offset)
                else:
                    two = (first[0, x, rows], first[1, x, rows])
                places = ((v0, REACH + x, rows), (v1, x, inner))
                for d, (ref, at, span) in enumerate(places):
                    change = buoy[x, rows] * two[d]
                    moved = ref[at, span] + change
                    ref[at, span] = moved
                    note(d, x, rows, change, moved)

        def block_z(x0, count, y0):
            rows = pl.ds(y0, ROWS)
            for x in range(count):
                x = x0 + x
                slope = across_z[x, rows] if first is None else first[2, x, rows]
                change = buoy[x, rows] * slope
                moved = v2[x, rows] + change
                v2[x, rows] = moved
                note(2, x, rows, change, moved)

        blocks(xs, ys, block)
        blocks(xs, ys, block_z)

    def spread(fields, source, step, note):
        p, v0, v1, v2 = fields
        across_z[...] = along_z(v2[...], behind[...])

        def block(x0, count, y0):
            rows = pl.ds(y0, ROWS)
            plane = window(xs, x0, lambda x: v0[REACH + x, rows])
            for offset in range(count):
                x = x0 + offset
                along_x = combine(lambda k: plane(offset + k - 1), lambda k: plane(offset - k))
                along_y = combine(
                    lambda k: v1[x, pl.ds(EDGE + y0 + k - 1, ROWS)],
                    lambda k: v1[x, pl.ds(EDGE + y0 - k, ROWS)],
                )
                flat[x, rows] = along_x + along_y

        def block_z(x0, count, y0):
            rows, inner = pl.ds(y0, ROWS), pl.ds(EDGE + y0, ROWS)
            for x in range(count):
                x = x0 + x
                change = bulk[x, rows] * (flat[x, rows] + across_z[x, rows])
                change = change + source[step, x, rows]
                moved = p[REACH + x, inner] + change
                p[REACH + x, inner] = moved
                note(x, rows, change, moved)

        blocks(xs, ys, block)
        blocks(xs, ys, block_z)

    fields = (p, v0, v1, v2)
    for step in range(steps):

        def keep_dv(d, x, rows, change, moved, step=step):
            dv[step, d, x, rows] = change

        def keep_dp(x, rows, change, moved, step=step):
            dp[step, x, rows] = change

        push(fields, fwd_slope if step == 0 else None, keep_dv)
        spread(fields, fwd_source, step, keep_dp)

    fields = (q, w0, w1, w2)
    for step in reversed(range(steps)):
        last = step == steps - 1

        def add_buoy(d, x, rows, change, moved, step=step, last=last):
            image = dv[step, d, x, rows] * moved
            buoy_img[x, rows] = image if last and d == 0 else buoy_img[x, rows] + image

        def add_bulk(x, rows, change, moved, step=step, last=last):
            image = dp[step, x, rows] * moved
            bulk_img[x, rows] = image if last else bulk_img[x, rows] + image

        push(fields, adj_slope if last else None, add_buoy)
        spread(fields, adj_source, step, add_bulk)

    tile_rows = tile_x * tile_y
    for chip in range(chips):
        for ref, hop in ((kept, 2 * chip), (traded, 2 * chip + 1)):
            cells = pl.ds(place_of(hop), tile_x)
            ref[chip, :tile_rows] = bulk_img[cells].reshape(tile_rows, zs)
            ref[chip, tile_rows : 2 * tile_rows] = buoy_img[cells].reshape(tile_rows, zs)
            ref[chip, 2 * tile_rows :] = jnp.full((8, zs), entry).astype(jnp.float32)


def merge_kernel(chips, kept, came, *outs):
    tile_rows = (kept.shape[1] - 8) // 2
    half = lax.div(lax.axis_index("tile"), 2 * chips)
    for index, out in enumerate(outs):
        chip, other = index % chips, index // chips
        field = jnp.where(half == other, 0, 1)
        rows = pl.ds(pl.multiple_of(field * tile_rows, tile_rows), tile_rows)
        for shot, source in enumerate((kept, came)):
            out[shot * tile_rows : (shot + 1) * tile_rows] = source[chip, rows]
            first = 2 * tile_rows + 4 * shot
            out[first : first + 4] = source[chip, 2 * tile_rows : 2 * tile_rows + 4]


def add_kernel(stripes, groups, held, *refs):
    came, parts, total = refs[:stripes], refs[stripes:-1], refs[-1]
    me, group = lax.axis_index("tile"), lax.axis_index("grp")
    residue = lax.rem(me, stripes)
    tile_rows = total.shape[0] // (2 * held)
    part = parts[0].shape[1]
    total[...] = jnp.zeros_like(total)
    for pair in came:
        for shot in range(2):
            first = 2 * tile_rows + 4 * shot
            entry = jnp.max(pair[first : first + 4]).astype(jnp.int32)
            corner, column = lax.div(entry, held), lax.rem(entry, held)
            slot = jnp.where(residue < corner, held, 0) + column
            rows = pl.ds(pl.multiple_of(slot * tile_rows, tile_rows), tile_rows)
            total[rows] = total[rows] + pair[shot * tile_rows : (shot + 1) * tile_rows]
    for out, hop in zip(parts, [0] + far_first(groups)):
        for owner in range(2):
            first = owner * (held * tile_rows) + (group ^ hop) * part
            out[owner] = total[pl.ds(pl.multiple_of(first, part), part)]


def far_first(groups):
    return list(range(groups - 1, 0, -1))


def sum_kernel(stripes, *refs):
    parts, (mine, other) = refs[:-2], refs[-2:]
    sums = parts[0][...]
    for values in parts[1:]:
        sums = sums + values[...]
    first_half = lax.axis_index("tile") < stripes
    mine[...] = jnp.where(first_half, sums[0], sums[1])
    other[...] = jnp.where(first_half, sums[1], sums[0])


def grads_kernel(scale, stripes, mine, came, speed_ref, density_ref, grads):
    part = mine.shape[0]
    rows = pl.ds(pl.multiple_of(lax.axis_index("grp") * part, part), part)
    speed, density = speed_ref[rows], density_ref[rows]
    first_half = lax.axis_index("tile") < stripes
    bulk_sum = jnp.where(first_half, mine[...], came[...])
    buoy_sum = jnp.where(first_half, came[...], mine[...])
    grads[0] = scale * (bulk_sum * (2.0 * density * speed))
    grads[1] = scale * (bulk_sum * (speed * speed) - buoy_sum / (density * density))


def per_device(speed, density, fwd_state, adj_state, aperture, src_pos, wavelet, rec_pos, residual):
    owners = lax.axis_size("tile")
    groups = lax.axis_size("grp")
    my_group = lax.axis_index("grp")
    held, tile_x, tile_y, depth = speed.shape
    stripes = aperture.shape[1]
    chips = stripes // 2
    steps = wavelet.shape[1]
    xs = stripes * tile_x
    f32 = jnp.float32
    cells = (xs, tile_y, depth)

    def shape(*dims):
        return jax.ShapeDtypeStruct(dims, f32)

    def across(values, hop):
        return lax.ppermute(values, "tile", [(t, t ^ hop) for t in range(owners)])

    far_speed = across(speed, stripes)
    far_density = across(density, stripes)
    lists = {hop: across(aperture, hop) for hop in range(stripes - 1, 0, -1)}
    four = [
        (xs + 2 * REACH, tile_y + 2 * EDGE, depth),
        (xs + 2 * REACH, tile_y, depth),
        (xs, tile_y + 2 * EDGE, depth),
        cells,
    ]
    near_speed, near_density, entry = pl.pallas_call(
        near_kernel,
        out_shape=[
            shape(*speed.shape),
            shape(*speed.shape),
            jax.ShapeDtypeStruct((8, depth), jnp.int32),
        ],
        in_specs=[VMEM] * 3,
        out_specs=[VMEM] * 3,
        compiler_params=PARAMS,
        cost_estimate=pl.CostEstimate(flops=4_000_000, bytes_accessed=6_000_000, transcendentals=0),
        name="hold_near_tiles",
    )(speed, density, aperture)
    pieces = pl.pallas_call(
        functools.partial(pick_kernel, chips),
        out_shape=[shape(2, tile_x, tile_y, depth)] * stripes,
        in_specs=[VMEM] * (4 + stripes),
        out_specs=[VMEM] * stripes,
        compiler_params=PARAMS,
        name="pick_tiles",
    )(near_speed, near_density, far_speed, far_density, entry, *[lists[h] for h in range(1, stripes)])
    moved = {hop: across(pieces[hop], hop) for hop in range(stripes - 1, 0, -1)}

    prepared = pl.pallas_call(
        functools.partial(prepare_kernel, steps),
        out_shape=[shape(3, *cells)] * 2
        + [shape(steps, *cells)] * 2
        + [jax.ShapeDtypeStruct((2 * depth, 2 * depth), jnp.bfloat16)] * 2
        + [shape(*dims) for dims in four + four],
        in_specs=[VMEM] * 2 + [SMEM] * 4 + [VMEM],
        out_specs=[VMEM] * 14,
        compiler_params=PARAMS,
        cost_estimate=pl.CostEstimate(flops=4_000_000, bytes_accessed=6_000_000, transcendentals=0),
        name="prepare",
    )(fwd_state, adj_state, src_pos, wavelet, jnp.swapaxes(rec_pos, 1, 2), residual, pieces[0])
    prepared, fields = prepared[:6], prepared[6:]
    pieces = [pieces[0]] + [moved[hop] for hop in range(1, stripes)]

    tile_rows = tile_x * tile_y
    sent = shape(chips, 2 * tile_rows + 8, depth)
    kept, traded, *_ = pl.pallas_call(
        functools.partial(wave_kernel, chips, steps, held),
        out_shape=[sent, sent] + [shape(*dims) for dims in four + four],
        in_specs=[VMEM] * (stripes + 15),
        out_specs=[VMEM] * 10,
        scratch_shapes=[
            pltpu.VMEM(cells, f32),
            pltpu.VMEM(cells, f32),
            pltpu.VMEM((steps,) + cells, f32),
            pltpu.VMEM((steps, 3) + cells, f32),
            pltpu.VMEM(cells, f32),
            pltpu.VMEM(cells, f32),
            pltpu.VMEM(cells, f32),
            pltpu.VMEM(cells, f32),
        ],
        input_output_aliases={stripes + 7 + index: 2 + index for index in range(8)},
        compiler_params=PARAMS,
        name="replay_and_adjoint",
    )(*pieces, *prepared, entry, *fields)

    stacks = pl.pallas_call(
        functools.partial(merge_kernel, chips),
        out_shape=[shape(2 * tile_rows + 8, depth)] * stripes,
        in_specs=[VMEM] * 2,
        out_specs=[VMEM] * stripes,
        compiler_params=PARAMS,
        name="merge_pair",
    )(kept, across(traded, 1))
    order = [1] + list(range(stripes - 1, 1, -1))
    came = [stacks[0]] + [across(stacks[chip], 2 * chip) for chip in order]

    rows = held * tile_rows
    part = rows // groups
    parts = pl.pallas_call(
        functools.partial(add_kernel, stripes, groups, held),
        out_shape=[shape(2, part, depth)] * groups,
        in_specs=[VMEM] * stripes,
        out_specs=[VMEM] * groups,
        scratch_shapes=[pltpu.VMEM((2 * rows, depth), f32)],
        compiler_params=PARAMS,
        name="add_stripes",
    )(*came)

    def along(values, hop):
        return lax.ppermute(values, "grp", [(g, g ^ hop) for g in range(groups)])

    parts = [parts[0]] + [along(values, hop) for values, hop in zip(parts[1:], far_first(groups))]
    mine, other = pl.pallas_call(
        functools.partial(sum_kernel, stripes),
        out_shape=[shape(part, depth)] * 2,
        in_specs=[VMEM] * groups,
        out_specs=[VMEM] * 2,
        compiler_params=PARAMS,
        name="sum_groups",
    )(*parts)
    grads = pl.pallas_call(
        functools.partial(grads_kernel, 1.0 / math.sqrt(groups * owners), stripes),
        out_shape=shape(2, part, depth),
        in_specs=[VMEM] * 4,
        out_specs=VMEM,
        compiler_params=PARAMS,
        name="gradients",
    )(
        mine,
        across(other, stripes),
        near_speed.reshape(rows, depth),
        near_density.reshape(rows, depth),
    )

    whole = jnp.zeros((2, groups, part, depth), f32)
    for hop in [0] + far_first(groups):
        values = grads if hop == 0 else along(grads, hop)
        place = my_group ^ hop
        whole = lax.dynamic_update_slice_in_dim(whole, values[:, None], place, axis=1)
    return (whole[0].reshape(speed.shape), whole[1].reshape(speed.shape))


def solution(mesh):
    return jax.shard_map(
        per_device,
        mesh=mesh,
        in_specs=(
            P("tile", None, None, None),
            P("tile", None, None, None),
            P(("grp", "tile"), None, None, None, None),
            P(("grp", "tile"), None, None, None, None),
            P(("grp", "tile"), None),
            P(("grp", "tile"), None),
            P(("grp", "tile"), None),
            P(("grp", "tile"), None, None),
            P(("grp", "tile"), None, None),
        ),
        out_specs=(P("tile", None, None, None), P("tile", None, None, None)),
        check_vma=False,
    )
```

```python
import functools
import math

import jax
import jax.numpy as jnp
from jax import lax
from jax.experimental import pallas as pl
from jax.experimental.pallas import tpu as pltpu
from jax.sharding import PartitionSpec as P

COEF = (1225.0 / 1024.0, -245.0 / 3072.0, 49.0 / 5120.0, -5.0 / 7168.0)
REACH = 4
EDGE = 8
ROWS = 8
SPAN = 8

SMEM = pl.BlockSpec(memory_space=pltpu.SMEM)
VMEM = pl.BlockSpec(memory_space=pltpu.VMEM)
PARAMS = pltpu.CompilerParams(vmem_limit_bytes=36 * 1024 * 1024)


def entry_of(list_ref):
    return jnp.max(list_ref[0:1, 0:1].astype(jnp.float32)).astype(jnp.int32)


def combine(ahead, behind):
    total = None
    for order in range(1, 5):
        upper, lower = ahead(order), behind(order)
        if upper is None and lower is None:
            continue
        if lower is None:
            term = upper
        elif upper is None:
            term = -lower
        else:
            term = upper - lower
        if order > 1:
            term = (COEF[order - 1] / COEF[0]) * term
        total = term if total is None else total + term
    return total


def band(first, depth):
    source = lax.broadcasted_iota(jnp.int32, (depth, depth), 0)
    target = lax.broadcasted_iota(jnp.int32, (depth, depth), 1)
    total = jnp.zeros((depth, depth), jnp.float32)
    for order in range(1, 5):
        weight = COEF[order - 1] / COEF[0]
        total = total + jnp.where(source == target + (first + order - 1), weight, 0.0)
        total = total - jnp.where(source == target + (first - order), weight, 0.0)
    return jnp.concatenate(halves(total), axis=1)


def halves(values):
    high = values.astype(jnp.bfloat16)
    return high, (values - high.astype(jnp.float32)).astype(jnp.bfloat16)


def along_z(values, matrix):
    xs, ys, zs = values.shape
    pair = jnp.concatenate(halves(values.reshape(xs * ys, zs)), axis=1)
    parts = jnp.dot(pair, matrix, preferred_element_type=jnp.float32)
    return (parts[:, :zs] + parts[:, zs:]).reshape(xs, ys, zs)


def blocks(xs, ys, body):
    if xs <= SPAN:
        for y0 in range(0, ys, ROWS):
            body(0, xs, y0)
        return

    def span(index, _):
        for y0 in range(0, ys, ROWS):
            body(index * SPAN, SPAN, y0)
        return 0

    lax.fori_loop(0, xs // SPAN, span, 0)


def window(xs, x0, load):
    kept = {}

    def at(offset):
        if xs <= SPAN and not 0 <= offset < xs:
            return None
        if offset not in kept:
            kept[offset] = load(x0 + offset)
        return kept[offset]

    return at


def slopes(xs, p, x0, y0, plane, offset):
    centre = plane(offset)
    here = x0 + offset + REACH
    return (
        combine(lambda k: plane(offset + k), lambda k: plane(offset + 1 - k)),
        combine(
            lambda k: p[here, pl.ds(EDGE + y0 + k, ROWS)],
            lambda k: centre if k == 1 else p[here, pl.ds(EDGE + y0 + 1 - k, ROWS)],
        ),
    )


def prepare_kernel(
    steps, fwd, adj, src, wave, rec, res, _piece,
    fwd_slope, adj_slope, fwd_source, adj_source, ahead, behind, *fields,
):
    xs, ys, zs = fwd_slope.shape[1:]
    for ref, first in ((ahead, 1), (behind, 0)):
        one = band(first, zs)
        ref[:zs] = one
        ref[zs:] = one

    def clear(ref):
        ref[...] = jnp.zeros(ref.shape, jnp.float32)

    for state, (p, v0, v1, v2), slope in (
        (fwd, fields[:4], fwd_slope),
        (adj, fields[4:], adj_slope),
    ):
        for ref in (p, v0):
            clear(ref.at[:REACH])
            clear(ref.at[REACH + xs :])
        for ref in (p.at[pl.ds(REACH, xs)], v1):
            clear(ref.at[:, :EDGE])
            clear(ref.at[:, EDGE + ys :])
        for x in range(xs):
            p[REACH + x, EDGE : EDGE + ys] = state[0, 0, x].astype(jnp.float32)
            v0[REACH + x] = state[0, 1, x].astype(jnp.float32)
            v1[x, EDGE : EDGE + ys] = state[0, 2, x].astype(jnp.float32)
            v2[x] = state[0, 3, x].astype(jnp.float32)

        def block(x0, count, y0, p=p, slope=slope):
            plane = window(xs, x0, lambda x: p[REACH + x, pl.ds(EDGE + y0, ROWS)])
            for offset in range(count):
                for d, values in enumerate(slopes(xs, p, x0, y0, plane, offset)):
                    slope[d, x0 + offset, pl.ds(y0, ROWS)] = values

        blocks(xs, ys, block)
        slope[2] = along_z(p[REACH : REACH + xs, EDGE : EDGE + ys], ahead[...])

    row = lax.broadcasted_iota(jnp.int32, (ys, zs), 0)
    lane = lax.broadcasted_iota(jnp.int32, (ys, zs), 1)
    src_mark = (row == src[0, 1]) & (lane == src[0, 2])
    for x in range(xs):
        rec_mark = (row == rec[0, 0, x]) & (lane == rec[0, 1, x])
        for step in range(steps):
            amplitude = jnp.where(x == src[0, 0], wave[0, step], 0.0)
            fwd_source[step, x] = jnp.where(src_mark, amplitude, 0.0)
            adj_source[step, x] = jnp.where(rec_mark, res[0, step, x], 0.0)


def near_kernel(speed, density, aperture, near_speed, near_density, entry):
    near_speed[...] = speed[...]
    near_density[...] = density[...]
    entry[...] = jnp.full(entry.shape, entry_of(aperture), jnp.int32)


def pick_kernel(chips, near_speed, near_density, far_speed, far_density, *refs):
    stripes = 2 * chips
    lists, outs = refs[:stripes], refs[stripes:]
    held = near_speed.shape[0]
    me = lax.axis_index("tile")
    residue, half = lax.rem(me, stripes), lax.div(me, stripes)
    for hop in range(stripes):
        entry = entry_of(lists[hop])
        corner, column = lax.div(entry, held), lax.rem(entry, held)
        here = (residue >= corner) == (half == 0)
        piece = outs[hop]

        @pl.when(here)
        def _():
            piece[0] = near_speed[column]
            piece[1] = near_density[column]

        @pl.when(jnp.logical_not(here))
        def _():
            piece[0] = far_speed[column]
            piece[1] = far_density[column]


def wave_kernel(chips, steps, held, *refs):
    stripes = 2 * chips
    pieces, refs = refs[:stripes], refs[stripes:]
    fwd_slope, adj_slope, fwd_source, adj_source, ahead, behind, entry_ref = refs[:7]
    kept, traded, p, v0, v1, v2, q, w0, w1, w2 = refs[15:25]
    bulk, buoy, dp, dv, bulk_img, buoy_img = refs[25:31]
    here_z, here_flat, back_z, back_flat = refs[31:]
    tile_x, tile_y = pieces[0].shape[1:3]
    xs, ys, zs = bulk.shape
    residue = lax.rem(lax.axis_index("tile"), stripes)
    entry = entry_of(entry_ref)
    corner = lax.div(entry, held)

    def place_of(hop):
        return lax.rem((residue ^ hop) - corner + stripes, stripes) * tile_x

    for hop in range(stripes):
        cells = pl.ds(place_of(hop), tile_x)
        speed, density = pieces[hop][0], pieces[hop][1]
        bulk[cells] = COEF[0] * (density * speed * speed)
        buoy[cells] = COEF[0] / density

    def push(fields, across_z, first, note):
        p, v0, v1, v2 = fields

        def block(x0, count, y0):
            rows, inner = pl.ds(y0, ROWS), pl.ds(EDGE + y0, ROWS)
            plane = window(xs, x0, lambda x: p[REACH + x, inner])
            for offset in range(count):
                x = x0 + offset
                if first is None:
                    two = slopes(xs, p, x0, y0, plane, offset)
                else:
                    two = (first[0, x, rows], first[1, x, rows])
                places = ((v0, REACH + x, rows), (v1, x, inner))
                for d, (ref, at, span) in enumerate(places):
                    change = buoy[x, rows] * two[d]
                    moved = ref[at, span] + change
                    ref[at, span] = moved
                    note(d, x, rows, change, moved)

        def block_z(x0, count, y0):
            rows = pl.ds(y0, ROWS)
            for x in range(count):
                x = x0 + x
                slope = across_z[x, rows] if first is None else first[2, x, rows]
                change = buoy[x, rows] * slope
                moved = v2[x, rows] + change
                v2[x, rows] = moved
                note(2, x, rows, change, moved)

        def product():
            if first is None:
                across_z[...] = along_z(p[REACH : REACH + xs, EDGE : EDGE + ys], ahead[...])

        return product, lambda: blocks(xs, ys, block), lambda: blocks(xs, ys, block_z)

    def spread(fields, across_z, flat, source, step, note):
        p, v0, v1, v2 = fields

        def block(x0, count, y0):
            rows = pl.ds(y0, ROWS)
            plane = window(xs, x0, lambda x: v0[REACH + x, rows])
            for offset in range(count):
                x = x0 + offset
                along_x = combine(lambda k: plane(offset + k - 1), lambda k: plane(offset - k))
                along_y = combine(
                    lambda k: v1[x, pl.ds(EDGE + y0 + k - 1, ROWS)],
                    lambda k: v1[x, pl.ds(EDGE + y0 - k, ROWS)],
                )
                flat[x, rows] = along_x + along_y

        def block_z(x0, count, y0):
            rows, inner = pl.ds(y0, ROWS), pl.ds(EDGE + y0, ROWS)
            for x in range(count):
                x = x0 + x
                change = bulk[x, rows] * (flat[x, rows] + across_z[x, rows])
                change = change + source[step, x, rows]
                moved = p[REACH + x, inner] + change
                p[REACH + x, inner] = moved
                note(x, rows, change, moved)

        def product():
            across_z[...] = along_z(v2[...], behind[...])

        return product, lambda: blocks(xs, ys, block), lambda: blocks(xs, ys, block_z)

    bulk_img[...] = jnp.zeros_like(bulk_img)
    buoy_img[...] = jnp.zeros_like(buoy_img)

    def note_v(step, late, forward):
        def note(d, x, rows, change, moved):
            value = change if forward else moved
            if late:
                buoy_img[x, rows] = buoy_img[x, rows] + dv[step, d, x, rows] * value
            else:
                dv[step, d, x, rows] = value

        return note

    def note_p(step, late, forward):
        def note(x, rows, change, moved):
            value = change if forward else moved
            if late:
                bulk_img[x, rows] = bulk_img[x, rows] + dp[step, x, rows] * value
            else:
                dp[step, x, rows] = value

        return note

    here, back = (p, v0, v1, v2), (q, w0, w1, w2)
    for time in range(steps):
        mirror = steps - 1 - time
        forward, adjoint = (time, time > mirror, True), (mirror, mirror <= time, False)
        start = time == 0
        for pair in (
            (
                push(here, here_z, fwd_slope if start else None, note_v(*forward)),
                push(back, back_z, adj_slope if start else None, note_v(*adjoint)),
            ),
            (
                spread(here, here_z, here_flat, fwd_source, time, note_p(*forward)),
                spread(back, back_z, back_flat, adj_source, mirror, note_p(*adjoint)),
            ),
        ):
            for stage in zip(*pair):
                for run in stage:
                    run()

    tile_rows = tile_x * tile_y
    for chip in range(chips):
        for ref, hop in ((kept, 2 * chip), (traded, 2 * chip + 1)):
            cells = pl.ds(place_of(hop), tile_x)
            ref[chip, :tile_rows] = bulk_img[cells].reshape(tile_rows, zs)
            ref[chip, tile_rows : 2 * tile_rows] = buoy_img[cells].reshape(tile_rows, zs)
            ref[chip, 2 * tile_rows :] = jnp.full((8, zs), entry).astype(jnp.float32)


def merge_kernel(chips, kept, came, *outs):
    rows = kept.shape[1] - 8
    for index, out in enumerate(outs):
        for shot, source in enumerate((kept, came)):
            out[shot * rows : (shot + 1) * rows] = source[index % chips, :rows]
            first = 2 * rows + 4 * shot
            out[first : first + 4] = source[index % chips, rows : rows + 4]


def add_kernel(chips, groups, held, *refs):
    came, parts, total = refs[: 2 * chips], refs[2 * chips : 2 * chips + groups], refs[-1]
    stripes = 2 * chips
    me, group = lax.axis_index("tile"), lax.axis_index("grp")
    tile_rows = total.shape[1] // (held + 1)
    part = parts[0].shape[1]
    total[...] = jnp.zeros_like(total)
    for pair in came:
        for shot in range(2):
            first = 4 * tile_rows + 4 * shot
            entry = jnp.max(pair[first : first + 4]).astype(jnp.int32)
            corner, column = lax.div(entry, held), lax.rem(entry, held)
            mine = (corner <= me) & (me < corner + stripes)
            slot = jnp.where(mine, column, held)
            rows = pl.ds(pl.multiple_of(slot * tile_rows, tile_rows), tile_rows)
            for field in range(2):
                first = (2 * shot + field) * tile_rows
                total[field, rows] = total[field, rows] + pair[first : first + tile_rows]
    for index, hop in enumerate([0] + far_first(groups)):
        first = pl.multiple_of((group ^ hop) * part, part)
        for field in range(2):
            parts[index][field] = total[field, pl.ds(first, part)]


def far_first(groups):
    return list(range(groups - 1, 0, -1))


def grads_kernel(scale, groups, *refs):
    parts, speed_ref, density_ref, grads = refs[:groups], *refs[groups:]
    part = parts[0].shape[1]
    rows = pl.ds(pl.multiple_of(lax.axis_index("grp") * part, part), part)
    speed, density = speed_ref[rows], density_ref[rows]
    bulk_sum, buoy_sum = parts[0][0], parts[0][1]
    for other in parts[1:]:
        bulk_sum = bulk_sum + other[0]
        buoy_sum = buoy_sum + other[1]
    grads[0] = scale * (bulk_sum * (2.0 * density * speed))
    grads[1] = scale * (bulk_sum * (speed * speed) - buoy_sum / (density * density))


def per_device(speed, density, fwd_state, adj_state, aperture, src_pos, wavelet, rec_pos, residual):
    owners = lax.axis_size("tile")
    groups = lax.axis_size("grp")
    my_group = lax.axis_index("grp")
    held, tile_x, tile_y, depth = speed.shape
    stripes = aperture.shape[1]
    chips = stripes // 2
    steps = wavelet.shape[1]
    xs = stripes * tile_x
    f32 = jnp.float32
    cells = (xs, tile_y, depth)

    def shape(*dims):
        return jax.ShapeDtypeStruct(dims, f32)

    def across(values, hop):
        return lax.ppermute(values, "tile", [(t, t ^ hop) for t in range(owners)])

    far_speed = across(speed, stripes)
    far_density = across(density, stripes)
    lists = {hop: across(aperture, hop) for hop in range(stripes - 1, 0, -1)}
    four = [
        (xs + 2 * REACH, tile_y + 2 * EDGE, depth),
        (xs + 2 * REACH, tile_y, depth),
        (xs, tile_y + 2 * EDGE, depth),
        cells,
    ]
    near_speed, near_density, entry = pl.pallas_call(
        near_kernel,
        out_shape=[
            shape(*speed.shape),
            shape(*speed.shape),
            jax.ShapeDtypeStruct((8, depth), jnp.int32),
        ],
        in_specs=[VMEM] * 3,
        out_specs=[VMEM] * 3,
        compiler_params=PARAMS,
        cost_estimate=pl.CostEstimate(flops=4_000_000, bytes_accessed=6_000_000, transcendentals=0),
        name="hold_near_tiles",
    )(speed, density, aperture)
    pieces = pl.pallas_call(
        functools.partial(pick_kernel, chips),
        out_shape=[shape(2, tile_x, tile_y, depth)] * stripes,
        in_specs=[VMEM] * (4 + stripes),
        out_specs=[VMEM] * stripes,
        compiler_params=PARAMS,
        name="pick_tiles",
    )(near_speed, near_density, far_speed, far_density, entry, *[lists[h] for h in range(1, stripes)])
    moved = {hop: across(pieces[hop], hop) for hop in range(stripes - 1, 0, -1)}

    prepared = pl.pallas_call(
        functools.partial(prepare_kernel, steps),
        out_shape=[shape(3, *cells)] * 2
        + [shape(steps, *cells)] * 2
        + [jax.ShapeDtypeStruct((2 * depth, 2 * depth), jnp.bfloat16)] * 2
        + [shape(*dims) for dims in four + four],
        in_specs=[VMEM] * 2 + [SMEM] * 4 + [VMEM],
        out_specs=[VMEM] * 14,
        compiler_params=PARAMS,
        cost_estimate=pl.CostEstimate(flops=4_000_000, bytes_accessed=6_000_000, transcendentals=0),
        name="prepare",
    )(fwd_state, adj_state, src_pos, wavelet, jnp.swapaxes(rec_pos, 1, 2), residual, pieces[0])
    prepared, fields = prepared[:6], prepared[6:]
    pieces = [pieces[0]] + [moved[hop] for hop in range(1, stripes)]

    tile_rows = tile_x * tile_y
    sent = shape(chips, 2 * tile_rows + 8, depth)
    kept, traded, *_ = pl.pallas_call(
        functools.partial(wave_kernel, chips, steps, held),
        out_shape=[sent, sent] + [shape(*dims) for dims in four + four],
        in_specs=[VMEM] * (stripes + 15),
        out_specs=[VMEM] * 10,
        scratch_shapes=[
            pltpu.VMEM(cells, f32),
            pltpu.VMEM(cells, f32),
            pltpu.VMEM((steps,) + cells, f32),
            pltpu.VMEM((steps, 3) + cells, f32),
        ]
        + [pltpu.VMEM(cells, f32)] * 6
        + [
        ],
        input_output_aliases={stripes + 7 + index: 2 + index for index in range(8)},
        compiler_params=PARAMS,
        name="replay_and_adjoint",
    )(*pieces, *prepared, entry, *fields)

    both = shape(4 * tile_rows + 8, depth)
    stacks = pl.pallas_call(
        functools.partial(merge_kernel, chips),
        out_shape=[both] * chips,
        in_specs=[VMEM] * 2,
        out_specs=[VMEM] * chips,
        compiler_params=PARAMS,
        name="merge_pair",
    )(kept, across(traded, 1))
    came = [
        across(stacks[chip], 2 * chip + stripes * half)
        for half in range(2)
        for chip in range(chips)
        if chip or half
    ]

    rows = held * tile_rows
    part = rows // groups
    part_shape = shape(2, part, depth)
    parts = pl.pallas_call(
        functools.partial(add_kernel, chips, groups, held),
        out_shape=[part_shape] * groups,
        in_specs=[VMEM] * stripes,
        out_specs=[VMEM] * groups,
        scratch_shapes=[pltpu.VMEM((2, rows + tile_rows, depth), f32)],
        compiler_params=PARAMS,
        name="add_stripes",
    )(stacks[0], *came)

    def along(values, hop):
        return lax.ppermute(values, "grp", [(g, g ^ hop) for g in range(groups)])

    parts = [parts[0]] + [along(values, hop) for values, hop in zip(parts[1:], far_first(groups))]
    grads = pl.pallas_call(
        functools.partial(grads_kernel, 1.0 / math.sqrt(groups * owners), groups),
        out_shape=part_shape,
        in_specs=[VMEM] * (groups + 2),
        out_specs=VMEM,
        compiler_params=PARAMS,
        name="gradients",
    )(*parts, near_speed.reshape(rows, depth), near_density.reshape(rows, depth))

    whole = jnp.zeros((2, groups, part, depth), f32)
    for hop in range(groups):
        values = grads
        if hop:
            values = lax.ppermute(grads, "grp", [(g, (g + hop) % groups) for g in range(groups)])
        place = lax.rem(my_group - hop + groups, groups)
        whole = lax.dynamic_update_slice_in_dim(whole, values[:, None], place, axis=1)
    return (whole[0].reshape(speed.shape), whole[1].reshape(speed.shape))


def solution(mesh):
    return jax.shard_map(
        per_device,
        mesh=mesh,
        in_specs=(
            P("tile", None, None, None),
            P("tile", None, None, None),
            P(("grp", "tile"), None, None, None, None),
            P(("grp", "tile"), None, None, None, None),
            P(("grp", "tile"), None),
            P(("grp", "tile"), None),
            P(("grp", "tile"), None),
            P(("grp", "tile"), None, None),
            P(("grp", "tile"), None, None),
        ),
        out_specs=(P("tile", None, None, None), P("tile", None, None, None)),
        check_vma=False,
    )
```

```python
import functools
import math

import jax
import jax.numpy as jnp
from jax import lax
from jax.experimental import pallas as pl
from jax.experimental.pallas import tpu as pltpu
from jax.sharding import PartitionSpec as P

COEF = (1225.0 / 1024.0, -245.0 / 3072.0, 49.0 / 5120.0, -5.0 / 7168.0)
REACH = 4
EDGE = 8
ROWS = 8
SPAN = 8

SMEM = pl.BlockSpec(memory_space=pltpu.SMEM)
VMEM = pl.BlockSpec(memory_space=pltpu.VMEM)
PARAMS = pltpu.CompilerParams(vmem_limit_bytes=36 * 1024 * 1024)


def entry_of(list_ref):
    return jnp.max(list_ref[0:1, 0:1].astype(jnp.float32)).astype(jnp.int32)


def combine(ahead, behind):
    total = None
    for order in range(1, 5):
        upper, lower = ahead(order), behind(order)
        if upper is None and lower is None:
            continue
        if lower is None:
            term = upper
        elif upper is None:
            term = -lower
        else:
            term = upper - lower
        if order > 1:
            term = (COEF[order - 1] / COEF[0]) * term
        total = term if total is None else total + term
    return total


def band(first, depth):
    source = lax.broadcasted_iota(jnp.int32, (depth, depth), 0)
    target = lax.broadcasted_iota(jnp.int32, (depth, depth), 1)
    total = jnp.zeros((depth, depth), jnp.float32)
    for order in range(1, 5):
        weight = COEF[order - 1] / COEF[0]
        total = total + jnp.where(source == target + (first + order - 1), weight, 0.0)
        total = total - jnp.where(source == target + (first - order), weight, 0.0)
    return jnp.concatenate(halves(total), axis=1)


def halves(values):
    high = values.astype(jnp.bfloat16)
    return high, (values - high.astype(jnp.float32)).astype(jnp.bfloat16)


def along_z(values, matrix):
    xs, ys, zs = values.shape
    pair = jnp.concatenate(halves(values.reshape(xs * ys, zs)), axis=1)
    parts = jnp.dot(pair, matrix, preferred_element_type=jnp.float32)
    return (parts[:, :zs] + parts[:, zs:]).reshape(xs, ys, zs)


def blocks(xs, ys, body):
    if xs <= SPAN:
        for y0 in range(0, ys, ROWS):
            body(0, xs, y0)
        return

    def span(index, _):
        for y0 in range(0, ys, ROWS):
            body(index * SPAN, SPAN, y0)
        return 0

    lax.fori_loop(0, xs // SPAN, span, 0)


def window(xs, x0, load):
    kept = {}

    def at(offset):
        if xs <= SPAN and not 0 <= offset < xs:
            return None
        if offset not in kept:
            kept[offset] = load(x0 + offset)
        return kept[offset]

    return at


def slopes(xs, p, x0, y0, plane, offset):
    centre = plane(offset)
    here = x0 + offset + REACH
    return (
        combine(lambda k: plane(offset + k), lambda k: plane(offset + 1 - k)),
        combine(
            lambda k: p[here, pl.ds(EDGE + y0 + k, ROWS)],
            lambda k: centre if k == 1 else p[here, pl.ds(EDGE + y0 + 1 - k, ROWS)],
        ),
    )


def prepare_kernel(
    steps, fwd, adj, src, wave, rec, res, _piece,
    fwd_slope, adj_slope, fwd_source, adj_source, ahead, behind, *fields,
):
    xs, ys, zs = fwd_slope.shape[1:]
    for ref, first in ((ahead, 1), (behind, 0)):
        one = band(first, zs)
        ref[:zs] = one
        ref[zs:] = one

    def clear(ref):
        ref[...] = jnp.zeros(ref.shape, jnp.float32)

    for state, (p, v0, v1, v2), slope in (
        (fwd, fields[:4], fwd_slope),
        (adj, fields[4:], adj_slope),
    ):
        for ref in (p, v0):
            clear(ref.at[:REACH])
            clear(ref.at[REACH + xs :])
        for ref in (p.at[pl.ds(REACH, xs)], v1):
            clear(ref.at[:, :EDGE])
            clear(ref.at[:, EDGE + ys :])
        for x in range(xs):
            p[REACH + x, EDGE : EDGE + ys] = state[0, 0, x].astype(jnp.float32)
            v0[REACH + x] = state[0, 1, x].astype(jnp.float32)
            v1[x, EDGE : EDGE + ys] = state[0, 2, x].astype(jnp.float32)
            v2[x] = state[0, 3, x].astype(jnp.float32)

        def block(x0, count, y0, p=p, slope=slope):
            plane = window(xs, x0, lambda x: p[REACH + x, pl.ds(EDGE + y0, ROWS)])
            for offset in range(count):
                for d, values in enumerate(slopes(xs, p, x0, y0, plane, offset)):
                    slope[d, x0 + offset, pl.ds(y0, ROWS)] = values

        blocks(xs, ys, block)
        slope[2] = along_z(p[REACH : REACH + xs, EDGE : EDGE + ys], ahead[...])

    row = lax.broadcasted_iota(jnp.int32, (ys, zs), 0)
    lane = lax.broadcasted_iota(jnp.int32, (ys, zs), 1)
    src_mark = (row == src[0, 1]) & (lane == src[0, 2])
    for x in range(xs):
        rec_mark = (row == rec[0, 0, x]) & (lane == rec[0, 1, x])
        for step in range(steps):
            amplitude = jnp.where(x == src[0, 0], wave[0, step], 0.0)
            fwd_source[step, x] = jnp.where(src_mark, amplitude, 0.0)
            adj_source[step, x] = jnp.where(rec_mark, res[0, step, x], 0.0)


def near_kernel(speed, density, aperture, near_speed, near_density, entry):
    near_speed[...] = speed[...]
    near_density[...] = density[...]
    entry[...] = jnp.full(entry.shape, entry_of(aperture), jnp.int32)


def pick_kernel(chips, near_speed, near_density, far_speed, far_density, *refs):
    stripes = 2 * chips
    lists, outs = refs[:stripes], refs[stripes:]
    held = near_speed.shape[0]
    me = lax.axis_index("tile")
    residue, half = lax.rem(me, stripes), lax.div(me, stripes)
    for hop in range(stripes):
        entry = entry_of(lists[hop])
        corner, column = lax.div(entry, held), lax.rem(entry, held)
        here = (residue >= corner) == (half == 0)
        piece = outs[hop]

        @pl.when(here)
        def _():
            piece[0] = near_speed[column]
            piece[1] = near_density[column]

        @pl.when(jnp.logical_not(here))
        def _():
            piece[0] = far_speed[column]
            piece[1] = far_density[column]


def wave_kernel(chips, steps, held, *refs):
    stripes = 2 * chips
    pieces, refs = refs[:stripes], refs[stripes:]
    fwd_slope, adj_slope, fwd_source, adj_source, ahead, behind, entry_ref = refs[:7]
    kept, traded, p, v0, v1, v2, q, w0, w1, w2 = refs[15:25]
    bulk, buoy, dp, dv, bulk_img, buoy_img, across_z, flat = refs[25:]
    tile_x, tile_y = pieces[0].shape[1:3]
    xs, ys, zs = bulk.shape
    residue = lax.rem(lax.axis_index("tile"), stripes)
    entry = entry_of(entry_ref)
    corner = lax.div(entry, held)

    def place_of(hop):
        return lax.rem((residue ^ hop) - corner + stripes, stripes) * tile_x

    for hop in range(stripes):
        cells = pl.ds(place_of(hop), tile_x)
        speed, density = pieces[hop][0], pieces[hop][1]
        bulk[cells] = COEF[0] * (density * speed * speed)
        buoy[cells] = COEF[0] / density

    def push(fields, first, note):
        p, v0, v1, v2 = fields
        if first is None:
            across_z[...] = along_z(p[REACH : REACH + xs, EDGE : EDGE + ys], ahead[...])

        def block(x0, count, y0):
            rows, inner = pl.ds(y0, ROWS), pl.ds(EDGE + y0, ROWS)
            plane = window(xs, x0, lambda x: p[REACH + x, inner])
            for offset in range(count):
                x = x0 + offset
                if first is None:
                    two = slopes(xs, p, x0, y0, plane, offset)
                else:
                    two = (first[0, x, rows], first[1, x, rows])
                light = buoy[x, rows]
                changes = (light * two[0], light * two[1])
                moved = (v0[REACH + x, rows] + changes[0], v1[x, inner] + changes[1])
                v0[REACH + x, rows] = moved[0]
                v1[x, inner] = moved[1]
                note(0, x, rows, changes, moved)

        def block_z(x0, count, y0):
            rows = pl.ds(y0, ROWS)
            for x in range(count):
                x = x0 + x
                slope = across_z[x, rows] if first is None else first[2, x, rows]
                change = buoy[x, rows] * slope
                moved = v2[x, rows] + change
                v2[x, rows] = moved
                note(2, x, rows, (change,), (moved,))

        blocks(xs, ys, block)
        blocks(xs, ys, block_z)

    def spread(fields, source, step, note):
        p, v0, v1, v2 = fields
        across_z[...] = along_z(v2[...], behind[...])

        def block(x0, count, y0):
            rows = pl.ds(y0, ROWS)
            plane = window(xs, x0, lambda x: v0[REACH + x, rows])
            for offset in range(count):
                x = x0 + offset
                along_x = combine(lambda k: plane(offset + k - 1), lambda k: plane(offset - k))
                along_y = combine(
                    lambda k: v1[x, pl.ds(EDGE + y0 + k - 1, ROWS)],
                    lambda k: v1[x, pl.ds(EDGE + y0 - k, ROWS)],
                )
                flat[x, rows] = along_x + along_y

        def block_z(x0, count, y0):
            rows, inner = pl.ds(y0, ROWS), pl.ds(EDGE + y0, ROWS)
            for x in range(count):
                x = x0 + x
                change = bulk[x, rows] * (flat[x, rows] + across_z[x, rows])
                change = change + source[step, x, rows]
                moved = p[REACH + x, inner] + change
                p[REACH + x, inner] = moved
                note(x, rows, change, moved)

        blocks(xs, ys, block)
        blocks(xs, ys, block_z)

    fields = (p, v0, v1, v2)
    for step in range(steps):

        def keep_dv(first, x, rows, changes, moved, step=step):
            for d, change in enumerate(changes, first):
                dv[step, d, x, rows] = change

        def keep_dp(x, rows, change, moved, step=step):
            dp[step, x, rows] = change

        push(fields, fwd_slope if step == 0 else None, keep_dv)
        spread(fields, fwd_source, step, keep_dp)

    fields = (q, w0, w1, w2)
    for step in reversed(range(steps)):
        last = step == steps - 1

        def add_buoy(first, x, rows, changes, moved, step=step, last=last):
            image = None if last and first == 0 else buoy_img[x, rows]
            for d, values in enumerate(moved, first):
                product = dv[step, d, x, rows] * values
                image = product if image is None else image + product
            buoy_img[x, rows] = image

        def add_bulk(x, rows, change, moved, step=step, last=last):
            image = dp[step, x, rows] * moved
            bulk_img[x, rows] = image if last else bulk_img[x, rows] + image

        push(fields, adj_slope if last else None, add_buoy)
        spread(fields, adj_source, step, add_bulk)

    tile_rows = tile_x * tile_y
    for chip in range(chips):
        for ref, hop in ((kept, 2 * chip), (traded, 2 * chip + 1)):
            cells = pl.ds(place_of(hop), tile_x)
            ref[chip, :tile_rows] = bulk_img[cells].reshape(tile_rows, zs)
            ref[chip, tile_rows : 2 * tile_rows] = buoy_img[cells].reshape(tile_rows, zs)
            ref[chip, 2 * tile_rows :] = jnp.full((8, zs), entry).astype(jnp.float32)


def merge_kernel(chips, kept, came, *outs):
    rows = kept.shape[1] - 8
    for index, out in enumerate(outs):
        for shot, source in enumerate((kept, came)):
            out[shot * rows : (shot + 1) * rows] = source[index % chips, :rows]
            first = 2 * rows + 4 * shot
            out[first : first + 4] = source[index % chips, rows : rows + 4]


def add_kernel(chips, groups, held, *refs):
    came, parts, total = refs[: 2 * chips], refs[2 * chips : 2 * chips + groups], refs[-1]
    stripes = 2 * chips
    me, group = lax.axis_index("tile"), lax.axis_index("grp")
    tile_rows = total.shape[1] // (held + 1)
    part = parts[0].shape[1]
    total[...] = jnp.zeros_like(total)
    for pair in came:
        for shot in range(2):
            first = 4 * tile_rows + 4 * shot
            entry = jnp.max(pair[first : first + 4]).astype(jnp.int32)
            corner, column = lax.div(entry, held), lax.rem(entry, held)
            mine = (corner <= me) & (me < corner + stripes)
            slot = jnp.where(mine, column, held)
            rows = pl.ds(pl.multiple_of(slot * tile_rows, tile_rows), tile_rows)
            for field in range(2):
                first = (2 * shot + field) * tile_rows
                total[field, rows] = total[field, rows] + pair[first : first + tile_rows]
    for index, hop in enumerate([0] + far_first(groups)):
        first = pl.multiple_of((group ^ hop) * part, part)
        for field in range(2):
            parts[index][field] = total[field, pl.ds(first, part)]


def far_first(groups):
    return list(range(groups - 1, 0, -1))


def grads_kernel(scale, groups, *refs):
    parts, speed_ref, density_ref, grads = refs[:groups], *refs[groups:]
    part = parts[0].shape[1]
    rows = pl.ds(pl.multiple_of(lax.axis_index("grp") * part, part), part)
    speed, density = speed_ref[rows], density_ref[rows]
    bulk_sum, buoy_sum = parts[0][0], parts[0][1]
    for other in parts[1:]:
        bulk_sum = bulk_sum + other[0]
        buoy_sum = buoy_sum + other[1]
    grads[0] = scale * (bulk_sum * (2.0 * density * speed))
    grads[1] = scale * (bulk_sum * (speed * speed) - buoy_sum / (density * density))


def per_device(speed, density, fwd_state, adj_state, aperture, src_pos, wavelet, rec_pos, residual):
    owners = lax.axis_size("tile")
    groups = lax.axis_size("grp")
    my_group = lax.axis_index("grp")
    held, tile_x, tile_y, depth = speed.shape
    stripes = aperture.shape[1]
    chips = stripes // 2
    steps = wavelet.shape[1]
    xs = stripes * tile_x
    f32 = jnp.float32
    cells = (xs, tile_y, depth)

    def shape(*dims):
        return jax.ShapeDtypeStruct(dims, f32)

    def across(values, hop):
        return lax.ppermute(values, "tile", [(t, t ^ hop) for t in range(owners)])

    far_speed = across(speed, stripes)
    far_density = across(density, stripes)
    lists = {hop: across(aperture, hop) for hop in range(stripes - 1, 0, -1)}
    four = [
        (xs + 2 * REACH, tile_y + 2 * EDGE, depth),
        (xs + 2 * REACH, tile_y, depth),
        (xs, tile_y + 2 * EDGE, depth),
        cells,
    ]
    near_speed, near_density, entry = pl.pallas_call(
        near_kernel,
        out_shape=[
            shape(*speed.shape),
            shape(*speed.shape),
            jax.ShapeDtypeStruct((8, depth), jnp.int32),
        ],
        in_specs=[VMEM] * 3,
        out_specs=[VMEM] * 3,
        compiler_params=PARAMS,
        cost_estimate=pl.CostEstimate(flops=4_000_000, bytes_accessed=6_000_000, transcendentals=0),
        name="hold_near_tiles",
    )(speed, density, aperture)
    pieces = pl.pallas_call(
        functools.partial(pick_kernel, chips),
        out_shape=[shape(2, tile_x, tile_y, depth)] * stripes,
        in_specs=[VMEM] * (4 + stripes),
        out_specs=[VMEM] * stripes,
        compiler_params=PARAMS,
        name="pick_tiles",
    )(near_speed, near_density, far_speed, far_density, entry, *[lists[h] for h in range(1, stripes)])
    moved = {hop: across(pieces[hop], hop) for hop in range(stripes - 1, 0, -1)}

    prepared = pl.pallas_call(
        functools.partial(prepare_kernel, steps),
        out_shape=[shape(3, *cells)] * 2
        + [shape(steps, *cells)] * 2
        + [jax.ShapeDtypeStruct((2 * depth, 2 * depth), jnp.bfloat16)] * 2
        + [shape(*dims) for dims in four + four],
        in_specs=[VMEM] * 2 + [SMEM] * 4 + [VMEM],
        out_specs=[VMEM] * 14,
        compiler_params=PARAMS,
        cost_estimate=pl.CostEstimate(flops=4_000_000, bytes_accessed=6_000_000, transcendentals=0),
        name="prepare",
    )(fwd_state, adj_state, src_pos, wavelet, jnp.swapaxes(rec_pos, 1, 2), residual, pieces[0])
    prepared, fields = prepared[:6], prepared[6:]
    pieces = [pieces[0]] + [moved[hop] for hop in range(1, stripes)]

    tile_rows = tile_x * tile_y
    sent = shape(chips, 2 * tile_rows + 8, depth)
    kept, traded, *_ = pl.pallas_call(
        functools.partial(wave_kernel, chips, steps, held),
        out_shape=[sent, sent] + [shape(*dims) for dims in four + four],
        in_specs=[VMEM] * (stripes + 15),
        out_specs=[VMEM] * 10,
        scratch_shapes=[
            pltpu.VMEM(cells, f32),
            pltpu.VMEM(cells, f32),
            pltpu.VMEM((steps,) + cells, f32),
            pltpu.VMEM((steps, 3) + cells, f32),
        ]
        + [pltpu.VMEM(cells, f32)] * 4
        + [
        ],
        input_output_aliases={stripes + 7 + index: 2 + index for index in range(8)},
        compiler_params=PARAMS,
        name="replay_and_adjoint",
    )(*pieces, *prepared, entry, *fields)

    both = shape(4 * tile_rows + 8, depth)
    stacks = pl.pallas_call(
        functools.partial(merge_kernel, chips),
        out_shape=[both] * chips,
        in_specs=[VMEM] * 2,
        out_specs=[VMEM] * chips,
        compiler_params=PARAMS,
        name="merge_pair",
    )(kept, across(traded, 1))
    came = [
        across(stacks[chip], 2 * chip + stripes * half)
        for half in range(2)
        for chip in range(chips)
        if chip or half
    ]

    rows = held * tile_rows
    part = rows // groups
    part_shape = shape(2, part, depth)
    parts = pl.pallas_call(
        functools.partial(add_kernel, chips, groups, held),
        out_shape=[part_shape] * groups,
        in_specs=[VMEM] * stripes,
        out_specs=[VMEM] * groups,
        scratch_shapes=[pltpu.VMEM((2, rows + tile_rows, depth), f32)],
        compiler_params=PARAMS,
        name="add_stripes",
    )(stacks[0], *came)

    def along(values, hop):
        return lax.ppermute(values, "grp", [(g, g ^ hop) for g in range(groups)])

    parts = [parts[0]] + [along(values, hop) for values, hop in zip(parts[1:], far_first(groups))]
    grads = pl.pallas_call(
        functools.partial(grads_kernel, 1.0 / math.sqrt(groups * owners), groups),
        out_shape=part_shape,
        in_specs=[VMEM] * (groups + 2),
        out_specs=VMEM,
        compiler_params=PARAMS,
        name="gradients",
    )(*parts, near_speed.reshape(rows, depth), near_density.reshape(rows, depth))

    whole = jnp.zeros((2, groups, part, depth), f32)
    for hop in range(groups):
        values = grads
        if hop:
            values = lax.ppermute(grads, "grp", [(g, (g + hop) % groups) for g in range(groups)])
        place = lax.rem(my_group - hop + groups, groups)
        whole = lax.dynamic_update_slice_in_dim(whole, values[:, None], place, axis=1)
    return (whole[0].reshape(speed.shape), whole[1].reshape(speed.shape))


def solution(mesh):
    return jax.shard_map(
        per_device,
        mesh=mesh,
        in_specs=(
            P("tile", None, None, None),
            P("tile", None, None, None),
            P(("grp", "tile"), None, None, None, None),
            P(("grp", "tile"), None, None, None, None),
            P(("grp", "tile"), None),
            P(("grp", "tile"), None),
            P(("grp", "tile"), None),
            P(("grp", "tile"), None, None),
            P(("grp", "tile"), None, None),
        ),
        out_specs=(P("tile", None, None, None), P("tile", None, None, None)),
        check_vma=False,
    )
```

```python
import functools
import math

import jax
import jax.numpy as jnp
from jax import lax
from jax.experimental import pallas as pl
from jax.experimental.pallas import tpu as pltpu
from jax.sharding import PartitionSpec as P

COEF = (1225.0 / 1024.0, -245.0 / 3072.0, 49.0 / 5120.0, -5.0 / 7168.0)
REACH = 4
SHARE = 15.0 / 16.0
ROWS = 8
SPAN = 8

SMEM = pl.BlockSpec(memory_space=pltpu.SMEM)
VMEM = pl.BlockSpec(memory_space=pltpu.VMEM)
PARAMS = pltpu.CompilerParams(vmem_limit_bytes=36 * 1024 * 1024)


def entry_of(list_ref):
    return jnp.max(list_ref[0:1, 0:1].astype(jnp.float32)).astype(jnp.int32)


def combine(ahead, behind):
    total = None
    for order in range(1, 5):
        upper, lower = ahead(order), behind(order)
        if upper is None and lower is None:
            continue
        if lower is None:
            term = upper
        elif upper is None:
            term = -lower
        else:
            term = upper - lower
        if order > 1:
            term = (COEF[order - 1] / COEF[0]) * term
        total = term if total is None else total + term
    return total


def band(size, length, first, sources_down):
    down = lax.broadcasted_iota(jnp.int32, (size, size), 0)
    across = lax.broadcasted_iota(jnp.int32, (size, size), 1)
    shift = down - across if sources_down else across - down
    shift = jnp.where((down & -length) == (across & -length), shift, size)
    total = jnp.zeros((size, size), jnp.float32)
    for order in range(1, 5):
        weight = SHARE * COEF[order - 1] / COEF[0]
        total = jnp.where(shift == first + order - 1, weight, total)
        total = jnp.where(shift == first - order, -weight, total)
    return total.astype(jnp.bfloat16)


def halves(values):
    xs, ys, zs = values.shape
    values = values.reshape(xs * ys, zs)
    high = values.astype(jnp.bfloat16)
    low = (values - high.astype(jnp.float32)).astype(jnp.bfloat16)
    return jnp.concatenate([high, low], axis=1)


def along_z(pair, matrix):
    return jnp.dot(pair, matrix, preferred_element_type=jnp.float32)


def along_y(pair, matrix):
    size, zs = matrix.shape[0], pair.shape[1] // 2
    parts = []
    for first in range(0, pair.shape[0], size):
        both = jnp.dot(matrix, pair[first : first + size], preferred_element_type=jnp.float32)
        parts.append(both[:, :zs] + both[:, zs:])
    return parts[0] if len(parts) == 1 else jnp.concatenate(parts, axis=0)


def blocks(xs, ys, body):
    if xs <= SPAN:
        for y0 in range(0, ys, ROWS):
            body(0, xs, y0)
        return

    def span(index, _):
        for y0 in range(0, ys, ROWS):
            body(index * SPAN, SPAN, y0)
        return 0

    lax.fori_loop(0, xs // SPAN, span, 0)


def window(xs, x0, load):
    kept = {}

    def at(offset):
        if xs <= SPAN and not 0 <= offset < xs:
            return None
        if offset not in kept:
            kept[offset] = load(x0 + offset)
        return kept[offset]

    return at


def slope_x(plane, offset):
    return combine(lambda k: plane(offset + k), lambda k: plane(offset + 1 - k))


def prepare_kernel(
    steps, fwd, adj, src, wave, rec, res, _piece,
    fwd_slope, adj_slope, fwd_source, adj_source, ahead_z, behind_z, ahead_y, behind_y, *fields,
):
    xs, ys, zs = fwd_slope.shape[1:]
    for z_ref, y_ref, first in ((ahead_z, ahead_y, 1), (behind_z, behind_y, 0)):
        z_ref[:zs] = band(zs, zs, first, True)
        z_ref[zs:] = z_ref[:zs]
        y_ref[...] = band(y_ref.shape[0], ys, first, False)

    for state, (p, v0, v1, v2), slope in (
        (fwd, fields[:4], fwd_slope),
        (adj, fields[4:], adj_slope),
    ):
        for ref in (p, v0):
            ref[:REACH] = jnp.zeros((REACH, ys, zs), jnp.float32)
            ref[REACH + xs :] = jnp.zeros((REACH, ys, zs), jnp.float32)
        for x in range(xs):
            p[REACH + x] = state[0, 0, x].astype(jnp.float32)
            v0[REACH + x] = state[0, 1, x].astype(jnp.float32)
            v1[x] = state[0, 2, x].astype(jnp.float32)
            v2[x] = state[0, 3, x].astype(jnp.float32)

        def block(x0, count, y0, p=p, slope=slope):
            plane = window(xs, x0, lambda x: p[REACH + x, pl.ds(y0, ROWS)])
            for offset in range(count):
                slope[0, x0 + offset, pl.ds(y0, ROWS)] = slope_x(plane, offset)

        blocks(xs, ys, block)
        pair = halves(p[REACH : REACH + xs])
        slope[1] = along_y(pair, ahead_y[...]).reshape(xs, ys, zs)
        slope[2] = along_z(pair, ahead_z[...]).reshape(xs, ys, zs)

    row = lax.broadcasted_iota(jnp.int32, (ys, zs), 0)
    lane = lax.broadcasted_iota(jnp.int32, (ys, zs), 1)
    src_mark = (row == src[0, 1]) & (lane == src[0, 2])
    for x in range(xs):
        rec_mark = (row == rec[0, 0, x]) & (lane == rec[0, 1, x])
        for step in range(steps):
            amplitude = jnp.where(x == src[0, 0], wave[0, step], 0.0)
            fwd_source[step, x] = jnp.where(src_mark, amplitude, 0.0)
            adj_source[step, x] = jnp.where(rec_mark, res[0, step, x], 0.0)


def near_kernel(speed, density, aperture, near_speed, near_density, entry):
    near_speed[...] = speed[...]
    near_density[...] = density[...]
    entry[...] = jnp.full(entry.shape, entry_of(aperture), jnp.int32)


def pick_kernel(chips, near_speed, near_density, far_speed, far_density, *refs):
    stripes = 2 * chips
    lists, outs = refs[:stripes], refs[stripes:]
    held = near_speed.shape[0]
    me = lax.axis_index("tile")
    residue, half = lax.rem(me, stripes), lax.div(me, stripes)
    for hop in range(stripes):
        entry = entry_of(lists[hop])
        corner, column = lax.div(entry, held), lax.rem(entry, held)
        here = (residue >= corner) == (half == 0)
        piece = outs[hop]

        @pl.when(here)
        def _():
            piece[0] = near_speed[column]
            piece[1] = near_density[column]

        @pl.when(jnp.logical_not(here))
        def _():
            piece[0] = far_speed[column]
            piece[1] = far_density[column]


def wave_kernel(chips, steps, held, *refs):
    stripes = 2 * chips
    pieces, refs = refs[:stripes], refs[stripes:]
    fwd_slope, adj_slope, fwd_source, adj_source, ahead_z, behind_z, ahead_y, behind_y = refs[:8]
    entry_ref = refs[8]
    kept, traded, p, v0, v1, v2, q, w0, w1, w2 = refs[17:27]
    bulk, buoy, buoy_x, dp, dv, bulk_img, buoy_img, across_y, across_z, flat = refs[27:]
    tile_x, tile_y = pieces[0].shape[1:3]
    xs, ys, zs = bulk.shape
    residue = lax.rem(lax.axis_index("tile"), stripes)
    entry = entry_of(entry_ref)
    corner = lax.div(entry, held)

    def place_of(hop):
        return lax.rem((residue ^ hop) - corner + stripes, stripes) * tile_x

    for hop in range(stripes):
        cells = pl.ds(place_of(hop), tile_x)
        speed, density = pieces[hop][0], pieces[hop][1]
        bulk[cells] = (COEF[0] / SHARE) * (density * speed * speed)
        light = (COEF[0] / SHARE) / density
        buoy[cells] = light
        buoy_x[cells] = SHARE * light

    def push(fields, first, note):
        p, v0, v1, v2 = fields
        if first is None:
            pair = halves(p[REACH : REACH + xs])
            across_y[...] = along_y(pair, ahead_y[...]).reshape(xs, ys, zs)
            across_z[...] = along_z(pair, ahead_z[...]).reshape(xs, ys, zs)

        def block(x0, count, y0):
            rows = pl.ds(y0, ROWS)
            plane = window(xs, x0, lambda x: p[REACH + x, rows])
            for offset in range(count):
                x = x0 + offset
                slope = slope_x(plane, offset) if first is None else first[0, x, rows]
                change = buoy_x[x, rows] * slope
                moved = v0[REACH + x, rows] + change
                v0[REACH + x, rows] = moved
                note(0, x, rows, (change,), (moved,))

        def block_yz(x0, count, y0):
            rows = pl.ds(y0, ROWS)
            for x in range(count):
                x = x0 + x
                slope_y = across_y[x, rows] if first is None else first[1, x, rows]
                slope_z = across_z[x, rows] if first is None else first[2, x, rows]
                light = buoy[x, rows]
                changes = (light * slope_y, light * slope_z)
                moved = (v1[x, rows] + changes[0], v2[x, rows] + changes[1])
                v1[x, rows] = moved[0]
                v2[x, rows] = moved[1]
                note(1, x, rows, changes, moved)

        blocks(xs, ys, block)
        blocks(xs, ys, block_yz)

    def spread(fields, source, step, note):
        p, v0, v1, v2 = fields
        across = along_y(halves(v1[...]), behind_y[...])
        across = across + along_z(halves(v2[...]), behind_z[...])
        across_z[...] = across.reshape(xs, ys, zs)

        def block(x0, count, y0):
            rows = pl.ds(y0, ROWS)
            plane = window(xs, x0, lambda x: v0[REACH + x, rows])
            for offset in range(count):
                along_x = combine(lambda k: plane(offset + k - 1), lambda k: plane(offset - k))
                flat[x0 + offset, rows] = SHARE * along_x

        def block_yz(x0, count, y0):
            rows = pl.ds(y0, ROWS)
            for x in range(count):
                x = x0 + x
                change = bulk[x, rows] * (flat[x, rows] + across_z[x, rows])
                change = change + source[step, x, rows]
                moved = p[REACH + x, rows] + change
                p[REACH + x, rows] = moved
                note(x, rows, change, moved)

        blocks(xs, ys, block)
        blocks(xs, ys, block_yz)

    fields = (p, v0, v1, v2)
    for step in range(steps):

        def keep_dv(first, x, rows, changes, moved, step=step):
            for d, change in enumerate(changes, first):
                dv[step, d, x, rows] = change

        def keep_dp(x, rows, change, moved, step=step):
            dp[step, x, rows] = change

        push(fields, fwd_slope if step == 0 else None, keep_dv)
        spread(fields, fwd_source, step, keep_dp)

    fields = (q, w0, w1, w2)
    for step in reversed(range(steps)):
        last = step == steps - 1

        def add_buoy(first, x, rows, changes, moved, step=step, last=last):
            image = None if last and first == 0 else buoy_img[x, rows]
            for d, values in enumerate(moved, first):
                product = dv[step, d, x, rows] * values
                image = product if image is None else image + product
            buoy_img[x, rows] = image

        def add_bulk(x, rows, change, moved, step=step, last=last):
            image = dp[step, x, rows] * moved
            bulk_img[x, rows] = image if last else bulk_img[x, rows] + image

        push(fields, adj_slope if last else None, add_buoy)
        spread(fields, adj_source, step, add_bulk)

    tile_rows = tile_x * tile_y
    for chip in range(chips):
        for ref, hop in ((kept, 2 * chip), (traded, 2 * chip + 1)):
            cells = pl.ds(place_of(hop), tile_x)
            ref[chip, :tile_rows] = bulk_img[cells].reshape(tile_rows, zs)
            ref[chip, tile_rows : 2 * tile_rows] = buoy_img[cells].reshape(tile_rows, zs)
            ref[chip, 2 * tile_rows :] = jnp.full((8, zs), entry).astype(jnp.float32)


def merge_kernel(chips, kept, came, *outs):
    rows = kept.shape[1] - 8
    for index, out in enumerate(outs):
        for shot, source in enumerate((kept, came)):
            out[shot * rows : (shot + 1) * rows] = source[index % chips, :rows]
            first = 2 * rows + 4 * shot
            out[first : first + 4] = source[index % chips, rows : rows + 4]


def add_kernel(chips, groups, held, *refs):
    came, parts, total = refs[: 2 * chips], refs[2 * chips : 2 * chips + groups], refs[-1]
    stripes = 2 * chips
    me, group = lax.axis_index("tile"), lax.axis_index("grp")
    tile_rows = total.shape[1] // (held + 1)
    part = parts[0].shape[1]
    total[...] = jnp.zeros_like(total)
    for pair in came:
        for shot in range(2):
            first = 4 * tile_rows + 4 * shot
            entry = jnp.max(pair[first : first + 4]).astype(jnp.int32)
            corner, column = lax.div(entry, held), lax.rem(entry, held)
            mine = (corner <= me) & (me < corner + stripes)
            slot = jnp.where(mine, column, held)
            rows = pl.ds(pl.multiple_of(slot * tile_rows, tile_rows), tile_rows)
            for field in range(2):
                first = (2 * shot + field) * tile_rows
                total[field, rows] = total[field, rows] + pair[first : first + tile_rows]
    for index, hop in enumerate([0] + far_first(groups)):
        first = pl.multiple_of((group ^ hop) * part, part)
        for field in range(2):
            parts[index][field] = total[field, pl.ds(first, part)]


def far_first(groups):
    return list(range(groups - 1, 0, -1))


def grads_kernel(scale, groups, *refs):
    parts, speed_ref, density_ref, grads = refs[:groups], *refs[groups:]
    part = parts[0].shape[1]
    rows = pl.ds(pl.multiple_of(lax.axis_index("grp") * part, part), part)
    speed, density = speed_ref[rows], density_ref[rows]
    bulk_sum, buoy_sum = parts[0][0], parts[0][1]
    for other in parts[1:]:
        bulk_sum = bulk_sum + other[0]
        buoy_sum = buoy_sum + other[1]
    grads[0] = scale * (bulk_sum * (2.0 * density * speed))
    grads[1] = scale * (bulk_sum * (speed * speed) - buoy_sum / (density * density))


def per_device(speed, density, fwd_state, adj_state, aperture, src_pos, wavelet, rec_pos, residual):
    owners = lax.axis_size("tile")
    groups = lax.axis_size("grp")
    my_group = lax.axis_index("grp")
    held, tile_x, tile_y, depth = speed.shape
    stripes = aperture.shape[1]
    chips = stripes // 2
    steps = wavelet.shape[1]
    xs = stripes * tile_x
    f32 = jnp.float32
    cells = (xs, tile_y, depth)

    def shape(*dims):
        return jax.ShapeDtypeStruct(dims, f32)

    def across(values, hop):
        return lax.ppermute(values, "tile", [(t, t ^ hop) for t in range(owners)])

    far_speed = across(speed, stripes)
    far_density = across(density, stripes)
    lists = {hop: across(aperture, hop) for hop in range(stripes - 1, 0, -1)}
    four = [
        (xs + 2 * REACH, tile_y, depth),
        (xs + 2 * REACH, tile_y, depth),
        cells,
        cells,
    ]
    near_speed, near_density, entry = pl.pallas_call(
        near_kernel,
        out_shape=[
            shape(*speed.shape),
            shape(*speed.shape),
            jax.ShapeDtypeStruct((8, depth), jnp.int32),
        ],
        in_specs=[VMEM] * 3,
        out_specs=[VMEM] * 3,
        compiler_params=PARAMS,
        cost_estimate=pl.CostEstimate(flops=4_000_000, bytes_accessed=6_000_000, transcendentals=0),
        name="hold_near_tiles",
    )(speed, density, aperture)
    pieces = pl.pallas_call(
        functools.partial(pick_kernel, chips),
        out_shape=[shape(2, tile_x, tile_y, depth)] * stripes,
        in_specs=[VMEM] * (4 + stripes),
        out_specs=[VMEM] * stripes,
        compiler_params=PARAMS,
        name="pick_tiles",
    )(near_speed, near_density, far_speed, far_density, entry, *[lists[h] for h in range(1, stripes)])
    moved = {hop: across(pieces[hop], hop) for hop in range(stripes - 1, 0, -1)}

    prepared = pl.pallas_call(
        functools.partial(prepare_kernel, steps),
        out_shape=[shape(3, *cells)] * 2
        + [shape(steps, *cells)] * 2
        + [jax.ShapeDtypeStruct((2 * depth, depth), jnp.bfloat16)] * 2
        + [jax.ShapeDtypeStruct((SPAN * tile_y, SPAN * tile_y), jnp.bfloat16)] * 2
        + [shape(*dims) for dims in four + four],
        in_specs=[VMEM] * 2 + [SMEM] * 4 + [VMEM],
        out_specs=[VMEM] * 16,
        compiler_params=PARAMS,
        cost_estimate=pl.CostEstimate(flops=4_000_000, bytes_accessed=6_000_000, transcendentals=0),
        name="prepare",
    )(fwd_state, adj_state, src_pos, wavelet, jnp.swapaxes(rec_pos, 1, 2), residual, pieces[0])
    prepared, fields = prepared[:8], prepared[8:]
    pieces = [pieces[0]] + [moved[hop] for hop in range(1, stripes)]

    tile_rows = tile_x * tile_y
    sent = shape(chips, 2 * tile_rows + 8, depth)
    kept, traded, *_ = pl.pallas_call(
        functools.partial(wave_kernel, chips, steps, held),
        out_shape=[sent, sent] + [shape(*dims) for dims in four + four],
        in_specs=[VMEM] * (stripes + 17),
        out_specs=[VMEM] * 10,
        scratch_shapes=[pltpu.VMEM(cells, f32)] * 3
        + [pltpu.VMEM((steps,) + cells, f32), pltpu.VMEM((steps, 3) + cells, f32)]
        + [pltpu.VMEM(cells, f32)] * 5,
        input_output_aliases={stripes + 9 + index: 2 + index for index in range(8)},
        compiler_params=PARAMS,
        name="replay_and_adjoint",
    )(*pieces, *prepared, entry, *fields)

    both = shape(4 * tile_rows + 8, depth)
    stacks = pl.pallas_call(
        functools.partial(merge_kernel, chips),
        out_shape=[both] * chips,
        in_specs=[VMEM] * 2,
        out_specs=[VMEM] * chips,
        compiler_params=PARAMS,
        name="merge_pair",
    )(kept, across(traded, 1))
    came = [
        across(stacks[chip], 2 * chip + stripes * half)
        for half in range(2)
        for chip in range(chips)
        if chip or half
    ]

    rows = held * tile_rows
    part = rows // groups
    part_shape = shape(2, part, depth)
    parts = pl.pallas_call(
        functools.partial(add_kernel, chips, groups, held),
        out_shape=[part_shape] * groups,
        in_specs=[VMEM] * stripes,
        out_specs=[VMEM] * groups,
        scratch_shapes=[pltpu.VMEM((2, rows + tile_rows, depth), f32)],
        compiler_params=PARAMS,
        name="add_stripes",
    )(stacks[0], *came)

    def along(values, hop):
        return lax.ppermute(values, "grp", [(g, g ^ hop) for g in range(groups)])

    parts = [parts[0]] + [along(values, hop) for values, hop in zip(parts[1:], far_first(groups))]
    grads = pl.pallas_call(
        functools.partial(grads_kernel, 1.0 / math.sqrt(groups * owners), groups),
        out_shape=part_shape,
        in_specs=[VMEM] * (groups + 2),
        out_specs=VMEM,
        compiler_params=PARAMS,
        name="gradients",
    )(*parts, near_speed.reshape(rows, depth), near_density.reshape(rows, depth))

    whole = jnp.zeros((2, groups, part, depth), f32)
    for hop in range(groups):
        values = grads
        if hop:
            values = lax.ppermute(grads, "grp", [(g, (g + hop) % groups) for g in range(groups)])
        place = lax.rem(my_group - hop + groups, groups)
        whole = lax.dynamic_update_slice_in_dim(whole, values[:, None], place, axis=1)
    return (whole[0].reshape(speed.shape), whole[1].reshape(speed.shape))


def solution(mesh):
    return jax.shard_map(
        per_device,
        mesh=mesh,
        in_specs=(
            P("tile", None, None, None),
            P("tile", None, None, None),
            P(("grp", "tile"), None, None, None, None),
            P(("grp", "tile"), None, None, None, None),
            P(("grp", "tile"), None),
            P(("grp", "tile"), None),
            P(("grp", "tile"), None),
            P(("grp", "tile"), None, None),
            P(("grp", "tile"), None, None),
        ),
        out_specs=(P("tile", None, None, None), P("tile", None, None, None)),
        check_vma=False,
    )
```

```python
import functools
import math

import jax
import jax.numpy as jnp
from jax import lax
from jax.experimental import pallas as pl
from jax.experimental.pallas import tpu as pltpu
from jax.sharding import PartitionSpec as P

COEF = (1225.0 / 1024.0, -245.0 / 3072.0, 49.0 / 5120.0, -5.0 / 7168.0)
REACH = 4
SHARE = 15.0 / 16.0
EDGE = 8
ROWS = 8
SPAN = 8

SMEM = pl.BlockSpec(memory_space=pltpu.SMEM)
VMEM = pl.BlockSpec(memory_space=pltpu.VMEM)
PARAMS = pltpu.CompilerParams(vmem_limit_bytes=36 * 1024 * 1024)


def entry_of(list_ref):
    return jnp.max(list_ref[0:1, 0:1].astype(jnp.float32)).astype(jnp.int32)


def combine(ahead, behind):
    total = None
    for order in range(1, 5):
        upper, lower = ahead(order), behind(order)
        if upper is None and lower is None:
            continue
        if lower is None:
            term = upper
        elif upper is None:
            term = -lower
        else:
            term = upper - lower
        if order > 1:
            term = (COEF[order - 1] / COEF[0]) * term
        total = term if total is None else total + term
    return total


def band(first, depth):
    source = lax.broadcasted_iota(jnp.int32, (depth, depth), 0)
    target = lax.broadcasted_iota(jnp.int32, (depth, depth), 1)
    total = jnp.zeros((depth, depth), jnp.float32)
    for order in range(1, 5):
        weight = SHARE * COEF[order - 1] / COEF[0]
        total = jnp.where(source == target + (first + order - 1), weight, total)
        total = jnp.where(source == target + (first - order), -weight, total)
    one = total.astype(jnp.bfloat16)
    return jnp.concatenate([one, one], axis=0)


def along_z(values, matrix):
    xs, ys, zs = values.shape
    values = values.reshape(xs * ys, zs)
    high = values.astype(jnp.bfloat16)
    low = (values - high.astype(jnp.float32)).astype(jnp.bfloat16)
    pair = jnp.concatenate([high, low], axis=1)
    parts = jnp.dot(pair, matrix, preferred_element_type=jnp.float32)
    return parts.reshape(xs, ys, zs)


def blocks(xs, ys, body):
    if xs <= SPAN:
        for y0 in range(0, ys, ROWS):
            body(0, xs, y0)
        return

    def span(index, _):
        for y0 in range(0, ys, ROWS):
            body(index * SPAN, SPAN, y0)
        return 0

    lax.fori_loop(0, xs // SPAN, span, 0)


def window(xs, x0, load):
    kept = {}

    def at(offset):
        if xs <= SPAN and not 0 <= offset < xs:
            return None
        if offset not in kept:
            kept[offset] = load(x0 + offset)
        return kept[offset]

    return at


def slopes(xs, p, x0, y0, plane, offset):
    centre = plane(offset)
    here = x0 + offset + REACH
    return (
        combine(lambda k: plane(offset + k), lambda k: plane(offset + 1 - k)),
        combine(
            lambda k: p[here, pl.ds(EDGE + y0 + k, ROWS)],
            lambda k: centre if k == 1 else p[here, pl.ds(EDGE + y0 + 1 - k, ROWS)],
        ),
    )


def prepare_kernel(
    steps, fwd, adj, src, wave, rec, res, _piece,
    fwd_slope, adj_slope, fwd_source, adj_source, ahead, behind, *fields,
):
    xs, ys, zs = fwd_slope.shape[1:]
    ahead[...] = band(1, zs)
    behind[...] = band(0, zs)

    def clear(ref):
        ref[...] = jnp.zeros(ref.shape, jnp.float32)

    for state, (p, v0, v1, v2), slope in (
        (fwd, fields[:4], fwd_slope),
        (adj, fields[4:], adj_slope),
    ):
        for ref in (p, v0):
            clear(ref.at[:REACH])
            clear(ref.at[REACH + xs :])
        for ref in (p.at[pl.ds(REACH, xs)], v1):
            clear(ref.at[:, :EDGE])
            clear(ref.at[:, EDGE + ys :])
        for x in range(xs):
            p[REACH + x, EDGE : EDGE + ys] = state[0, 0, x].astype(jnp.float32)
            v0[REACH + x] = state[0, 1, x].astype(jnp.float32)
            v1[x, EDGE : EDGE + ys] = state[0, 2, x].astype(jnp.float32)
            v2[x] = state[0, 3, x].astype(jnp.float32)

        def block(x0, count, y0, p=p, slope=slope):
            plane = window(xs, x0, lambda x: p[REACH + x, pl.ds(EDGE + y0, ROWS)])
            for offset in range(count):
                for d, values in enumerate(slopes(xs, p, x0, y0, plane, offset)):
                    slope[d, x0 + offset, pl.ds(y0, ROWS)] = values

        blocks(xs, ys, block)
        slope[2] = along_z(p[REACH : REACH + xs, EDGE : EDGE + ys], ahead[...])

    row = lax.broadcasted_iota(jnp.int32, (ys, zs), 0)
    lane = lax.broadcasted_iota(jnp.int32, (ys, zs), 1)
    src_mark = (row == src[0, 1]) & (lane == src[0, 2])
    for x in range(xs):
        rec_mark = (row == rec[0, 0, x]) & (lane == rec[0, 1, x])
        for step in range(steps):
            amplitude = jnp.where(x == src[0, 0], wave[0, step], 0.0)
            fwd_source[step, x] = jnp.where(src_mark, amplitude, 0.0)
            adj_source[step, x] = jnp.where(rec_mark, res[0, step, x], 0.0)


def near_kernel(speed, density, aperture, near_speed, near_density, entry):
    near_speed[...] = speed[...]
    near_density[...] = density[...]
    entry[...] = jnp.full(entry.shape, entry_of(aperture), jnp.int32)


def pick_kernel(chips, near_speed, near_density, far_speed, far_density, *refs):
    stripes = 2 * chips
    lists, outs = refs[:stripes], refs[stripes:]
    held = near_speed.shape[0]
    me = lax.axis_index("tile")
    residue, half = lax.rem(me, stripes), lax.div(me, stripes)
    for hop in range(stripes):
        entry = entry_of(lists[hop])
        corner, column = lax.div(entry, held), lax.rem(entry, held)
        here = (residue >= corner) == (half == 0)
        piece = outs[hop]

        @pl.when(here)
        def _():
            piece[0] = near_speed[column]
            piece[1] = near_density[column]

        @pl.when(jnp.logical_not(here))
        def _():
            piece[0] = far_speed[column]
            piece[1] = far_density[column]


def wave_kernel(chips, steps, held, *refs):
    stripes = 2 * chips
    pieces, refs = refs[:stripes], refs[stripes:]
    fwd_slope, adj_slope, fwd_source, adj_source, ahead, behind, entry_ref = refs[:7]
    kept, traded, p, v0, v1, v2, q, w0, w1, w2 = refs[15:25]
    bulk, buoy, buoy_z, dp, dv, bulk_img, buoy_img, across_z, flat = refs[25:]
    tile_x, tile_y = pieces[0].shape[1:3]
    xs, ys, zs = bulk.shape
    residue = lax.rem(lax.axis_index("tile"), stripes)
    entry = entry_of(entry_ref)
    corner = lax.div(entry, held)

    def place_of(hop):
        return lax.rem((residue ^ hop) - corner + stripes, stripes) * tile_x

    for hop in range(stripes):
        cells = pl.ds(place_of(hop), tile_x)
        speed, density = pieces[hop][0], pieces[hop][1]
        bulk[cells] = COEF[0] * (density * speed * speed)
        light = COEF[0] / density
        buoy[cells] = light
        buoy_z[cells] = light / SHARE

    def push(fields, first, note):
        p, v0, v1, v2 = fields
        if first is None:
            across_z[...] = along_z(p[REACH : REACH + xs, EDGE : EDGE + ys], ahead[...])

        def block(x0, count, y0):
            rows, inner = pl.ds(y0, ROWS), pl.ds(EDGE + y0, ROWS)
            plane = window(xs, x0, lambda x: p[REACH + x, inner])
            for offset in range(count):
                x = x0 + offset
                if first is None:
                    two = slopes(xs, p, x0, y0, plane, offset)
                else:
                    two = (first[0, x, rows], first[1, x, rows])
                light = buoy[x, rows]
                changes = (light * two[0], light * two[1])
                moved = (v0[REACH + x, rows] + changes[0], v1[x, inner] + changes[1])
                v0[REACH + x, rows] = moved[0]
                v1[x, inner] = moved[1]
                note(0, x, rows, changes, moved)

        def block_z(x0, count, y0):
            rows = pl.ds(y0, ROWS)
            for x in range(count):
                x = x0 + x
                slope = across_z[x, rows] if first is None else first[2, x, rows]
                change = buoy_z[x, rows] * slope
                moved = v2[x, rows] + change
                v2[x, rows] = moved
                note(2, x, rows, (change,), (moved,))

        blocks(xs, ys, block)
        blocks(xs, ys, block_z)

    def spread(fields, source, step, note):
        p, v0, v1, v2 = fields
        across_z[...] = along_z(v2[...], behind[...])

        def block(x0, count, y0):
            rows = pl.ds(y0, ROWS)
            plane = window(xs, x0, lambda x: v0[REACH + x, rows])
            for offset in range(count):
                x = x0 + offset
                along_x = combine(lambda k: plane(offset + k - 1), lambda k: plane(offset - k))
                along_y = combine(
                    lambda k: v1[x, pl.ds(EDGE + y0 + k - 1, ROWS)],
                    lambda k: v1[x, pl.ds(EDGE + y0 - k, ROWS)],
                )
                flat[x, rows] = along_x + along_y

        def block_z(x0, count, y0):
            rows, inner = pl.ds(y0, ROWS), pl.ds(EDGE + y0, ROWS)
            for x in range(count):
                x = x0 + x
                change = bulk[x, rows] * (flat[x, rows] + (1.0 / SHARE) * across_z[x, rows])
                change = change + source[step, x, rows]
                moved = p[REACH + x, inner] + change
                p[REACH + x, inner] = moved
                note(x, rows, change, moved)

        blocks(xs, ys, block)
        blocks(xs, ys, block_z)

    fields = (p, v0, v1, v2)
    for step in range(steps):

        def keep_dv(first, x, rows, changes, moved, step=step):
            for d, change in enumerate(changes, first):
                dv[step, d, x, rows] = change

        def keep_dp(x, rows, change, moved, step=step):
            dp[step, x, rows] = change

        push(fields, fwd_slope if step == 0 else None, keep_dv)
        spread(fields, fwd_source, step, keep_dp)

    fields = (q, w0, w1, w2)
    for step in reversed(range(steps)):
        last = step == steps - 1

        def add_buoy(first, x, rows, changes, moved, step=step, last=last):
            image = None if last and first == 0 else buoy_img[x, rows]
            for d, values in enumerate(moved, first):
                product = dv[step, d, x, rows] * values
                image = product if image is None else image + product
            buoy_img[x, rows] = image

        def add_bulk(x, rows, change, moved, step=step, last=last):
            image = dp[step, x, rows] * moved
            bulk_img[x, rows] = image if last else bulk_img[x, rows] + image

        push(fields, adj_slope if last else None, add_buoy)
        spread(fields, adj_source, step, add_bulk)

    tile_rows = tile_x * tile_y
    for chip in range(chips):
        for ref, hop in ((kept, 2 * chip), (traded, 2 * chip + 1)):
            cells = pl.ds(place_of(hop), tile_x)
            ref[chip, :tile_rows] = bulk_img[cells].reshape(tile_rows, zs)
            ref[chip, tile_rows : 2 * tile_rows] = buoy_img[cells].reshape(tile_rows, zs)
            ref[chip, 2 * tile_rows :] = jnp.full((8, zs), entry).astype(jnp.float32)


def merge_kernel(chips, kept, came, *outs):
    rows = kept.shape[1] - 8
    for index, out in enumerate(outs):
        for shot, source in enumerate((kept, came)):
            out[shot * rows : (shot + 1) * rows] = source[index % chips, :rows]
            first = 2 * rows + 4 * shot
            out[first : first + 4] = source[index % chips, rows : rows + 4]


def add_kernel(chips, groups, held, *refs):
    came, parts, total = refs[: 2 * chips], refs[2 * chips : 2 * chips + groups], refs[-1]
    stripes = 2 * chips
    me, group = lax.axis_index("tile"), lax.axis_index("grp")
    tile_rows = total.shape[1] // (held + 1)
    part = parts[0].shape[1]
    total[...] = jnp.zeros_like(total)
    for pair in came:
        for shot in range(2):
            first = 4 * tile_rows + 4 * shot
            entry = jnp.max(pair[first : first + 4]).astype(jnp.int32)
            corner, column = lax.div(entry, held), lax.rem(entry, held)
            mine = (corner <= me) & (me < corner + stripes)
            slot = jnp.where(mine, column, held)
            rows = pl.ds(pl.multiple_of(slot * tile_rows, tile_rows), tile_rows)
            for field in range(2):
                first = (2 * shot + field) * tile_rows
                total[field, rows] = total[field, rows] + pair[first : first + tile_rows]
    for index, hop in enumerate([0] + far_first(groups)):
        first = pl.multiple_of((group ^ hop) * part, part)
        for field in range(2):
            parts[index][field] = total[field, pl.ds(first, part)]


def far_first(groups):
    return list(range(groups - 1, 0, -1))


def grads_kernel(scale, groups, *refs):
    parts, speed_ref, density_ref, grads = refs[:groups], *refs[groups:]
    part = parts[0].shape[1]
    rows = pl.ds(pl.multiple_of(lax.axis_index("grp") * part, part), part)
    speed, density = speed_ref[rows], density_ref[rows]
    bulk_sum, buoy_sum = parts[0][0], parts[0][1]
    for other in parts[1:]:
        bulk_sum = bulk_sum + other[0]
        buoy_sum = buoy_sum + other[1]
    grads[0] = scale * (bulk_sum * (2.0 * density * speed))
    grads[1] = scale * (bulk_sum * (speed * speed) - buoy_sum / (density * density))


def per_device(speed, density, fwd_state, adj_state, aperture, src_pos, wavelet, rec_pos, residual):
    owners = lax.axis_size("tile")
    groups = lax.axis_size("grp")
    my_group = lax.axis_index("grp")
    held, tile_x, tile_y, depth = speed.shape
    stripes = aperture.shape[1]
    chips = stripes // 2
    steps = wavelet.shape[1]
    xs = stripes * tile_x
    f32 = jnp.float32
    cells = (xs, tile_y, depth)

    def shape(*dims):
        return jax.ShapeDtypeStruct(dims, f32)

    def across(values, hop):
        return lax.ppermute(values, "tile", [(t, t ^ hop) for t in range(owners)])

    far_speed = across(speed, stripes)
    far_density = across(density, stripes)
    lists = {hop: across(aperture, hop) for hop in range(stripes - 1, 0, -1)}
    four = [
        (xs + 2 * REACH, tile_y + 2 * EDGE, depth),
        (xs + 2 * REACH, tile_y, depth),
        (xs, tile_y + 2 * EDGE, depth),
        cells,
    ]
    near_speed, near_density, entry = pl.pallas_call(
        near_kernel,
        out_shape=[
            shape(*speed.shape),
            shape(*speed.shape),
            jax.ShapeDtypeStruct((8, depth), jnp.int32),
        ],
        in_specs=[VMEM] * 3,
        out_specs=[VMEM] * 3,
        compiler_params=PARAMS,
        cost_estimate=pl.CostEstimate(flops=4_000_000, bytes_accessed=6_000_000, transcendentals=0),
        name="hold_near_tiles",
    )(speed, density, aperture)
    pieces = pl.pallas_call(
        functools.partial(pick_kernel, chips),
        out_shape=[shape(2, tile_x, tile_y, depth)] * stripes,
        in_specs=[VMEM] * (4 + stripes),
        out_specs=[VMEM] * stripes,
        compiler_params=PARAMS,
        name="pick_tiles",
    )(near_speed, near_density, far_speed, far_density, entry, *[lists[h] for h in range(1, stripes)])
    moved = {hop: across(pieces[hop], hop) for hop in range(stripes - 1, 0, -1)}

    prepared = pl.pallas_call(
        functools.partial(prepare_kernel, steps),
        out_shape=[shape(3, *cells)] * 2
        + [shape(steps, *cells)] * 2
        + [jax.ShapeDtypeStruct((2 * depth, depth), jnp.bfloat16)] * 2
        + [shape(*dims) for dims in four + four],
        in_specs=[VMEM] * 2 + [SMEM] * 4 + [VMEM],
        out_specs=[VMEM] * 14,
        compiler_params=PARAMS,
        cost_estimate=pl.CostEstimate(flops=4_000_000, bytes_accessed=6_000_000, transcendentals=0),
        name="prepare",
    )(fwd_state, adj_state, src_pos, wavelet, jnp.swapaxes(rec_pos, 1, 2), residual, pieces[0])
    prepared, fields = prepared[:6], prepared[6:]
    pieces = [pieces[0]] + [moved[hop] for hop in range(1, stripes)]

    tile_rows = tile_x * tile_y
    sent = shape(chips, 2 * tile_rows + 8, depth)
    kept, traded, *_ = pl.pallas_call(
        functools.partial(wave_kernel, chips, steps, held),
        out_shape=[sent, sent] + [shape(*dims) for dims in four + four],
        in_specs=[VMEM] * (stripes + 15),
        out_specs=[VMEM] * 10,
        scratch_shapes=[pltpu.VMEM(cells, f32)] * 3
        + [pltpu.VMEM((steps,) + cells, f32), pltpu.VMEM((steps, 3) + cells, f32)]
        + [pltpu.VMEM(cells, f32)] * 4,
        input_output_aliases={stripes + 7 + index: 2 + index for index in range(8)},
        compiler_params=PARAMS,
        name="replay_and_adjoint",
    )(*pieces, *prepared, entry, *fields)

    both = shape(4 * tile_rows + 8, depth)
    stacks = pl.pallas_call(
        functools.partial(merge_kernel, chips),
        out_shape=[both] * chips,
        in_specs=[VMEM] * 2,
        out_specs=[VMEM] * chips,
        compiler_params=PARAMS,
        name="merge_pair",
    )(kept, across(traded, 1))
    came = [
        across(stacks[chip], 2 * chip + stripes * half)
        for half in range(2)
        for chip in range(chips)
        if chip or half
    ]

    rows = held * tile_rows
    part = rows // groups
    part_shape = shape(2, part, depth)
    parts = pl.pallas_call(
        functools.partial(add_kernel, chips, groups, held),
        out_shape=[part_shape] * groups,
        in_specs=[VMEM] * stripes,
        out_specs=[VMEM] * groups,
        scratch_shapes=[pltpu.VMEM((2, rows + tile_rows, depth), f32)],
        compiler_params=PARAMS,
        name="add_stripes",
    )(stacks[0], *came)

    def along(values, hop):
        return lax.ppermute(values, "grp", [(g, g ^ hop) for g in range(groups)])

    parts = [parts[0]] + [along(values, hop) for values, hop in zip(parts[1:], far_first(groups))]
    grads = pl.pallas_call(
        functools.partial(grads_kernel, 1.0 / math.sqrt(groups * owners), groups),
        out_shape=part_shape,
        in_specs=[VMEM] * (groups + 2),
        out_specs=VMEM,
        compiler_params=PARAMS,
        name="gradients",
    )(*parts, near_speed.reshape(rows, depth), near_density.reshape(rows, depth))

    whole = jnp.zeros((2, groups, part, depth), f32)
    for hop in [0, 2, 1] + list(range(3, groups)):
        values = grads
        if hop:
            values = lax.ppermute(grads, "grp", [(g, (g + hop) % groups) for g in range(groups)])
        place = lax.rem(my_group - hop + groups, groups)
        whole = lax.dynamic_update_slice_in_dim(whole, values[:, None], place, axis=1)
    return (whole[0].reshape(speed.shape), whole[1].reshape(speed.shape))


def solution(mesh):
    return jax.shard_map(
        per_device,
        mesh=mesh,
        in_specs=(
            P("tile", None, None, None),
            P("tile", None, None, None),
            P(("grp", "tile"), None, None, None, None),
            P(("grp", "tile"), None, None, None, None),
            P(("grp", "tile"), None),
            P(("grp", "tile"), None),
            P(("grp", "tile"), None),
            P(("grp", "tile"), None, None),
            P(("grp", "tile"), None, None),
        ),
        out_specs=(P("tile", None, None, None), P("tile", None, None, None)),
        check_vma=False,
    )
```

```python
import functools
import math

import jax
import jax.numpy as jnp
from jax import lax
from jax.experimental import pallas as pl
from jax.experimental.pallas import tpu as pltpu
from jax.sharding import PartitionSpec as P

COEF = (1225.0 / 1024.0, -245.0 / 3072.0, 49.0 / 5120.0, -5.0 / 7168.0)
REACH = 4
EDGE = 8
ROWS = 8
SPAN = 8

SMEM = pl.BlockSpec(memory_space=pltpu.SMEM)
VMEM = pl.BlockSpec(memory_space=pltpu.VMEM)
PARAMS = pltpu.CompilerParams(vmem_limit_bytes=36 * 1024 * 1024)


def entry_of(list_ref):
    return jnp.max(list_ref[0:1, 0:1].astype(jnp.float32)).astype(jnp.int32)


def combine(ahead, behind):
    total = None
    for order in range(1, 5):
        upper, lower = ahead(order), behind(order)
        if upper is None and lower is None:
            continue
        if lower is None:
            term = upper
        elif upper is None:
            term = -lower
        else:
            term = upper - lower
        if order > 1:
            term = (COEF[order - 1] / COEF[0]) * term
        total = term if total is None else total + term
    return total


def band(first, depth):
    source = lax.broadcasted_iota(jnp.int32, (depth, depth), 0)
    target = lax.broadcasted_iota(jnp.int32, (depth, depth), 1)
    total = jnp.zeros((depth, depth), jnp.float32)
    for order in range(1, 5):
        weight = COEF[order - 1] / COEF[0]
        total = total + jnp.where(source == target + (first + order - 1), weight, 0.0)
        total = total - jnp.where(source == target + (first - order), weight, 0.0)
    return jnp.concatenate(halves(total), axis=1)


def halves(values):
    high = values.astype(jnp.bfloat16)
    return high, (values - high.astype(jnp.float32)).astype(jnp.bfloat16)


def along_z(values, matrix):
    xs, ys, zs = values.shape
    pair = jnp.concatenate(halves(values.reshape(xs * ys, zs)), axis=1)
    parts = jnp.dot(pair, matrix, preferred_element_type=jnp.float32)
    return (parts[:, :zs] + parts[:, zs:]).reshape(xs, ys, zs)


def blocks(xs, ys, body):
    if xs <= SPAN:
        for y0 in range(0, ys, ROWS):
            body(0, xs, y0)
        return

    def span(index, _):
        for y0 in range(0, ys, ROWS):
            body(index * SPAN, SPAN, y0)
        return 0

    lax.fori_loop(0, xs // SPAN, span, 0)


def window(xs, x0, load):
    kept = {}

    def at(offset):
        if xs <= SPAN and not 0 <= offset < xs:
            return None
        if offset not in kept:
            kept[offset] = load(x0 + offset)
        return kept[offset]

    return at


def slopes(xs, p, x0, y0, plane, offset):
    centre = plane(offset)
    here = x0 + offset + REACH
    return (
        combine(lambda k: plane(offset + k), lambda k: plane(offset + 1 - k)),
        combine(
            lambda k: p[here, pl.ds(EDGE + y0 + k, ROWS)],
            lambda k: centre if k == 1 else p[here, pl.ds(EDGE + y0 + 1 - k, ROWS)],
        ),
    )


def prepare_kernel(
    steps, fwd, adj, src, wave, rec, res, _piece,
    fwd_slope, adj_slope, fwd_source, adj_source, ahead, behind, *fields,
):
    xs, ys, zs = fwd_slope.shape[1:]
    for ref, first in ((ahead, 1), (behind, 0)):
        one = band(first, zs)
        ref[:zs] = one
        ref[zs:] = one

    def clear(ref):
        ref[...] = jnp.zeros(ref.shape, jnp.float32)

    for state, (p, v0, v1, v2), slope in (
        (fwd, fields[:4], fwd_slope),
        (adj, fields[4:], adj_slope),
    ):
        for ref in (p, v0):
            clear(ref.at[:REACH])
            clear(ref.at[REACH + xs :])
        for ref in (p.at[pl.ds(REACH, xs)], v1):
            clear(ref.at[:, :EDGE])
            clear(ref.at[:, EDGE + ys :])
        for x in range(xs):
            p[REACH + x, EDGE : EDGE + ys] = state[0, 0, x].astype(jnp.float32)
            v0[REACH + x] = state[0, 1, x].astype(jnp.float32)
            v1[x, EDGE : EDGE + ys] = state[0, 2, x].astype(jnp.float32)
            v2[x] = state[0, 3, x].astype(jnp.float32)

        def block(x0, count, y0, p=p, slope=slope):
            plane = window(xs, x0, lambda x: p[REACH + x, pl.ds(EDGE + y0, ROWS)])
            for offset in range(count):
                for d, values in enumerate(slopes(xs, p, x0, y0, plane, offset)):
                    slope[d, x0 + offset, pl.ds(y0, ROWS)] = values

        blocks(xs, ys, block)
        slope[2] = along_z(p[REACH : REACH + xs, EDGE : EDGE + ys], ahead[...])

    row = lax.broadcasted_iota(jnp.int32, (ys, zs), 0)
    lane = lax.broadcasted_iota(jnp.int32, (ys, zs), 1)
    src_mark = (row == src[0, 1]) & (lane == src[0, 2])
    for x in range(xs):
        rec_mark = (row == rec[0, 0, x]) & (lane == rec[0, 1, x])
        for step in range(steps):
            amplitude = jnp.where(x == src[0, 0], wave[0, step], 0.0)
            fwd_source[step, x] = jnp.where(src_mark, amplitude, 0.0)
            adj_source[step, x] = jnp.where(rec_mark, res[0, step, x], 0.0)


def near_kernel(speed, density, aperture, near_speed, near_density, entry):
    near_speed[...] = speed[...]
    near_density[...] = density[...]
    entry[...] = jnp.full(entry.shape, entry_of(aperture), jnp.int32)


def pick_kernel(chips, near_speed, near_density, far_speed, far_density, *refs):
    stripes = 2 * chips
    lists, outs = refs[:stripes], refs[stripes:]
    held = near_speed.shape[0]
    me = lax.axis_index("tile")
    residue, half = lax.rem(me, stripes), lax.div(me, stripes)
    for hop in range(stripes):
        entry = entry_of(lists[hop])
        corner, column = lax.div(entry, held), lax.rem(entry, held)
        here = (residue >= corner) == (half == 0)
        piece = outs[hop]

        @pl.when(here)
        def _():
            piece[0] = near_speed[column]
            piece[1] = near_density[column]

        @pl.when(jnp.logical_not(here))
        def _():
            piece[0] = far_speed[column]
            piece[1] = far_density[column]


def wave_kernel(chips, steps, held, *refs):
    stripes = 2 * chips
    pieces, refs = refs[:stripes], refs[stripes:]
    fwd_slope, adj_slope, fwd_source, adj_source, ahead, behind, entry_ref = refs[:7]
    kept, traded, p, v0, v1, v2, q, w0, w1, w2 = refs[15:25]
    bulk, buoy, dp, dv, bulk_img, buoy_img, across_z, flat = refs[25:]
    tile_x, tile_y = pieces[0].shape[1:3]
    xs, ys, zs = bulk.shape
    residue = lax.rem(lax.axis_index("tile"), stripes)
    entry = entry_of(entry_ref)
    corner = lax.div(entry, held)

    def place_of(hop):
        return lax.rem((residue ^ hop) - corner + stripes, stripes) * tile_x

    for hop in range(stripes):
        cells = pl.ds(place_of(hop), tile_x)
        speed, density = pieces[hop][0], pieces[hop][1]
        bulk[cells] = COEF[0] * (density * speed * speed)
        buoy[cells] = COEF[0] / density

    def push(fields, first, note):
        p, v0, v1, v2 = fields
        if first is None:
            across_z[...] = along_z(p[REACH : REACH + xs, EDGE : EDGE + ys], ahead[...])

        def block(x0, count, y0):
            rows, inner = pl.ds(y0, ROWS), pl.ds(EDGE + y0, ROWS)
            plane = window(xs, x0, lambda x: p[REACH + x, inner])
            for offset in range(count):
                x = x0 + offset
                if first is None:
                    two = slopes(xs, p, x0, y0, plane, offset)
                else:
                    two = (first[0, x, rows], first[1, x, rows])
                light = buoy[x, rows]
                changes = (light * two[0], light * two[1])
                moved = (v0[REACH + x, rows] + changes[0], v1[x, inner] + changes[1])
                v0[REACH + x, rows] = moved[0]
                v1[x, inner] = moved[1]
                note(0, x, rows, changes, moved)

        def block_z(x0, count, y0):
            rows = pl.ds(y0, ROWS)
            for x in range(count):
                x = x0 + x
                slope = across_z[x, rows] if first is None else first[2, x, rows]
                change = buoy[x, rows] * slope
                moved = v2[x, rows] + change
                v2[x, rows] = moved
                note(2, x, rows, (change,), (moved,))

        blocks(xs, ys, block)
        blocks(xs, ys, block_z)

    def spread(fields, source, step, note):
        p, v0, v1, v2 = fields
        across_z[...] = along_z(v2[...], behind[...])

        def block(x0, count, y0):
            rows = pl.ds(y0, ROWS)
            plane = window(xs, x0, lambda x: v0[REACH + x, rows])
            for offset in range(count):
                x = x0 + offset
                along_x = combine(lambda k: plane(offset + k - 1), lambda k: plane(offset - k))
                along_y = combine(
                    lambda k: v1[x, pl.ds(EDGE + y0 + k - 1, ROWS)],
                    lambda k: v1[x, pl.ds(EDGE + y0 - k, ROWS)],
                )
                flat[x, rows] = along_x + along_y

        def block_z(x0, count, y0):
            rows, inner = pl.ds(y0, ROWS), pl.ds(EDGE + y0, ROWS)
            for x in range(count):
                x = x0 + x
                change = bulk[x, rows] * (flat[x, rows] + across_z[x, rows])
                change = change + source[step, x, rows]
                moved = p[REACH + x, inner] + change
                p[REACH + x, inner] = moved
                note(x, rows, change, moved)

        blocks(xs, ys, block)
        blocks(xs, ys, block_z)

    fields = (p, v0, v1, v2)
    for step in range(steps):

        def keep_dv(first, x, rows, changes, moved, step=step):
            for d, change in enumerate(changes, first):
                dv[step, d, x, rows] = change

        def keep_dp(x, rows, change, moved, step=step):
            dp[step, x, rows] = change

        push(fields, fwd_slope if step == 0 else None, keep_dv)
        spread(fields, fwd_source, step, keep_dp)

    fields = (q, w0, w1, w2)
    for step in reversed(range(steps)):
        last = step == steps - 1

        def add_buoy(first, x, rows, changes, moved, step=step, last=last):
            image = None if last and first == 0 else buoy_img[x, rows]
            for d, values in enumerate(moved, first):
                product = dv[step, d, x, rows] * values
                image = product if image is None else image + product
            buoy_img[x, rows] = image

        def add_bulk(x, rows, change, moved, step=step, last=last):
            image = dp[step, x, rows] * moved
            bulk_img[x, rows] = image if last else bulk_img[x, rows] + image

        push(fields, adj_slope if last else None, add_buoy)
        spread(fields, adj_source, step, add_bulk)

    tile_rows = tile_x * tile_y
    for chip in range(chips):
        for ref, hop in ((kept, 2 * chip), (traded, 2 * chip + 1)):
            cells = pl.ds(place_of(hop), tile_x)
            ref[chip, :tile_rows] = bulk_img[cells].reshape(tile_rows, zs)
            ref[chip, tile_rows : 2 * tile_rows] = buoy_img[cells].reshape(tile_rows, zs)
            ref[chip, 2 * tile_rows :] = jnp.full((8, zs), entry).astype(jnp.float32)


def return_order(chips):
    even = list(range(chips, 2 * chips)) + list(range(1, chips))
    return list(zip(even, reversed(even)))


def merge_kernel(chips, kept, came, *outs):
    rows = kept.shape[1] - 8
    odd = lax.rem(lax.axis_index("tile"), 2) == 1
    for out, (even_hop, odd_hop) in zip(outs, [(0, 0)] + return_order(chips)):
        chip = jnp.where(odd, odd_hop % chips, even_hop % chips)
        for shot, source in enumerate((kept, came)):
            out[shot * rows : (shot + 1) * rows] = source[chip, :rows]
            first = 2 * rows + 4 * shot
            out[first : first + 4] = source[chip, rows : rows + 4]


def add_kernel(chips, groups, held, *refs):
    came, parts, total = refs[: 2 * chips], refs[2 * chips : 2 * chips + groups], refs[-1]
    stripes = 2 * chips
    me, group = lax.axis_index("tile"), lax.axis_index("grp")
    tile_rows = total.shape[1] // (held + 1)
    part = parts[0].shape[1]
    total[...] = jnp.zeros_like(total)
    for pair in came:
        for shot in range(2):
            first = 4 * tile_rows + 4 * shot
            entry = jnp.max(pair[first : first + 4]).astype(jnp.int32)
            corner, column = lax.div(entry, held), lax.rem(entry, held)
            mine = (corner <= me) & (me < corner + stripes)
            slot = jnp.where(mine, column, held)
            rows = pl.ds(pl.multiple_of(slot * tile_rows, tile_rows), tile_rows)
            for field in range(2):
                first = (2 * shot + field) * tile_rows
                total[field, rows] = total[field, rows] + pair[first : first + tile_rows]
    for index, hop in enumerate([0] + far_first(groups)):
        first = pl.multiple_of((group ^ hop) * part, part)
        for field in range(2):
            parts[index][field] = total[field, pl.ds(first, part)]


def far_first(groups):
    return list(range(groups - 1, 0, -1))


def grads_kernel(scale, groups, *refs):
    parts, speed_ref, density_ref, grads = refs[:groups], *refs[groups:]
    part = parts[0].shape[1]
    rows = pl.ds(pl.multiple_of(lax.axis_index("grp") * part, part), part)
    speed, density = speed_ref[rows], density_ref[rows]
    bulk_sum, buoy_sum = parts[0][0], parts[0][1]
    for other in parts[1:]:
        bulk_sum = bulk_sum + other[0]
        buoy_sum = buoy_sum + other[1]
    grads[0] = scale * (bulk_sum * (2.0 * density * speed))
    grads[1] = scale * (bulk_sum * (speed * speed) - buoy_sum / (density * density))


def per_device(speed, density, fwd_state, adj_state, aperture, src_pos, wavelet, rec_pos, residual):
    owners = lax.axis_size("tile")
    groups = lax.axis_size("grp")
    my_group = lax.axis_index("grp")
    held, tile_x, tile_y, depth = speed.shape
    stripes = aperture.shape[1]
    chips = stripes // 2
    steps = wavelet.shape[1]
    xs = stripes * tile_x
    f32 = jnp.float32
    cells = (xs, tile_y, depth)

    def shape(*dims):
        return jax.ShapeDtypeStruct(dims, f32)

    def across(values, hop):
        return lax.ppermute(values, "tile", [(t, t ^ hop) for t in range(owners)])

    far_speed = across(speed, stripes)
    far_density = across(density, stripes)
    lists = {hop: across(aperture, hop) for hop in range(stripes - 1, 0, -1)}
    four = [
        (xs + 2 * REACH, tile_y + 2 * EDGE, depth),
        (xs + 2 * REACH, tile_y, depth),
        (xs, tile_y + 2 * EDGE, depth),
        cells,
    ]
    near_speed, near_density, entry = pl.pallas_call(
        near_kernel,
        out_shape=[
            shape(*speed.shape),
            shape(*speed.shape),
            jax.ShapeDtypeStruct((8, depth), jnp.int32),
        ],
        in_specs=[VMEM] * 3,
        out_specs=[VMEM] * 3,
        compiler_params=PARAMS,
        cost_estimate=pl.CostEstimate(flops=4_000_000, bytes_accessed=6_000_000, transcendentals=0),
        name="hold_near_tiles",
    )(speed, density, aperture)
    pieces = pl.pallas_call(
        functools.partial(pick_kernel, chips),
        out_shape=[shape(2, tile_x, tile_y, depth)] * stripes,
        in_specs=[VMEM] * (4 + stripes),
        out_specs=[VMEM] * stripes,
        compiler_params=PARAMS,
        name="pick_tiles",
    )(near_speed, near_density, far_speed, far_density, entry, *[lists[h] for h in range(1, stripes)])
    moved = {hop: across(pieces[hop], hop) for hop in range(stripes - 1, 0, -1)}

    prepared = pl.pallas_call(
        functools.partial(prepare_kernel, steps),
        out_shape=[shape(3, *cells)] * 2
        + [shape(steps, *cells)] * 2
        + [jax.ShapeDtypeStruct((2 * depth, 2 * depth), jnp.bfloat16)] * 2
        + [shape(*dims) for dims in four + four],
        in_specs=[VMEM] * 2 + [SMEM] * 4 + [VMEM],
        out_specs=[VMEM] * 14,
        compiler_params=PARAMS,
        cost_estimate=pl.CostEstimate(flops=4_000_000, bytes_accessed=6_000_000, transcendentals=0),
        name="prepare",
    )(fwd_state, adj_state, src_pos, wavelet, jnp.swapaxes(rec_pos, 1, 2), residual, pieces[0])
    prepared, fields = prepared[:6], prepared[6:]
    pieces = [pieces[0]] + [moved[hop] for hop in range(1, stripes)]

    tile_rows = tile_x * tile_y
    sent = shape(chips, 2 * tile_rows + 8, depth)
    kept, traded, *_ = pl.pallas_call(
        functools.partial(wave_kernel, chips, steps, held),
        out_shape=[sent, sent] + [shape(*dims) for dims in four + four],
        in_specs=[VMEM] * (stripes + 15),
        out_specs=[VMEM] * 10,
        scratch_shapes=[
            pltpu.VMEM(cells, f32),
            pltpu.VMEM(cells, f32),
            pltpu.VMEM((steps,) + cells, f32),
            pltpu.VMEM((steps, 3) + cells, f32),
        ]
        + [pltpu.VMEM(cells, f32)] * 4
        + [
        ],
        input_output_aliases={stripes + 7 + index: 2 + index for index in range(8)},
        compiler_params=PARAMS,
        name="replay_and_adjoint",
    )(*pieces, *prepared, entry, *fields)

    both = shape(4 * tile_rows + 8, depth)
    stacks = pl.pallas_call(
        functools.partial(merge_kernel, chips),
        out_shape=[both] * stripes,
        in_specs=[VMEM] * 2,
        out_specs=[VMEM] * stripes,
        compiler_params=PARAMS,
        name="merge_pair",
    )(kept, across(traded, 1))
    came = [
        lax.ppermute(values, "tile", [(t, t ^ (2 * hops[t % 2])) for t in range(owners)])
        for values, hops in zip(stacks[1:], return_order(chips))
    ]
    came = came[-1:] + came[:-1]

    rows = held * tile_rows
    part = rows // groups
    part_shape = shape(2, part, depth)
    parts = pl.pallas_call(
        functools.partial(add_kernel, chips, groups, held),
        out_shape=[part_shape] * groups,
        in_specs=[VMEM] * stripes,
        out_specs=[VMEM] * groups,
        scratch_shapes=[pltpu.VMEM((2, rows + tile_rows, depth), f32)],
        compiler_params=PARAMS,
        name="add_stripes",
    )(stacks[0], *came)

    def along(values, hop):
        return lax.ppermute(values, "grp", [(g, g ^ hop) for g in range(groups)])

    parts = [parts[0]] + [along(values, hop) for values, hop in zip(parts[1:], far_first(groups))]
    grads = pl.pallas_call(
        functools.partial(grads_kernel, 1.0 / math.sqrt(groups * owners), groups),
        out_shape=part_shape,
        in_specs=[VMEM] * (groups + 2),
        out_specs=VMEM,
        compiler_params=PARAMS,
        name="gradients",
    )(*parts, near_speed.reshape(rows, depth), near_density.reshape(rows, depth))

    whole = jnp.zeros((2, groups, part, depth), f32)
    for hop in range(groups):
        values = grads
        if hop:
            values = lax.ppermute(grads, "grp", [(g, (g + hop) % groups) for g in range(groups)])
        place = lax.rem(my_group - hop + groups, groups)
        whole = lax.dynamic_update_slice_in_dim(whole, values[:, None], place, axis=1)
    return (whole[0].reshape(speed.shape), whole[1].reshape(speed.shape))


def solution(mesh):
    return jax.shard_map(
        per_device,
        mesh=mesh,
        in_specs=(
            P("tile", None, None, None),
            P("tile", None, None, None),
            P(("grp", "tile"), None, None, None, None),
            P(("grp", "tile"), None, None, None, None),
            P(("grp", "tile"), None),
            P(("grp", "tile"), None),
            P(("grp", "tile"), None),
            P(("grp", "tile"), None, None),
            P(("grp", "tile"), None, None),
        ),
        out_specs=(P("tile", None, None, None), P("tile", None, None, None)),
        check_vma=False,
    )
```

```python
import functools
import math

import jax
import jax.numpy as jnp
from jax import lax
from jax.experimental import pallas as pl
from jax.experimental.pallas import tpu as pltpu
from jax.sharding import PartitionSpec as P

COEF = (1225.0 / 1024.0, -245.0 / 3072.0, 49.0 / 5120.0, -5.0 / 7168.0)
REACH = 4
EDGE = 8
ROWS = 8
SPAN = 8

SMEM = pl.BlockSpec(memory_space=pltpu.SMEM)
VMEM = pl.BlockSpec(memory_space=pltpu.VMEM)
PARAMS = pltpu.CompilerParams(vmem_limit_bytes=36 * 1024 * 1024)


def entry_of(list_ref):
    return jnp.max(list_ref[0:1, 0:1].astype(jnp.float32)).astype(jnp.int32)


def combine(ahead, behind):
    total = None
    for order in range(1, 5):
        upper, lower = ahead(order), behind(order)
        if upper is None and lower is None:
            continue
        if lower is None:
            term = upper
        elif upper is None:
            term = -lower
        else:
            term = upper - lower
        if order > 1:
            term = (COEF[order - 1] / COEF[0]) * term
        total = term if total is None else total + term
    return total


def band(first, depth):
    source = lax.broadcasted_iota(jnp.int32, (depth, depth), 0)
    target = lax.broadcasted_iota(jnp.int32, (depth, depth), 1)
    total = jnp.zeros((depth, depth), jnp.float32)
    for order in range(1, 5):
        weight = COEF[order - 1] / COEF[0]
        total = total + jnp.where(source == target + (first + order - 1), weight, 0.0)
        total = total - jnp.where(source == target + (first - order), weight, 0.0)
    return jnp.concatenate(halves(total), axis=1)


def halves(values):
    high = values.astype(jnp.bfloat16)
    return high, (values - high.astype(jnp.float32)).astype(jnp.bfloat16)


def along_z(values, matrix):
    xs, ys, zs = values.shape
    pair = jnp.concatenate(halves(values.reshape(xs * ys, zs)), axis=1)
    parts = jnp.dot(pair, matrix, preferred_element_type=jnp.float32)
    return (parts[:, :zs] + parts[:, zs:]).reshape(xs, ys, zs)


def blocks(xs, ys, body):
    if xs <= SPAN:
        for y0 in range(0, ys, ROWS):
            body(0, xs, y0)
        return

    def span(index, _):
        for y0 in range(0, ys, ROWS):
            body(index * SPAN, SPAN, y0)
        return 0

    lax.fori_loop(0, xs // SPAN, span, 0)


def window(xs, x0, load):
    kept = {}

    def at(offset):
        if xs <= SPAN and not 0 <= offset < xs:
            return None
        if offset not in kept:
            kept[offset] = load(x0 + offset)
        return kept[offset]

    return at


def slopes(xs, p, x0, y0, plane, offset):
    centre = plane(offset)
    here = x0 + offset + REACH
    return (
        combine(lambda k: plane(offset + k), lambda k: plane(offset + 1 - k)),
        combine(
            lambda k: p[here, pl.ds(EDGE + y0 + k, ROWS)],
            lambda k: centre if k == 1 else p[here, pl.ds(EDGE + y0 + 1 - k, ROWS)],
        ),
    )


def prepare_kernel(
    steps, fwd, adj, src, wave, rec, res, _piece,
    fwd_slope, adj_slope, fwd_source, adj_source, ahead, behind, *fields,
):
    xs, ys, zs = fwd_slope.shape[1:]
    for ref, first in ((ahead, 1), (behind, 0)):
        one = band(first, zs)
        ref[:zs] = one
        ref[zs:] = one

    def clear(ref):
        ref[...] = jnp.zeros(ref.shape, jnp.float32)

    for state, (p, v0, v1, v2), slope in (
        (fwd, fields[:4], fwd_slope),
        (adj, fields[4:], adj_slope),
    ):
        for ref in (p, v0):
            clear(ref.at[:REACH])
            clear(ref.at[REACH + xs :])
        for ref in (p.at[pl.ds(REACH, xs)], v1):
            clear(ref.at[:, :EDGE])
            clear(ref.at[:, EDGE + ys :])
        for x in range(xs):
            p[REACH + x, EDGE : EDGE + ys] = state[0, 0, x].astype(jnp.float32)
            v0[REACH + x] = state[0, 1, x].astype(jnp.float32)
            v1[x, EDGE : EDGE + ys] = state[0, 2, x].astype(jnp.float32)
            v2[x] = state[0, 3, x].astype(jnp.float32)

        def block(x0, count, y0, p=p, slope=slope):
            plane = window(xs, x0, lambda x: p[REACH + x, pl.ds(EDGE + y0, ROWS)])
            for offset in range(count):
                for d, values in enumerate(slopes(xs, p, x0, y0, plane, offset)):
                    slope[d, x0 + offset, pl.ds(y0, ROWS)] = values

        blocks(xs, ys, block)
        slope[2] = along_z(p[REACH : REACH + xs, EDGE : EDGE + ys], ahead[...])

    row = lax.broadcasted_iota(jnp.int32, (ys, zs), 0)
    lane = lax.broadcasted_iota(jnp.int32, (ys, zs), 1)
    src_mark = (row == src[0, 1]) & (lane == src[0, 2])
    for x in range(xs):
        rec_mark = (row == rec[0, 0, x]) & (lane == rec[0, 1, x])
        for step in range(steps):
            amplitude = jnp.where(x == src[0, 0], wave[0, step], 0.0)
            fwd_source[step, x] = jnp.where(src_mark, amplitude, 0.0)
            adj_source[step, x] = jnp.where(rec_mark, res[0, step, x], 0.0)


def near_kernel(speed, density, aperture, near_speed, near_density, entry):
    near_speed[...] = speed[...]
    near_density[...] = density[...]
    entry[...] = jnp.full(entry.shape, entry_of(aperture), jnp.int32)


def pick_kernel(chips, near_speed, near_density, far_speed, far_density, *refs):
    stripes = 2 * chips
    lists, outs = refs[:stripes], refs[stripes:]
    held = near_speed.shape[0]
    me = lax.axis_index("tile")
    residue, half = lax.rem(me, stripes), lax.div(me, stripes)
    for hop in range(stripes):
        entry = entry_of(lists[hop])
        corner, column = lax.div(entry, held), lax.rem(entry, held)
        here = (residue >= corner) == (half == 0)
        piece = outs[hop]

        @pl.when(here)
        def _():
            piece[0] = near_speed[column]
            piece[1] = near_density[column]

        @pl.when(jnp.logical_not(here))
        def _():
            piece[0] = far_speed[column]
            piece[1] = far_density[column]


def wave_kernel(chips, steps, held, *refs):
    stripes = 2 * chips
    pieces, refs = refs[:stripes], refs[stripes:]
    fwd_slope, adj_slope, fwd_source, adj_source, ahead, behind, entry_ref = refs[:7]
    kept, traded, p, v0, v1, v2, q, w0, w1, w2 = refs[15:25]
    bulk, buoy, dp, dv, bulk_img, buoy_img, across_z, flat = refs[25:]
    tile_x, tile_y = pieces[0].shape[1:3]
    xs, ys, zs = bulk.shape
    residue = lax.rem(lax.axis_index("tile"), stripes)
    entry = entry_of(entry_ref)
    corner = lax.div(entry, held)

    def place_of(hop):
        return lax.rem((residue ^ hop) - corner + stripes, stripes) * tile_x

    for hop in range(stripes):
        cells = pl.ds(place_of(hop), tile_x)
        speed, density = pieces[hop][0], pieces[hop][1]
        bulk[cells] = COEF[0] * (density * speed * speed)
        buoy[cells] = COEF[0] / density

    def push(fields, first, note):
        p, v0, v1, v2 = fields
        if first is None:
            across_z[...] = along_z(p[REACH : REACH + xs, EDGE : EDGE + ys], ahead[...])

        def block(x0, count, y0):
            rows, inner = pl.ds(y0, ROWS), pl.ds(EDGE + y0, ROWS)
            plane = window(xs, x0, lambda x: p[REACH + x, inner])
            for offset in range(count):
                x = x0 + offset
                if first is None:
                    two = slopes(xs, p, x0, y0, plane, offset)
                else:
                    two = (first[0, x, rows], first[1, x, rows])
                light = buoy[x, rows]
                changes = (light * two[0], light * two[1])
                moved = (v0[REACH + x, rows] + changes[0], v1[x, inner] + changes[1])
                v0[REACH + x, rows] = moved[0]
                v1[x, inner] = moved[1]
                note(0, x, rows, changes, moved)

        def block_z(x0, count, y0):
            rows = pl.ds(y0, ROWS)
            for x in range(count):
                x = x0 + x
                slope = across_z[x, rows] if first is None else first[2, x, rows]
                change = buoy[x, rows] * slope
                moved = v2[x, rows] + change
                v2[x, rows] = moved
                note(2, x, rows, (change,), (moved,))

        blocks(xs, ys, block)
        blocks(xs, ys, block_z)

    def spread(fields, source, step, note):
        p, v0, v1, v2 = fields
        across_z[...] = along_z(v2[...], behind[...])

        def block(x0, count, y0):
            rows = pl.ds(y0, ROWS)
            plane = window(xs, x0, lambda x: v0[REACH + x, rows])
            for offset in range(count):
                x = x0 + offset
                along_x = combine(lambda k: plane(offset + k - 1), lambda k: plane(offset - k))
                along_y = combine(
                    lambda k: v1[x, pl.ds(EDGE + y0 + k - 1, ROWS)],
                    lambda k: v1[x, pl.ds(EDGE + y0 - k, ROWS)],
                )
                flat[x, rows] = along_x + along_y

        def block_z(x0, count, y0):
            rows, inner = pl.ds(y0, ROWS), pl.ds(EDGE + y0, ROWS)
            for x in range(count):
                x = x0 + x
                change = bulk[x, rows] * (flat[x, rows] + across_z[x, rows])
                change = change + source[step, x, rows]
                moved = p[REACH + x, inner] + change
                p[REACH + x, inner] = moved
                note(x, rows, change, moved)

        blocks(xs, ys, block)
        blocks(xs, ys, block_z)

    fields = (p, v0, v1, v2)
    for step in range(steps):

        def keep_dv(first, x, rows, changes, moved, step=step):
            for d, change in enumerate(changes, first):
                dv[step, d, x, rows] = change

        def keep_dp(x, rows, change, moved, step=step):
            dp[step, x, rows] = change

        push(fields, fwd_slope if step == 0 else None, keep_dv)
        spread(fields, fwd_source, step, keep_dp)

    fields = (q, w0, w1, w2)
    for step in reversed(range(steps)):
        last = step == steps - 1

        def add_buoy(first, x, rows, changes, moved, step=step, last=last):
            image = None if last and first == 0 else buoy_img[x, rows]
            for d, values in enumerate(moved, first):
                product = dv[step, d, x, rows] * values
                image = product if image is None else image + product
            buoy_img[x, rows] = image

        def add_bulk(x, rows, change, moved, step=step, last=last):
            image = dp[step, x, rows] * moved
            bulk_img[x, rows] = image if last else bulk_img[x, rows] + image

        push(fields, adj_slope if last else None, add_buoy)
        spread(fields, adj_source, step, add_bulk)

    tile_rows = tile_x * tile_y
    for chip in range(chips):
        for ref, hop in ((kept, 2 * chip), (traded, 2 * chip + 1)):
            cells = pl.ds(place_of(hop), tile_x)
            ref[chip, :tile_rows] = bulk_img[cells].reshape(tile_rows, zs)
            ref[chip, tile_rows : 2 * tile_rows] = buoy_img[cells].reshape(tile_rows, zs)
            ref[chip, 2 * tile_rows :] = jnp.full((8, zs), entry).astype(jnp.float32)


def return_order(chips):
    even = [chips] + list(range(1, chips)) + list(range(chips + 1, 2 * chips))
    return list(zip(even, reversed(even)))


def merge_kernel(chips, kept, came, *outs):
    rows = kept.shape[1] - 8
    odd = lax.rem(lax.axis_index("tile"), 2) == 1
    for out, (even_hop, odd_hop) in zip(outs, [(0, 0)] + return_order(chips)):
        chip = jnp.where(odd, odd_hop % chips, even_hop % chips)
        for shot, source in enumerate((kept, came)):
            out[shot * rows : (shot + 1) * rows] = source[chip, :rows]
            first = 2 * rows + 4 * shot
            out[first : first + 4] = source[chip, rows : rows + 4]


def add_kernel(chips, groups, held, *refs):
    came, parts, total = refs[: 2 * chips], refs[2 * chips : 2 * chips + groups], refs[-1]
    stripes = 2 * chips
    me, group = lax.axis_index("tile"), lax.axis_index("grp")
    tile_rows = total.shape[1] // (held + 1)
    part = parts[0].shape[1]
    total[...] = jnp.zeros_like(total)
    for pair in came:
        for shot in range(2):
            first = 4 * tile_rows + 4 * shot
            entry = jnp.max(pair[first : first + 4]).astype(jnp.int32)
            corner, column = lax.div(entry, held), lax.rem(entry, held)
            mine = (corner <= me) & (me < corner + stripes)
            slot = jnp.where(mine, column, held)
            rows = pl.ds(pl.multiple_of(slot * tile_rows, tile_rows), tile_rows)
            for field in range(2):
                first = (2 * shot + field) * tile_rows
                total[field, rows] = total[field, rows] + pair[first : first + tile_rows]
    for index, hop in enumerate([0] + far_first(groups)):
        first = pl.multiple_of((group ^ hop) * part, part)
        for field in range(2):
            parts[index][field] = total[field, pl.ds(first, part)]


def far_first(groups):
    return list(range(groups - 1, 0, -1))


def grads_kernel(scale, groups, *refs):
    parts, speed_ref, density_ref, grads = refs[:groups], *refs[groups:]
    part = parts[0].shape[1]
    rows = pl.ds(pl.multiple_of(lax.axis_index("grp") * part, part), part)
    speed, density = speed_ref[rows], density_ref[rows]
    bulk_sum, buoy_sum = parts[0][0], parts[0][1]
    for other in parts[1:]:
        bulk_sum = bulk_sum + other[0]
        buoy_sum = buoy_sum + other[1]
    grads[0] = scale * (bulk_sum * (2.0 * density * speed))
    grads[1] = scale * (bulk_sum * (speed * speed) - buoy_sum / (density * density))


def per_device(speed, density, fwd_state, adj_state, aperture, src_pos, wavelet, rec_pos, residual):
    owners = lax.axis_size("tile")
    groups = lax.axis_size("grp")
    my_group = lax.axis_index("grp")
    held, tile_x, tile_y, depth = speed.shape
    stripes = aperture.shape[1]
    chips = stripes // 2
    steps = wavelet.shape[1]
    xs = stripes * tile_x
    f32 = jnp.float32
    cells = (xs, tile_y, depth)

    def shape(*dims):
        return jax.ShapeDtypeStruct(dims, f32)

    def across(values, hop):
        return lax.ppermute(values, "tile", [(t, t ^ hop) for t in range(owners)])

    far_speed = across(speed, stripes)
    far_density = across(density, stripes)
    lists = {hop: across(aperture, hop) for hop in range(stripes - 1, 0, -1)}
    four = [
        (xs + 2 * REACH, tile_y + 2 * EDGE, depth),
        (xs + 2 * REACH, tile_y, depth),
        (xs, tile_y + 2 * EDGE, depth),
        cells,
    ]
    near_speed, near_density, entry = pl.pallas_call(
        near_kernel,
        out_shape=[
            shape(*speed.shape),
            shape(*speed.shape),
            jax.ShapeDtypeStruct((8, depth), jnp.int32),
        ],
        in_specs=[VMEM] * 3,
        out_specs=[VMEM] * 3,
        compiler_params=PARAMS,
        cost_estimate=pl.CostEstimate(flops=4_000_000, bytes_accessed=6_000_000, transcendentals=0),
        name="hold_near_tiles",
    )(speed, density, aperture)
    pieces = pl.pallas_call(
        functools.partial(pick_kernel, chips),
        out_shape=[shape(2, tile_x, tile_y, depth)] * stripes,
        in_specs=[VMEM] * (4 + stripes),
        out_specs=[VMEM] * stripes,
        compiler_params=PARAMS,
        name="pick_tiles",
    )(near_speed, near_density, far_speed, far_density, entry, *[lists[h] for h in range(1, stripes)])
    moved = {hop: across(pieces[hop], hop) for hop in range(stripes - 1, 0, -1)}

    prepared = pl.pallas_call(
        functools.partial(prepare_kernel, steps),
        out_shape=[shape(3, *cells)] * 2
        + [shape(steps, *cells)] * 2
        + [jax.ShapeDtypeStruct((2 * depth, 2 * depth), jnp.bfloat16)] * 2
        + [shape(*dims) for dims in four + four],
        in_specs=[VMEM] * 2 + [SMEM] * 4 + [VMEM],
        out_specs=[VMEM] * 14,
        compiler_params=PARAMS,
        cost_estimate=pl.CostEstimate(flops=4_000_000, bytes_accessed=6_000_000, transcendentals=0),
        name="prepare",
    )(fwd_state, adj_state, src_pos, wavelet, jnp.swapaxes(rec_pos, 1, 2), residual, pieces[0])
    prepared, fields = prepared[:6], prepared[6:]
    pieces = [pieces[0]] + [moved[hop] for hop in range(1, stripes)]

    tile_rows = tile_x * tile_y
    sent = shape(chips, 2 * tile_rows + 8, depth)
    kept, traded, *_ = pl.pallas_call(
        functools.partial(wave_kernel, chips, steps, held),
        out_shape=[sent, sent] + [shape(*dims) for dims in four + four],
        in_specs=[VMEM] * (stripes + 15),
        out_specs=[VMEM] * 10,
        scratch_shapes=[
            pltpu.VMEM(cells, f32),
            pltpu.VMEM(cells, f32),
            pltpu.VMEM((steps,) + cells, f32),
            pltpu.VMEM((steps, 3) + cells, f32),
        ]
        + [pltpu.VMEM(cells, f32)] * 4
        + [
        ],
        input_output_aliases={stripes + 7 + index: 2 + index for index in range(8)},
        compiler_params=PARAMS,
        name="replay_and_adjoint",
    )(*pieces, *prepared, entry, *fields)

    both = shape(4 * tile_rows + 8, depth)
    stacks = pl.pallas_call(
        functools.partial(merge_kernel, chips),
        out_shape=[both] * stripes,
        in_specs=[VMEM] * 2,
        out_specs=[VMEM] * stripes,
        compiler_params=PARAMS,
        name="merge_pair",
    )(kept, across(traded, 1))
    came = [
        lax.ppermute(values, "tile", [(t, t ^ (2 * hops[t % 2])) for t in range(owners)])
        for values, hops in zip(stacks[1:], return_order(chips))
    ]
    came = came[-1:] + came[:-1]

    rows = held * tile_rows
    part = rows // groups
    part_shape = shape(2, part, depth)
    parts = pl.pallas_call(
        functools.partial(add_kernel, chips, groups, held),
        out_shape=[part_shape] * groups,
        in_specs=[VMEM] * stripes,
        out_specs=[VMEM] * groups,
        scratch_shapes=[pltpu.VMEM((2, rows + tile_rows, depth), f32)],
        compiler_params=PARAMS,
        name="add_stripes",
    )(stacks[0], *came)

    def along(values, hop):
        return lax.ppermute(values, "grp", [(g, g ^ hop) for g in range(groups)])

    parts = [parts[0]] + [along(values, hop) for values, hop in zip(parts[1:], far_first(groups))]
    grads = pl.pallas_call(
        functools.partial(grads_kernel, 1.0 / math.sqrt(groups * owners), groups),
        out_shape=part_shape,
        in_specs=[VMEM] * (groups + 2),
        out_specs=VMEM,
        compiler_params=PARAMS,
        name="gradients",
    )(*parts, near_speed.reshape(rows, depth), near_density.reshape(rows, depth))

    whole = jnp.zeros((2, groups, part, depth), f32)
    for hop in range(groups):
        values = grads
        if hop:
            values = lax.ppermute(grads, "grp", [(g, (g + hop) % groups) for g in range(groups)])
        place = lax.rem(my_group - hop + groups, groups)
        whole = lax.dynamic_update_slice_in_dim(whole, values[:, None], place, axis=1)
    return (whole[0].reshape(speed.shape), whole[1].reshape(speed.shape))


def solution(mesh):
    return jax.shard_map(
        per_device,
        mesh=mesh,
        in_specs=(
            P("tile", None, None, None),
            P("tile", None, None, None),
            P(("grp", "tile"), None, None, None, None),
            P(("grp", "tile"), None, None, None, None),
            P(("grp", "tile"), None),
            P(("grp", "tile"), None),
            P(("grp", "tile"), None),
            P(("grp", "tile"), None, None),
            P(("grp", "tile"), None, None),
        ),
        out_specs=(P("tile", None, None, None), P("tile", None, None, None)),
        check_vma=False,
    )
```

```python
import functools
import math

import jax
import jax.numpy as jnp
from jax import lax
from jax.experimental import pallas as pl
from jax.experimental.pallas import tpu as pltpu
from jax.sharding import PartitionSpec as P

COEF = (1225.0 / 1024.0, -245.0 / 3072.0, 49.0 / 5120.0, -5.0 / 7168.0)
REACH = 4
EDGE = 8
ROWS = 8
SPAN = 8

SMEM = pl.BlockSpec(memory_space=pltpu.SMEM)
VMEM = pl.BlockSpec(memory_space=pltpu.VMEM)
PARAMS = pltpu.CompilerParams(vmem_limit_bytes=36 * 1024 * 1024)


def entry_of(list_ref):
    return jnp.max(list_ref[0:1, 0:1].astype(jnp.float32)).astype(jnp.int32)


def combine(ahead, behind):
    total = None
    for order in range(1, 5):
        upper, lower = ahead(order), behind(order)
        if upper is None and lower is None:
            continue
        if lower is None:
            term = upper
        elif upper is None:
            term = -lower
        else:
            term = upper - lower
        if order > 1:
            term = (COEF[order - 1] / COEF[0]) * term
        total = term if total is None else total + term
    return total


def band(first, depth):
    source = lax.broadcasted_iota(jnp.int32, (depth, depth), 0)
    target = lax.broadcasted_iota(jnp.int32, (depth, depth), 1)
    total = jnp.zeros((depth, depth), jnp.float32)
    for order in range(1, 5):
        weight = COEF[order - 1] / COEF[0]
        total = total + jnp.where(source == target + (first + order - 1), weight, 0.0)
        total = total - jnp.where(source == target + (first - order), weight, 0.0)
    return jnp.concatenate(halves(total), axis=1)


def halves(values):
    high = values.astype(jnp.bfloat16)
    return high, (values - high.astype(jnp.float32)).astype(jnp.bfloat16)


def along_z(values, matrix):
    xs, ys, zs = values.shape
    pair = jnp.concatenate(halves(values.reshape(xs * ys, zs)), axis=1)
    parts = jnp.dot(pair, matrix, preferred_element_type=jnp.float32)
    return (parts[:, :zs] + parts[:, zs:]).reshape(xs, ys, zs)


def blocks(xs, ys, body):
    if xs <= SPAN:
        for y0 in range(0, ys, ROWS):
            body(0, xs, y0)
        return

    def span(index, _):
        for y0 in range(0, ys, ROWS):
            body(index * SPAN, SPAN, y0)
        return 0

    lax.fori_loop(0, xs // SPAN, span, 0)


def window(xs, x0, load):
    kept = {}

    def at(offset):
        if xs <= SPAN and not 0 <= offset < xs:
            return None
        if offset not in kept:
            kept[offset] = load(x0 + offset)
        return kept[offset]

    return at


def slopes(xs, p, x0, y0, plane, offset):
    centre = plane(offset)
    here = x0 + offset + REACH
    return (
        combine(lambda k: plane(offset + k), lambda k: plane(offset + 1 - k)),
        combine(
            lambda k: p[here, pl.ds(EDGE + y0 + k, ROWS)],
            lambda k: centre if k == 1 else p[here, pl.ds(EDGE + y0 + 1 - k, ROWS)],
        ),
    )


def prepare_kernel(
    steps, fwd, adj, src, wave, rec, res, _piece,
    fwd_slope, adj_slope, fwd_source, adj_source, ahead, behind, *fields,
):
    xs, ys, zs = fwd_slope.shape[1:]
    for ref, first in ((ahead, 1), (behind, 0)):
        one = band(first, zs)
        ref[:zs] = one
        ref[zs:] = one

    def clear(ref):
        ref[...] = jnp.zeros(ref.shape, jnp.float32)

    for state, (p, v0, v1, v2), slope in (
        (fwd, fields[:4], fwd_slope),
        (adj, fields[4:], adj_slope),
    ):
        for ref in (p, v0):
            clear(ref.at[:REACH])
            clear(ref.at[REACH + xs :])
        for ref in (p.at[pl.ds(REACH, xs)], v1):
            clear(ref.at[:, :EDGE])
            clear(ref.at[:, EDGE + ys :])
        for x in range(xs):
            p[REACH + x, EDGE : EDGE + ys] = state[0, 0, x].astype(jnp.float32)
            v0[REACH + x] = state[0, 1, x].astype(jnp.float32)
            v1[x, EDGE : EDGE + ys] = state[0, 2, x].astype(jnp.float32)
            v2[x] = state[0, 3, x].astype(jnp.float32)

        def block(x0, count, y0, p=p, slope=slope):
            plane = window(xs, x0, lambda x: p[REACH + x, pl.ds(EDGE + y0, ROWS)])
            for offset in range(count):
                for d, values in enumerate(slopes(xs, p, x0, y0, plane, offset)):
                    slope[d, x0 + offset, pl.ds(y0, ROWS)] = values

        blocks(xs, ys, block)
        slope[2] = along_z(p[REACH : REACH + xs, EDGE : EDGE + ys], ahead[...])

    row = lax.broadcasted_iota(jnp.int32, (ys, zs), 0)
    lane = lax.broadcasted_iota(jnp.int32, (ys, zs), 1)
    src_mark = (row == src[0, 1]) & (lane == src[0, 2])
    for x in range(xs):
        rec_mark = (row == rec[0, 0, x]) & (lane == rec[0, 1, x])
        for step in range(steps):
            amplitude = jnp.where(x == src[0, 0], wave[0, step], 0.0)
            fwd_source[step, x] = jnp.where(src_mark, amplitude, 0.0)
            adj_source[step, x] = jnp.where(rec_mark, res[0, step, x], 0.0)


def near_kernel(speed, density, aperture, near_speed, near_density, entry):
    near_speed[...] = speed[...]
    near_density[...] = density[...]
    entry[...] = jnp.full(entry.shape, entry_of(aperture), jnp.int32)


def pick_kernel(chips, near_speed, near_density, far_speed, far_density, *refs):
    stripes = 2 * chips
    lists, outs = refs[:stripes], refs[stripes:]
    held = near_speed.shape[0]
    me = lax.axis_index("tile")
    residue, half = lax.rem(me, stripes), lax.div(me, stripes)
    for hop in range(stripes):
        entry = entry_of(lists[hop])
        corner, column = lax.div(entry, held), lax.rem(entry, held)
        here = (residue >= corner) == (half == 0)
        piece = outs[hop]

        @pl.when(here)
        def _():
            piece[0] = near_speed[column]
            piece[1] = near_density[column]

        @pl.when(jnp.logical_not(here))
        def _():
            piece[0] = far_speed[column]
            piece[1] = far_density[column]


def wave_kernel(chips, steps, held, *refs):
    stripes = 2 * chips
    pieces, refs = refs[:stripes], refs[stripes:]
    fwd_slope, adj_slope, fwd_source, adj_source, ahead, behind, entry_ref = refs[:7]
    kept, traded, p, v0, v1, v2, q, w0, w1, w2 = refs[15:25]
    bulk, buoy, dp, dv, bulk_img, buoy_img, across_z, flat = refs[25:]
    tile_x, tile_y = pieces[0].shape[1:3]
    xs, ys, zs = bulk.shape
    residue = lax.rem(lax.axis_index("tile"), stripes)
    entry = entry_of(entry_ref)
    corner = lax.div(entry, held)

    def place_of(hop):
        return lax.rem((residue ^ hop) - corner + stripes, stripes) * tile_x

    for hop in range(stripes):
        cells = pl.ds(place_of(hop), tile_x)
        speed, density = pieces[hop][0], pieces[hop][1]
        bulk[cells] = COEF[0] * (density * speed * speed)
        buoy[cells] = COEF[0] / density

    def push(fields, first, note):
        p, v0, v1, v2 = fields
        if first is None:
            across_z[...] = along_z(p[REACH : REACH + xs, EDGE : EDGE + ys], ahead[...])

        def block(x0, count, y0):
            rows, inner = pl.ds(y0, ROWS), pl.ds(EDGE + y0, ROWS)
            plane = window(xs, x0, lambda x: p[REACH + x, inner])
            for offset in range(count):
                x = x0 + offset
                if first is None:
                    two = slopes(xs, p, x0, y0, plane, offset)
                else:
                    two = (first[0, x, rows], first[1, x, rows])
                light = buoy[x, rows]
                changes = (light * two[0], light * two[1])
                moved = (v0[REACH + x, rows] + changes[0], v1[x, inner] + changes[1])
                v0[REACH + x, rows] = moved[0]
                v1[x, inner] = moved[1]
                note(0, x, rows, changes, moved)

        def block_z(x0, count, y0):
            rows = pl.ds(y0, ROWS)
            for x in range(count):
                x = x0 + x
                slope = across_z[x, rows] if first is None else first[2, x, rows]
                change = buoy[x, rows] * slope
                moved = v2[x, rows] + change
                v2[x, rows] = moved
                note(2, x, rows, (change,), (moved,))

        blocks(xs, ys, block)
        blocks(xs, ys, block_z)

    def spread(fields, source, step, note):
        p, v0, v1, v2 = fields
        across_z[...] = along_z(v2[...], behind[...])

        def block(x0, count, y0):
            rows = pl.ds(y0, ROWS)
            plane = window(xs, x0, lambda x: v0[REACH + x, rows])
            for offset in range(count):
                x = x0 + offset
                along_x = combine(lambda k: plane(offset + k - 1), lambda k: plane(offset - k))
                along_y = combine(
                    lambda k: v1[x, pl.ds(EDGE + y0 + k - 1, ROWS)],
                    lambda k: v1[x, pl.ds(EDGE + y0 - k, ROWS)],
                )
                flat[x, rows] = along_x + along_y

        def block_z(x0, count, y0):
            rows, inner = pl.ds(y0, ROWS), pl.ds(EDGE + y0, ROWS)
            for x in range(count):
                x = x0 + x
                change = bulk[x, rows] * (flat[x, rows] + across_z[x, rows])
                change = change + source[step, x, rows]
                moved = p[REACH + x, inner] + change
                p[REACH + x, inner] = moved
                note(x, rows, change, moved)

        blocks(xs, ys, block)
        blocks(xs, ys, block_z)

    fields = (p, v0, v1, v2)
    for step in range(steps):

        def keep_dv(first, x, rows, changes, moved, step=step):
            for d, change in enumerate(changes, first):
                dv[step, d, x, rows] = change

        def keep_dp(x, rows, change, moved, step=step):
            dp[step, x, rows] = change

        push(fields, fwd_slope if step == 0 else None, keep_dv)
        spread(fields, fwd_source, step, keep_dp)

    fields = (q, w0, w1, w2)
    for step in reversed(range(steps)):
        last = step == steps - 1

        def add_buoy(first, x, rows, changes, moved, step=step, last=last):
            image = None if last and first == 0 else buoy_img[x, rows]
            for d, values in enumerate(moved, first):
                product = dv[step, d, x, rows] * values
                image = product if image is None else image + product
            buoy_img[x, rows] = image

        def add_bulk(x, rows, change, moved, step=step, last=last):
            image = dp[step, x, rows] * moved
            bulk_img[x, rows] = image if last else bulk_img[x, rows] + image

        push(fields, adj_slope if last else None, add_buoy)
        spread(fields, adj_source, step, add_bulk)

    tile_rows = tile_x * tile_y
    for chip in range(chips):
        for ref, hop in ((kept, 2 * chip), (traded, 2 * chip + 1)):
            cells = pl.ds(place_of(hop), tile_x)
            ref[chip, :tile_rows] = bulk_img[cells].reshape(tile_rows, zs)
            ref[chip, tile_rows : 2 * tile_rows] = buoy_img[cells].reshape(tile_rows, zs)
            ref[chip, 2 * tile_rows :] = jnp.full((8, zs), entry).astype(jnp.float32)


def return_order(chips):
    even = [chips] + list(range(1, chips)) + list(range(chips + 1, 2 * chips))
    return list(zip(even, reversed(even)))


def merge_kernel(chips, kept, came, *outs):
    rows = kept.shape[1] - 8
    odd = lax.rem(lax.axis_index("tile"), 2) == 1
    for out, (even_hop, odd_hop) in zip(outs, [(0, 0)] + return_order(chips)):
        chip = jnp.where(odd, odd_hop % chips, even_hop % chips)
        for shot, source in enumerate((kept, came)):
            out[shot * rows : (shot + 1) * rows] = source[chip, :rows]
            first = 2 * rows + 4 * shot
            out[first : first + 4] = source[chip, rows : rows + 4]


def add_kernel(chips, groups, held, *refs):
    came, parts, total = refs[: 2 * chips], refs[-2], refs[-1]
    stripes = 2 * chips
    me = lax.axis_index("tile")
    tile_rows = total.shape[1] // (held + 1)
    total[...] = jnp.zeros_like(total)
    for pair in came:
        for shot in range(2):
            first = 4 * tile_rows + 4 * shot
            entry = jnp.max(pair[first : first + 4]).astype(jnp.int32)
            corner, column = lax.div(entry, held), lax.rem(entry, held)
            mine = (corner <= me) & (me < corner + stripes)
            slot = jnp.where(mine, column, held)
            rows = pl.ds(pl.multiple_of(slot * tile_rows, tile_rows), tile_rows)
            for field in range(2):
                first = (2 * shot + field) * tile_rows
                total[field, rows] = total[field, rows] + pair[first : first + tile_rows]
    part = parts.shape[2]
    for group in range(groups):
        for field in range(2):
            parts[group, field] = total[field, group * part : (group + 1) * part]


def grads_kernel(scale, groups, parts, speed_ref, density_ref, grads):
    part = parts.shape[2]
    rows = pl.ds(pl.multiple_of(lax.axis_index("grp") * part, part), part)
    speed, density = speed_ref[rows], density_ref[rows]
    bulk_sum, buoy_sum = parts[0, 0], parts[0, 1]
    for group in range(1, groups):
        bulk_sum = bulk_sum + parts[group, 0]
        buoy_sum = buoy_sum + parts[group, 1]
    grad_speed = scale * (bulk_sum * (2.0 * density * speed))
    grad_density = scale * (bulk_sum * (speed * speed) - buoy_sum / (density * density))
    for group in range(groups):
        grads[group, 0] = grad_speed
        grads[group, 1] = grad_density


def per_device(speed, density, fwd_state, adj_state, aperture, src_pos, wavelet, rec_pos, residual):
    owners = lax.axis_size("tile")
    groups = lax.axis_size("grp")
    held, tile_x, tile_y, depth = speed.shape
    stripes = aperture.shape[1]
    chips = stripes // 2
    steps = wavelet.shape[1]
    xs = stripes * tile_x
    f32 = jnp.float32
    cells = (xs, tile_y, depth)

    def shape(*dims):
        return jax.ShapeDtypeStruct(dims, f32)

    def across(values, hop):
        return lax.ppermute(values, "tile", [(t, t ^ hop) for t in range(owners)])

    far_speed = across(speed, stripes)
    far_density = across(density, stripes)
    lists = {hop: across(aperture, hop) for hop in range(stripes - 1, 0, -1)}
    four = [
        (xs + 2 * REACH, tile_y + 2 * EDGE, depth),
        (xs + 2 * REACH, tile_y, depth),
        (xs, tile_y + 2 * EDGE, depth),
        cells,
    ]
    near_speed, near_density, entry = pl.pallas_call(
        near_kernel,
        out_shape=[
            shape(*speed.shape),
            shape(*speed.shape),
            jax.ShapeDtypeStruct((8, depth), jnp.int32),
        ],
        in_specs=[VMEM] * 3,
        out_specs=[VMEM] * 3,
        compiler_params=PARAMS,
        cost_estimate=pl.CostEstimate(flops=4_000_000, bytes_accessed=6_000_000, transcendentals=0),
        name="hold_near_tiles",
    )(speed, density, aperture)
    pieces = pl.pallas_call(
        functools.partial(pick_kernel, chips),
        out_shape=[shape(2, tile_x, tile_y, depth)] * stripes,
        in_specs=[VMEM] * (4 + stripes),
        out_specs=[VMEM] * stripes,
        compiler_params=PARAMS,
        name="pick_tiles",
    )(near_speed, near_density, far_speed, far_density, entry, *[lists[h] for h in range(1, stripes)])
    moved = {hop: across(pieces[hop], hop) for hop in range(stripes - 1, 0, -1)}

    prepared = pl.pallas_call(
        functools.partial(prepare_kernel, steps),
        out_shape=[shape(3, *cells)] * 2
        + [shape(steps, *cells)] * 2
        + [jax.ShapeDtypeStruct((2 * depth, 2 * depth), jnp.bfloat16)] * 2
        + [shape(*dims) for dims in four + four],
        in_specs=[VMEM] * 2 + [SMEM] * 4 + [VMEM],
        out_specs=[VMEM] * 14,
        compiler_params=PARAMS,
        cost_estimate=pl.CostEstimate(flops=4_000_000, bytes_accessed=6_000_000, transcendentals=0),
        name="prepare",
    )(fwd_state, adj_state, src_pos, wavelet, jnp.swapaxes(rec_pos, 1, 2), residual, pieces[0])
    prepared, fields = prepared[:6], prepared[6:]
    pieces = [pieces[0]] + [moved[hop] for hop in range(1, stripes)]

    tile_rows = tile_x * tile_y
    sent = shape(chips, 2 * tile_rows + 8, depth)
    kept, traded, *_ = pl.pallas_call(
        functools.partial(wave_kernel, chips, steps, held),
        out_shape=[sent, sent] + [shape(*dims) for dims in four + four],
        in_specs=[VMEM] * (stripes + 15),
        out_specs=[VMEM] * 10,
        scratch_shapes=[
            pltpu.VMEM(cells, f32),
            pltpu.VMEM(cells, f32),
            pltpu.VMEM((steps,) + cells, f32),
            pltpu.VMEM((steps, 3) + cells, f32),
        ]
        + [pltpu.VMEM(cells, f32)] * 4
        + [
        ],
        input_output_aliases={stripes + 7 + index: 2 + index for index in range(8)},
        compiler_params=PARAMS,
        name="replay_and_adjoint",
    )(*pieces, *prepared, entry, *fields)

    both = shape(4 * tile_rows + 8, depth)
    stacks = pl.pallas_call(
        functools.partial(merge_kernel, chips),
        out_shape=[both] * stripes,
        in_specs=[VMEM] * 2,
        out_specs=[VMEM] * stripes,
        compiler_params=PARAMS,
        name="merge_pair",
    )(kept, across(traded, 1))
    came = [
        lax.ppermute(values, "tile", [(t, t ^ (2 * hops[t % 2])) for t in range(owners)])
        for values, hops in zip(stacks[1:], return_order(chips))
    ]
    came = came[-1:] + came[:-1]

    rows = held * tile_rows
    part = rows // groups
    part_shape = shape(groups, 2, part, depth)
    parts = pl.pallas_call(
        functools.partial(add_kernel, chips, groups, held),
        out_shape=part_shape,
        in_specs=[VMEM] * stripes,
        out_specs=VMEM,
        scratch_shapes=[pltpu.VMEM((2, rows + tile_rows, depth), f32)],
        compiler_params=PARAMS,
        name="add_stripes",
    )(stacks[0], *came)

    def trade(values):
        return lax.all_to_all(values, "grp", split_axis=0, concat_axis=0, tiled=True)

    grads = pl.pallas_call(
        functools.partial(grads_kernel, 1.0 / math.sqrt(groups * owners), groups),
        out_shape=part_shape,
        in_specs=[VMEM] * 3,
        out_specs=VMEM,
        compiler_params=PARAMS,
        name="gradients",
    )(trade(parts), near_speed.reshape(rows, depth), near_density.reshape(rows, depth))
    whole = trade(grads)
    return (whole[:, 0].reshape(speed.shape), whole[:, 1].reshape(speed.shape))


def solution(mesh):
    return jax.shard_map(
        per_device,
        mesh=mesh,
        in_specs=(
            P("tile", None, None, None),
            P("tile", None, None, None),
            P(("grp", "tile"), None, None, None, None),
            P(("grp", "tile"), None, None, None, None),
            P(("grp", "tile"), None),
            P(("grp", "tile"), None),
            P(("grp", "tile"), None),
            P(("grp", "tile"), None, None),
            P(("grp", "tile"), None, None),
        ),
        out_specs=(P("tile", None, None, None), P("tile", None, None, None)),
        check_vma=False,
    )
```

```python
import functools
import math

import jax
import jax.numpy as jnp
from jax import lax
from jax.experimental import pallas as pl
from jax.experimental.pallas import tpu as pltpu
from jax.sharding import PartitionSpec as P

COEF = (1225.0 / 1024.0, -245.0 / 3072.0, 49.0 / 5120.0, -5.0 / 7168.0)
REACH = 4
EDGE = 8
ROWS = 8
SPAN = 8

SMEM = pl.BlockSpec(memory_space=pltpu.SMEM)
VMEM = pl.BlockSpec(memory_space=pltpu.VMEM)
PARAMS = pltpu.CompilerParams(vmem_limit_bytes=36 * 1024 * 1024)


def entry_of(list_ref):
    return jnp.max(list_ref[0:1, 0:1].astype(jnp.float32)).astype(jnp.int32)


def combine(ahead, behind):
    total = None
    for order in range(1, 5):
        upper, lower = ahead(order), behind(order)
        if upper is None and lower is None:
            continue
        if lower is None:
            term = upper
        elif upper is None:
            term = -lower
        else:
            term = upper - lower
        if order > 1:
            term = (COEF[order - 1] / COEF[0]) * term
        total = term if total is None else total + term
    return total


def band(first, depth):
    source = lax.broadcasted_iota(jnp.int32, (depth, depth), 0)
    target = lax.broadcasted_iota(jnp.int32, (depth, depth), 1)
    total = jnp.zeros((depth, depth), jnp.float32)
    for order in range(1, 5):
        weight = COEF[order - 1] / COEF[0]
        total = total + jnp.where(source == target + (first + order - 1), weight, 0.0)
        total = total - jnp.where(source == target + (first - order), weight, 0.0)
    return jnp.concatenate(halves(total), axis=1)


def halves(values):
    high = values.astype(jnp.bfloat16)
    return high, (values - high.astype(jnp.float32)).astype(jnp.bfloat16)


def along_z(values, matrix):
    xs, ys, zs = values.shape
    pair = jnp.concatenate(halves(values.reshape(xs * ys, zs)), axis=1)
    parts = jnp.dot(pair, matrix, preferred_element_type=jnp.float32)
    return (parts[:, :zs] + parts[:, zs:]).reshape(xs, ys, zs)


def blocks(xs, ys, body):
    if xs <= SPAN:
        for y0 in range(0, ys, ROWS):
            body(0, xs, y0)
        return

    def span(index, _):
        for y0 in range(0, ys, ROWS):
            body(index * SPAN, SPAN, y0)
        return 0

    lax.fori_loop(0, xs // SPAN, span, 0)


def window(xs, x0, load):
    kept = {}

    def at(offset):
        if xs <= SPAN and not 0 <= offset < xs:
            return None
        if offset not in kept:
            kept[offset] = load(x0 + offset)
        return kept[offset]

    return at


def slopes(xs, p, x0, y0, plane, offset):
    centre = plane(offset)
    here = x0 + offset + REACH
    return (
        combine(lambda k: plane(offset + k), lambda k: plane(offset + 1 - k)),
        combine(
            lambda k: p[here, pl.ds(EDGE + y0 + k, ROWS)],
            lambda k: centre if k == 1 else p[here, pl.ds(EDGE + y0 + 1 - k, ROWS)],
        ),
    )


def prepare_kernel(
    steps, fwd, adj, src, wave, rec, res, _piece,
    fwd_slope, adj_slope, fwd_source, adj_source, ahead, behind, *fields,
):
    xs, ys, zs = fwd_slope.shape[1:]
    for ref, first in ((ahead, 1), (behind, 0)):
        one = band(first, zs)
        ref[:zs] = one
        ref[zs:] = one

    def clear(ref):
        ref[...] = jnp.zeros(ref.shape, jnp.float32)

    for state, (p, v0, v1, v2), slope in (
        (fwd, fields[:4], fwd_slope),
        (adj, fields[4:], adj_slope),
    ):
        for ref in (p, v0):
            clear(ref.at[:REACH])
            clear(ref.at[REACH + xs :])
        for ref in (p.at[pl.ds(REACH, xs)], v1):
            clear(ref.at[:, :EDGE])
            clear(ref.at[:, EDGE + ys :])
        for x in range(xs):
            p[REACH + x, EDGE : EDGE + ys] = state[0, 0, x].astype(jnp.float32)
            v0[REACH + x] = state[0, 1, x].astype(jnp.float32)
            v1[x, EDGE : EDGE + ys] = state[0, 2, x].astype(jnp.float32)
            v2[x] = state[0, 3, x].astype(jnp.float32)

        def block(x0, count, y0, p=p, slope=slope):
            plane = window(xs, x0, lambda x: p[REACH + x, pl.ds(EDGE + y0, ROWS)])
            for offset in range(count):
                for d, values in enumerate(slopes(xs, p, x0, y0, plane, offset)):
                    slope[d, x0 + offset, pl.ds(y0, ROWS)] = values

        blocks(xs, ys, block)
        slope[2] = along_z(p[REACH : REACH + xs, EDGE : EDGE + ys], ahead[...])

    row = lax.broadcasted_iota(jnp.int32, (ys, zs), 0)
    lane = lax.broadcasted_iota(jnp.int32, (ys, zs), 1)
    src_mark = (row == src[0, 1]) & (lane == src[0, 2])
    for x in range(xs):
        rec_mark = (row == rec[0, 0, x]) & (lane == rec[0, 1, x])
        for step in range(steps):
            amplitude = jnp.where(x == src[0, 0], wave[0, step], 0.0)
            fwd_source[step, x] = jnp.where(src_mark, amplitude, 0.0)
            adj_source[step, x] = jnp.where(rec_mark, res[0, step, x], 0.0)


def near_kernel(speed, density, aperture, near_speed, near_density, entry):
    near_speed[...] = speed[...]
    near_density[...] = density[...]
    entry[...] = jnp.full(entry.shape, entry_of(aperture), jnp.int32)


def pick_kernel(chips, near_speed, near_density, far_speed, far_density, *refs):
    stripes = 2 * chips
    lists, outs = refs[:stripes], refs[stripes:]
    held = near_speed.shape[0]
    me = lax.axis_index("tile")
    residue, half = lax.rem(me, stripes), lax.div(me, stripes)
    for hop in range(stripes):
        entry = entry_of(lists[hop])
        corner, column = lax.div(entry, held), lax.rem(entry, held)
        here = (residue >= corner) == (half == 0)
        piece = outs[hop]

        @pl.when(here)
        def _():
            piece[0] = near_speed[column]
            piece[1] = near_density[column]

        @pl.when(jnp.logical_not(here))
        def _():
            piece[0] = far_speed[column]
            piece[1] = far_density[column]


def wave_kernel(chips, steps, held, *refs):
    stripes = 2 * chips
    pieces, refs = refs[:stripes], refs[stripes:]
    fwd_slope, adj_slope, fwd_source, adj_source, ahead, behind, entry_ref = refs[:7]
    kept, traded, p, v0, v1, v2, q, w0, w1, w2 = refs[15:25]
    bulk, buoy, dp, dv, bulk_img, buoy_img, across_z, flat = refs[25:]
    tile_x, tile_y = pieces[0].shape[1:3]
    xs, ys, zs = bulk.shape
    residue = lax.rem(lax.axis_index("tile"), stripes)
    entry = entry_of(entry_ref)
    corner = lax.div(entry, held)

    def place_of(hop):
        return lax.rem((residue ^ hop) - corner + stripes, stripes) * tile_x

    for hop in range(stripes):
        cells = pl.ds(place_of(hop), tile_x)
        speed, density = pieces[hop][0], pieces[hop][1]
        bulk[cells] = COEF[0] * (density * speed * speed)
        buoy[cells] = COEF[0] / density

    def push(fields, first, note):
        p, v0, v1, v2 = fields
        if first is None:
            across_z[...] = along_z(p[REACH : REACH + xs, EDGE : EDGE + ys], ahead[...])

        def block(x0, count, y0):
            rows, inner = pl.ds(y0, ROWS), pl.ds(EDGE + y0, ROWS)
            plane = window(xs, x0, lambda x: p[REACH + x, inner])
            for offset in range(count):
                x = x0 + offset
                if first is None:
                    two = slopes(xs, p, x0, y0, plane, offset)
                else:
                    two = (first[0, x, rows], first[1, x, rows])
                light = buoy[x, rows]
                changes = (light * two[0], light * two[1])
                moved = (v0[REACH + x, rows] + changes[0], v1[x, inner] + changes[1])
                v0[REACH + x, rows] = moved[0]
                v1[x, inner] = moved[1]
                note(0, x, rows, changes, moved)

        def block_z(x0, count, y0):
            rows = pl.ds(y0, ROWS)
            for x in range(count):
                x = x0 + x
                slope = across_z[x, rows] if first is None else first[2, x, rows]
                change = buoy[x, rows] * slope
                moved = v2[x, rows] + change
                v2[x, rows] = moved
                note(2, x, rows, (change,), (moved,))

        blocks(xs, ys, block)
        blocks(xs, ys, block_z)

    def spread(fields, source, step, note):
        p, v0, v1, v2 = fields
        across_z[...] = along_z(v2[...], behind[...])

        def block(x0, count, y0):
            rows = pl.ds(y0, ROWS)
            plane = window(xs, x0, lambda x: v0[REACH + x, rows])
            for offset in range(count):
                x = x0 + offset
                along_x = combine(lambda k: plane(offset + k - 1), lambda k: plane(offset - k))
                along_y = combine(
                    lambda k: v1[x, pl.ds(EDGE + y0 + k - 1, ROWS)],
                    lambda k: v1[x, pl.ds(EDGE + y0 - k, ROWS)],
                )
                flat[x, rows] = along_x + along_y

        def block_z(x0, count, y0):
            rows, inner = pl.ds(y0, ROWS), pl.ds(EDGE + y0, ROWS)
            for x in range(count):
                x = x0 + x
                change = bulk[x, rows] * (flat[x, rows] + across_z[x, rows])
                change = change + source[step, x, rows]
                moved = p[REACH + x, inner] + change
                p[REACH + x, inner] = moved
                note(x, rows, change, moved)

        blocks(xs, ys, block)
        blocks(xs, ys, block_z)

    fields = (p, v0, v1, v2)
    for step in range(steps):

        def keep_dv(first, x, rows, changes, moved, step=step):
            for d, change in enumerate(changes, first):
                dv[step, d, x, rows] = change

        def keep_dp(x, rows, change, moved, step=step):
            dp[step, x, rows] = change

        push(fields, fwd_slope if step == 0 else None, keep_dv)
        spread(fields, fwd_source, step, keep_dp)

    fields = (q, w0, w1, w2)
    for step in reversed(range(steps)):
        last = step == steps - 1

        def add_buoy(first, x, rows, changes, moved, step=step, last=last):
            image = None if last and first == 0 else buoy_img[x, rows]
            for d, values in enumerate(moved, first):
                product = dv[step, d, x, rows] * values
                image = product if image is None else image + product
            buoy_img[x, rows] = image

        def add_bulk(x, rows, change, moved, step=step, last=last):
            image = dp[step, x, rows] * moved
            bulk_img[x, rows] = image if last else bulk_img[x, rows] + image

        push(fields, adj_slope if last else None, add_buoy)
        spread(fields, adj_source, step, add_bulk)

    tile_rows = tile_x * tile_y
    for chip in range(chips):
        for ref, hop in ((kept, 2 * chip), (traded, 2 * chip + 1)):
            cells = pl.ds(place_of(hop), tile_x)
            ref[chip, :tile_rows] = bulk_img[cells].reshape(tile_rows, zs)
            ref[chip, tile_rows : 2 * tile_rows] = buoy_img[cells].reshape(tile_rows, zs)
            ref[chip, 2 * tile_rows :] = jnp.full((8, zs), entry).astype(jnp.float32)


def return_order(chips):
    even = [chips] + list(range(1, chips)) + list(range(chips + 1, 2 * chips))
    return list(zip(even, reversed(even)))


def merge_kernel(chips, kept, came, *outs):
    rows = kept.shape[1] - 8
    odd = lax.rem(lax.axis_index("tile"), 2) == 1
    for out, (even_hop, odd_hop) in zip(outs, [(0, 0)] + return_order(chips)):
        chip = jnp.where(odd, odd_hop % chips, even_hop % chips)
        for shot, source in enumerate((kept, came)):
            out[shot * rows : (shot + 1) * rows] = source[chip, :rows]
            first = 2 * rows + 4 * shot
            out[first : first + 4] = source[chip, rows : rows + 4]


def add_kernel(chips, groups, held, *refs):
    came, parts, total = refs[: 2 * chips], refs[2 * chips : 2 * chips + groups], refs[-1]
    stripes = 2 * chips
    me, group = lax.axis_index("tile"), lax.axis_index("grp")
    tile_rows = total.shape[1] // (held + 1)
    part = parts[0].shape[1]
    total[...] = jnp.zeros_like(total)
    for pair in came:
        for shot in range(2):
            first = 4 * tile_rows + 4 * shot
            entry = jnp.max(pair[first : first + 4]).astype(jnp.int32)
            corner, column = lax.div(entry, held), lax.rem(entry, held)
            mine = (corner <= me) & (me < corner + stripes)
            slot = jnp.where(mine, column, held)
            rows = pl.ds(pl.multiple_of(slot * tile_rows, tile_rows), tile_rows)
            for field in range(2):
                first = (2 * shot + field) * tile_rows
                total[field, rows] = total[field, rows] + pair[first : first + tile_rows]
    for index, hop in enumerate([0] + far_first(groups)):
        first = pl.multiple_of((group ^ hop) * part, part)
        for field in range(2):
            parts[index][field] = total[field, pl.ds(first, part)]


def far_first(groups):
    return list(range(groups // 2, groups)) + list(range(1, groups // 2))


def grads_kernel(scale, groups, *refs):
    parts, speed_ref, density_ref, grads = refs[:groups], *refs[groups:]
    part = parts[0].shape[1]
    rows = pl.ds(pl.multiple_of(lax.axis_index("grp") * part, part), part)
    speed, density = speed_ref[rows], density_ref[rows]
    bulk_sum, buoy_sum = parts[0][0], parts[0][1]
    for other in parts[1:]:
        bulk_sum = bulk_sum + other[0]
        buoy_sum = buoy_sum + other[1]
    grads[0] = scale * (bulk_sum * (2.0 * density * speed))
    grads[1] = scale * (bulk_sum * (speed * speed) - buoy_sum / (density * density))


def per_device(speed, density, fwd_state, adj_state, aperture, src_pos, wavelet, rec_pos, residual):
    owners = lax.axis_size("tile")
    groups = lax.axis_size("grp")
    my_group = lax.axis_index("grp")
    held, tile_x, tile_y, depth = speed.shape
    stripes = aperture.shape[1]
    chips = stripes // 2
    steps = wavelet.shape[1]
    xs = stripes * tile_x
    f32 = jnp.float32
    cells = (xs, tile_y, depth)

    def shape(*dims):
        return jax.ShapeDtypeStruct(dims, f32)

    def across(values, hop):
        return lax.ppermute(values, "tile", [(t, t ^ hop) for t in range(owners)])

    far_speed = across(speed, stripes)
    far_density = across(density, stripes)
    lists = {hop: across(aperture, hop) for hop in range(stripes - 1, 0, -1)}
    four = [
        (xs + 2 * REACH, tile_y + 2 * EDGE, depth),
        (xs + 2 * REACH, tile_y, depth),
        (xs, tile_y + 2 * EDGE, depth),
        cells,
    ]
    near_speed, near_density, entry = pl.pallas_call(
        near_kernel,
        out_shape=[
            shape(*speed.shape),
            shape(*speed.shape),
            jax.ShapeDtypeStruct((8, depth), jnp.int32),
        ],
        in_specs=[VMEM] * 3,
        out_specs=[VMEM] * 3,
        compiler_params=PARAMS,
        cost_estimate=pl.CostEstimate(flops=4_000_000, bytes_accessed=6_000_000, transcendentals=0),
        name="hold_near_tiles",
    )(speed, density, aperture)
    pieces = pl.pallas_call(
        functools.partial(pick_kernel, chips),
        out_shape=[shape(2, tile_x, tile_y, depth)] * stripes,
        in_specs=[VMEM] * (4 + stripes),
        out_specs=[VMEM] * stripes,
        compiler_params=PARAMS,
        name="pick_tiles",
    )(near_speed, near_density, far_speed, far_density, entry, *[lists[h] for h in range(1, stripes)])
    moved = {hop: across(pieces[hop], hop) for hop in range(stripes - 1, 0, -1)}

    prepared = pl.pallas_call(
        functools.partial(prepare_kernel, steps),
        out_shape=[shape(3, *cells)] * 2
        + [shape(steps, *cells)] * 2
        + [jax.ShapeDtypeStruct((2 * depth, 2 * depth), jnp.bfloat16)] * 2
        + [shape(*dims) for dims in four + four],
        in_specs=[VMEM] * 2 + [SMEM] * 4 + [VMEM],
        out_specs=[VMEM] * 14,
        compiler_params=PARAMS,
        cost_estimate=pl.CostEstimate(flops=4_000_000, bytes_accessed=6_000_000, transcendentals=0),
        name="prepare",
    )(fwd_state, adj_state, src_pos, wavelet, jnp.swapaxes(rec_pos, 1, 2), residual, pieces[0])
    prepared, fields = prepared[:6], prepared[6:]
    pieces = [pieces[0]] + [moved[hop] for hop in range(1, stripes)]

    tile_rows = tile_x * tile_y
    sent = shape(chips, 2 * tile_rows + 8, depth)
    kept, traded, *_ = pl.pallas_call(
        functools.partial(wave_kernel, chips, steps, held),
        out_shape=[sent, sent] + [shape(*dims) for dims in four + four],
        in_specs=[VMEM] * (stripes + 15),
        out_specs=[VMEM] * 10,
        scratch_shapes=[
            pltpu.VMEM(cells, f32),
            pltpu.VMEM(cells, f32),
            pltpu.VMEM((steps,) + cells, f32),
            pltpu.VMEM((steps, 3) + cells, f32),
        ]
        + [pltpu.VMEM(cells, f32)] * 4
        + [
        ],
        input_output_aliases={stripes + 7 + index: 2 + index for index in range(8)},
        compiler_params=PARAMS,
        name="replay_and_adjoint",
    )(*pieces, *prepared, entry, *fields)

    both = shape(4 * tile_rows + 8, depth)
    stacks = pl.pallas_call(
        functools.partial(merge_kernel, chips),
        out_shape=[both] * stripes,
        in_specs=[VMEM] * 2,
        out_specs=[VMEM] * stripes,
        compiler_params=PARAMS,
        name="merge_pair",
    )(kept, across(traded, 1))
    came = [
        lax.ppermute(values, "tile", [(t, t ^ (2 * hops[t % 2])) for t in range(owners)])
        for values, hops in zip(stacks[1:], return_order(chips))
    ]
    came = came[-1:] + came[:-1]

    rows = held * tile_rows
    part = rows // groups
    part_shape = shape(2, part, depth)
    parts = pl.pallas_call(
        functools.partial(add_kernel, chips, groups, held),
        out_shape=[part_shape] * groups,
        in_specs=[VMEM] * stripes,
        out_specs=[VMEM] * groups,
        scratch_shapes=[pltpu.VMEM((2, rows + tile_rows, depth), f32)],
        compiler_params=PARAMS,
        name="add_stripes",
    )(stacks[0], *came)

    def along(values, hop):
        return lax.ppermute(values, "grp", [(g, g ^ hop) for g in range(groups)])

    parts = [parts[0]] + [along(values, hop) for values, hop in zip(parts[1:], far_first(groups))]
    grads = pl.pallas_call(
        functools.partial(grads_kernel, 1.0 / math.sqrt(groups * owners), groups),
        out_shape=part_shape,
        in_specs=[VMEM] * (groups + 2),
        out_specs=VMEM,
        compiler_params=PARAMS,
        name="gradients",
    )(*parts, near_speed.reshape(rows, depth), near_density.reshape(rows, depth))

    whole = jnp.zeros((2, groups, part, depth), f32)
    for hop in range(groups):
        values = grads
        if hop:
            values = lax.ppermute(grads, "grp", [(g, (g + hop) % groups) for g in range(groups)])
        place = lax.rem(my_group - hop + groups, groups)
        whole = lax.dynamic_update_slice_in_dim(whole, values[:, None], place, axis=1)
    return (whole[0].reshape(speed.shape), whole[1].reshape(speed.shape))


def solution(mesh):
    return jax.shard_map(
        per_device,
        mesh=mesh,
        in_specs=(
            P("tile", None, None, None),
            P("tile", None, None, None),
            P(("grp", "tile"), None, None, None, None),
            P(("grp", "tile"), None, None, None, None),
            P(("grp", "tile"), None),
            P(("grp", "tile"), None),
            P(("grp", "tile"), None),
            P(("grp", "tile"), None, None),
            P(("grp", "tile"), None, None),
        ),
        out_specs=(P("tile", None, None, None), P("tile", None, None, None)),
        check_vma=False,
    )
```

```python
import functools
import math

import jax
import jax.numpy as jnp
from jax import lax
from jax.experimental import pallas as pl
from jax.experimental.pallas import tpu as pltpu
from jax.sharding import PartitionSpec as P

COEF = (1225.0 / 1024.0, -245.0 / 3072.0, 49.0 / 5120.0, -5.0 / 7168.0)
REACH = 4
EDGE = 8
ROWS = 8
SPAN = 8

SMEM = pl.BlockSpec(memory_space=pltpu.SMEM)
VMEM = pl.BlockSpec(memory_space=pltpu.VMEM)
PARAMS = pltpu.CompilerParams(vmem_limit_bytes=36 * 1024 * 1024)


def entry_of(list_ref):
    return jnp.max(list_ref[0:1, 0:1].astype(jnp.float32)).astype(jnp.int32)


def combine(ahead, behind):
    total = None
    for order in range(1, 5):
        upper, lower = ahead(order), behind(order)
        if upper is None and lower is None:
            continue
        if lower is None:
            term = upper
        elif upper is None:
            term = -lower
        else:
            term = upper - lower
        if order > 1:
            term = (COEF[order - 1] / COEF[0]) * term
        total = term if total is None else total + term
    return total


def band(first, depth):
    source = lax.broadcasted_iota(jnp.int32, (depth, depth), 0)
    target = lax.broadcasted_iota(jnp.int32, (depth, depth), 1)
    total = jnp.zeros((depth, depth), jnp.float32)
    for order in range(1, 5):
        weight = COEF[order - 1] / COEF[0]
        total = total + jnp.where(source == target + (first + order - 1), weight, 0.0)
        total = total - jnp.where(source == target + (first - order), weight, 0.0)
    return jnp.concatenate(halves(total), axis=1)


def halves(values):
    high = values.astype(jnp.bfloat16)
    return high, (values - high.astype(jnp.float32)).astype(jnp.bfloat16)


def along_z(values, matrix):
    xs, ys, zs = values.shape
    pair = jnp.concatenate(halves(values.reshape(xs * ys, zs)), axis=1)
    parts = jnp.dot(pair, matrix, preferred_element_type=jnp.float32)
    return (parts[:, :zs] + parts[:, zs:]).reshape(xs, ys, zs)


def blocks(xs, ys, body):
    if xs <= SPAN:
        for y0 in range(0, ys, ROWS):
            body(0, xs, y0)
        return

    def span(index, _):
        for y0 in range(0, ys, ROWS):
            body(index * SPAN, SPAN, y0)
        return 0

    lax.fori_loop(0, xs // SPAN, span, 0)


def window(xs, x0, load):
    kept = {}

    def at(offset):
        if xs <= SPAN and not 0 <= offset < xs:
            return None
        if offset not in kept:
            kept[offset] = load(x0 + offset)
        return kept[offset]

    return at


def slopes(xs, p, x0, y0, plane, offset):
    centre = plane(offset)
    here = x0 + offset + REACH
    return (
        combine(lambda k: plane(offset + k), lambda k: plane(offset + 1 - k)),
        combine(
            lambda k: p[here, pl.ds(EDGE + y0 + k, ROWS)],
            lambda k: centre if k == 1 else p[here, pl.ds(EDGE + y0 + 1 - k, ROWS)],
        ),
    )


def prepare_kernel(
    steps, fwd, adj, src, wave, rec, res, _piece,
    fwd_slope, adj_slope, fwd_source, adj_source, ahead, behind, *fields,
):
    xs, ys, zs = fwd_slope.shape[1:]
    for ref, first in ((ahead, 1), (behind, 0)):
        one = band(first, zs)
        ref[:zs] = one
        ref[zs:] = one

    def clear(ref):
        ref[...] = jnp.zeros(ref.shape, jnp.float32)

    for state, (p, v0, v1, v2), slope in (
        (fwd, fields[:4], fwd_slope),
        (adj, fields[4:], adj_slope),
    ):
        for ref in (p, v0):
            clear(ref.at[:REACH])
            clear(ref.at[REACH + xs :])
        for ref in (p.at[pl.ds(REACH, xs)], v1):
            clear(ref.at[:, :EDGE])
            clear(ref.at[:, EDGE + ys :])
        for x in range(xs):
            p[REACH + x, EDGE : EDGE + ys] = state[0, 0, x].astype(jnp.float32)
            v0[REACH + x] = state[0, 1, x].astype(jnp.float32)
            v1[x, EDGE : EDGE + ys] = state[0, 2, x].astype(jnp.float32)
            v2[x] = state[0, 3, x].astype(jnp.float32)

        def block(x0, count, y0, p=p, slope=slope):
            plane = window(xs, x0, lambda x: p[REACH + x, pl.ds(EDGE + y0, ROWS)])
            for offset in range(count):
                for d, values in enumerate(slopes(xs, p, x0, y0, plane, offset)):
                    slope[d, x0 + offset, pl.ds(y0, ROWS)] = values

        blocks(xs, ys, block)
        slope[2] = along_z(p[REACH : REACH + xs, EDGE : EDGE + ys], ahead[...])

    row = lax.broadcasted_iota(jnp.int32, (ys, zs), 0)
    lane = lax.broadcasted_iota(jnp.int32, (ys, zs), 1)
    src_mark = (row == src[0, 1]) & (lane == src[0, 2])
    for x in range(xs):
        rec_mark = (row == rec[0, 0, x]) & (lane == rec[0, 1, x])
        for step in range(steps):
            amplitude = jnp.where(x == src[0, 0], wave[0, step], 0.0)
            fwd_source[step, x] = jnp.where(src_mark, amplitude, 0.0)
            adj_source[step, x] = jnp.where(rec_mark, res[0, step, x], 0.0)


def near_kernel(speed, density, aperture, near_speed, near_density, entry):
    near_speed[...] = speed[...]
    near_density[...] = density[...]
    entry[...] = jnp.full(entry.shape, entry_of(aperture), jnp.int32)


def pick_kernel(chips, near_speed, near_density, far_speed, far_density, *refs):
    stripes = 2 * chips
    lists, outs = refs[:stripes], refs[stripes:]
    held = near_speed.shape[0]
    me = lax.axis_index("tile")
    residue, half = lax.rem(me, stripes), lax.div(me, stripes)
    for hop in range(stripes):
        entry = entry_of(lists[hop])
        corner, column = lax.div(entry, held), lax.rem(entry, held)
        here = (residue >= corner) == (half == 0)
        piece = outs[hop]

        @pl.when(here)
        def _():
            piece[0] = near_speed[column]
            piece[1] = near_density[column]

        @pl.when(jnp.logical_not(here))
        def _():
            piece[0] = far_speed[column]
            piece[1] = far_density[column]


def gather_order(stripes):
    return [0] + list(range(2, stripes, 2)) + list(range(1, stripes, 2))


def wave_kernel(chips, steps, held, *refs):
    stripes = 2 * chips
    pieces, refs = refs[:stripes], refs[stripes:]
    fwd_slope, adj_slope, fwd_source, adj_source, ahead, behind, entry_ref = refs[:7]
    kept, traded, p, v0, v1, v2, q, w0, w1, w2 = refs[15:25]
    bulk, buoy, dp, dv, bulk_img, buoy_img, across_z, flat = refs[25:]
    tile_x, tile_y = pieces[0].shape[1:3]
    xs, ys, zs = bulk.shape
    residue = lax.rem(lax.axis_index("tile"), stripes)
    entry = entry_of(entry_ref)
    corner = lax.div(entry, held)

    def place_of(hop):
        return lax.rem((residue ^ hop) - corner + stripes, stripes) * tile_x

    for hop, piece in zip(gather_order(stripes), pieces):
        cells = pl.ds(place_of(hop), tile_x)
        speed, density = piece[0], piece[1]
        bulk[cells] = COEF[0] * (density * speed * speed)
        buoy[cells] = COEF[0] / density

    def push(fields, first, note):
        p, v0, v1, v2 = fields
        if first is None:
            across_z[...] = along_z(p[REACH : REACH + xs, EDGE : EDGE + ys], ahead[...])

        def block(x0, count, y0):
            rows, inner = pl.ds(y0, ROWS), pl.ds(EDGE + y0, ROWS)
            plane = window(xs, x0, lambda x: p[REACH + x, inner])
            for offset in range(count):
                x = x0 + offset
                if first is None:
                    two = slopes(xs, p, x0, y0, plane, offset)
                else:
                    two = (first[0, x, rows], first[1, x, rows])
                light = buoy[x, rows]
                changes = (light * two[0], light * two[1])
                moved = (v0[REACH + x, rows] + changes[0], v1[x, inner] + changes[1])
                v0[REACH + x, rows] = moved[0]
                v1[x, inner] = moved[1]
                note(0, x, rows, changes, moved)

        def block_z(x0, count, y0):
            rows = pl.ds(y0, ROWS)
            for x in range(count):
                x = x0 + x
                slope = across_z[x, rows] if first is None else first[2, x, rows]
                change = buoy[x, rows] * slope
                moved = v2[x, rows] + change
                v2[x, rows] = moved
                note(2, x, rows, (change,), (moved,))

        blocks(xs, ys, block)
        blocks(xs, ys, block_z)

    def spread(fields, source, step, note):
        p, v0, v1, v2 = fields
        across_z[...] = along_z(v2[...], behind[...])

        def block(x0, count, y0):
            rows = pl.ds(y0, ROWS)
            plane = window(xs, x0, lambda x: v0[REACH + x, rows])
            for offset in range(count):
                x = x0 + offset
                along_x = combine(lambda k: plane(offset + k - 1), lambda k: plane(offset - k))
                along_y = combine(
                    lambda k: v1[x, pl.ds(EDGE + y0 + k - 1, ROWS)],
                    lambda k: v1[x, pl.ds(EDGE + y0 - k, ROWS)],
                )
                flat[x, rows] = along_x + along_y

        def block_z(x0, count, y0):
            rows, inner = pl.ds(y0, ROWS), pl.ds(EDGE + y0, ROWS)
            for x in range(count):
                x = x0 + x
                change = bulk[x, rows] * (flat[x, rows] + across_z[x, rows])
                change = change + source[step, x, rows]
                moved = p[REACH + x, inner] + change
                p[REACH + x, inner] = moved
                note(x, rows, change, moved)

        blocks(xs, ys, block)
        blocks(xs, ys, block_z)

    fields = (p, v0, v1, v2)
    for step in range(steps):

        def keep_dv(first, x, rows, changes, moved, step=step):
            for d, change in enumerate(changes, first):
                dv[step, d, x, rows] = change

        def keep_dp(x, rows, change, moved, step=step):
            dp[step, x, rows] = change

        push(fields, fwd_slope if step == 0 else None, keep_dv)
        spread(fields, fwd_source, step, keep_dp)

    fields = (q, w0, w1, w2)
    for step in reversed(range(steps)):
        last = step == steps - 1

        def add_buoy(first, x, rows, changes, moved, step=step, last=last):
            image = None if last and first == 0 else buoy_img[x, rows]
            for d, values in enumerate(moved, first):
                product = dv[step, d, x, rows] * values
                image = product if image is None else image + product
            buoy_img[x, rows] = image

        def add_bulk(x, rows, change, moved, step=step, last=last):
            image = dp[step, x, rows] * moved
            bulk_img[x, rows] = image if last else bulk_img[x, rows] + image

        push(fields, adj_slope if last else None, add_buoy)
        spread(fields, adj_source, step, add_bulk)

    tile_rows = tile_x * tile_y
    for chip in range(chips):
        for ref, hop in ((kept, 2 * chip), (traded, 2 * chip + 1)):
            cells = pl.ds(place_of(hop), tile_x)
            ref[chip, :tile_rows] = bulk_img[cells].reshape(tile_rows, zs)
            ref[chip, tile_rows : 2 * tile_rows] = buoy_img[cells].reshape(tile_rows, zs)
            ref[chip, 2 * tile_rows :] = jnp.full((8, zs), entry).astype(jnp.float32)


def return_order(chips):
    even = [chips] + list(range(1, chips)) + list(range(chips + 1, 2 * chips))
    return list(zip(even, reversed(even)))


def merge_kernel(chips, kept, came, *outs):
    rows = kept.shape[1] - 8
    odd = lax.rem(lax.axis_index("tile"), 2) == 1
    for out, (even_hop, odd_hop) in zip(outs, [(0, 0)] + return_order(chips)):
        chip = jnp.where(odd, odd_hop % chips, even_hop % chips)
        for shot, source in enumerate((kept, came)):
            out[shot * rows : (shot + 1) * rows] = source[chip, :rows]
            first = 2 * rows + 4 * shot
            out[first : first + 4] = source[chip, rows : rows + 4]


def add_kernel(chips, groups, held, *refs):
    came, parts, total = refs[: 2 * chips], refs[2 * chips : 2 * chips + groups], refs[-1]
    stripes = 2 * chips
    me, group = lax.axis_index("tile"), lax.axis_index("grp")
    tile_rows = total.shape[1] // (held + 1)
    part = parts[0].shape[1]
    total[...] = jnp.zeros_like(total)
    for pair in came:
        for shot in range(2):
            first = 4 * tile_rows + 4 * shot
            entry = jnp.max(pair[first : first + 4]).astype(jnp.int32)
            corner, column = lax.div(entry, held), lax.rem(entry, held)
            mine = (corner <= me) & (me < corner + stripes)
            slot = jnp.where(mine, column, held)
            rows = pl.ds(pl.multiple_of(slot * tile_rows, tile_rows), tile_rows)
            for field in range(2):
                first = (2 * shot + field) * tile_rows
                total[field, rows] = total[field, rows] + pair[first : first + tile_rows]
    for index, hop in enumerate([0] + far_first(groups)):
        first = pl.multiple_of((group ^ hop) * part, part)
        for field in range(2):
            parts[index][field] = total[field, pl.ds(first, part)]


def far_first(groups):
    return list(range(groups - 1, 0, -1))


def grads_kernel(scale, groups, *refs):
    parts, speed_ref, density_ref, grads = refs[:groups], *refs[groups:]
    part = parts[0].shape[1]
    rows = pl.ds(pl.multiple_of(lax.axis_index("grp") * part, part), part)
    speed, density = speed_ref[rows], density_ref[rows]
    bulk_sum, buoy_sum = parts[0][0], parts[0][1]
    for other in parts[1:]:
        bulk_sum = bulk_sum + other[0]
        buoy_sum = buoy_sum + other[1]
    grads[0] = scale * (bulk_sum * (2.0 * density * speed))
    grads[1] = scale * (bulk_sum * (speed * speed) - buoy_sum / (density * density))


def per_device(speed, density, fwd_state, adj_state, aperture, src_pos, wavelet, rec_pos, residual):
    owners = lax.axis_size("tile")
    groups = lax.axis_size("grp")
    my_group = lax.axis_index("grp")
    held, tile_x, tile_y, depth = speed.shape
    stripes = aperture.shape[1]
    chips = stripes // 2
    steps = wavelet.shape[1]
    xs = stripes * tile_x
    f32 = jnp.float32
    cells = (xs, tile_y, depth)

    def shape(*dims):
        return jax.ShapeDtypeStruct(dims, f32)

    def across(values, hop):
        return lax.ppermute(values, "tile", [(t, t ^ hop) for t in range(owners)])

    far_speed = across(speed, stripes)
    far_density = across(density, stripes)
    lists = {hop: across(aperture, hop) for hop in range(stripes - 1, 0, -1)}
    four = [
        (xs + 2 * REACH, tile_y + 2 * EDGE, depth),
        (xs + 2 * REACH, tile_y, depth),
        (xs, tile_y + 2 * EDGE, depth),
        cells,
    ]
    near_speed, near_density, entry = pl.pallas_call(
        near_kernel,
        out_shape=[
            shape(*speed.shape),
            shape(*speed.shape),
            jax.ShapeDtypeStruct((8, depth), jnp.int32),
        ],
        in_specs=[VMEM] * 3,
        out_specs=[VMEM] * 3,
        compiler_params=PARAMS,
        cost_estimate=pl.CostEstimate(flops=4_000_000, bytes_accessed=6_000_000, transcendentals=0),
        name="hold_near_tiles",
    )(speed, density, aperture)
    pieces = pl.pallas_call(
        functools.partial(pick_kernel, chips),
        out_shape=[shape(2, tile_x, tile_y, depth)] * stripes,
        in_specs=[VMEM] * (4 + stripes),
        out_specs=[VMEM] * stripes,
        compiler_params=PARAMS,
        name="pick_tiles",
    )(near_speed, near_density, far_speed, far_density, entry, *[lists[h] for h in range(1, stripes)])

    prepared = pl.pallas_call(
        functools.partial(prepare_kernel, steps),
        out_shape=[shape(3, *cells)] * 2
        + [shape(steps, *cells)] * 2
        + [jax.ShapeDtypeStruct((2 * depth, 2 * depth), jnp.bfloat16)] * 2
        + [shape(*dims) for dims in four + four],
        in_specs=[VMEM] * 2 + [SMEM] * 4 + [VMEM],
        out_specs=[VMEM] * 14,
        compiler_params=PARAMS,
        cost_estimate=pl.CostEstimate(flops=4_000_000, bytes_accessed=6_000_000, transcendentals=0),
        name="prepare",
    )(fwd_state, adj_state, src_pos, wavelet, jnp.swapaxes(rec_pos, 1, 2), residual, pieces[0])
    prepared, fields = prepared[:6], prepared[6:]
    pieces = [across(pieces[hop], hop) if hop else pieces[0] for hop in gather_order(stripes)]

    tile_rows = tile_x * tile_y
    sent = shape(chips, 2 * tile_rows + 8, depth)
    kept, traded, *_ = pl.pallas_call(
        functools.partial(wave_kernel, chips, steps, held),
        out_shape=[sent, sent] + [shape(*dims) for dims in four + four],
        in_specs=[VMEM] * (stripes + 15),
        out_specs=[VMEM] * 10,
        scratch_shapes=[
            pltpu.VMEM(cells, f32),
            pltpu.VMEM(cells, f32),
            pltpu.VMEM((steps,) + cells, f32),
            pltpu.VMEM((steps, 3) + cells, f32),
        ]
        + [pltpu.VMEM(cells, f32)] * 4
        + [
        ],
        input_output_aliases={stripes + 7 + index: 2 + index for index in range(8)},
        compiler_params=PARAMS,
        name="replay_and_adjoint",
    )(*pieces, *prepared, entry, *fields)

    both = shape(4 * tile_rows + 8, depth)
    stacks = pl.pallas_call(
        functools.partial(merge_kernel, chips),
        out_shape=[both] * stripes,
        in_specs=[VMEM] * 2,
        out_specs=[VMEM] * stripes,
        compiler_params=PARAMS,
        name="merge_pair",
    )(kept, across(traded, 1))
    came = [
        lax.ppermute(values, "tile", [(t, t ^ (2 * hops[t % 2])) for t in range(owners)])
        for values, hops in zip(stacks[1:], return_order(chips))
    ]
    came = came[-1:] + came[:-1]

    rows = held * tile_rows
    part = rows // groups
    part_shape = shape(2, part, depth)
    parts = pl.pallas_call(
        functools.partial(add_kernel, chips, groups, held),
        out_shape=[part_shape] * groups,
        in_specs=[VMEM] * stripes,
        out_specs=[VMEM] * groups,
        scratch_shapes=[pltpu.VMEM((2, rows + tile_rows, depth), f32)],
        compiler_params=PARAMS,
        name="add_stripes",
    )(stacks[0], *came)

    def along(values, hop):
        return lax.ppermute(values, "grp", [(g, g ^ hop) for g in range(groups)])

    parts = [parts[0]] + [along(values, hop) for values, hop in zip(parts[1:], far_first(groups))]
    grads = pl.pallas_call(
        functools.partial(grads_kernel, 1.0 / math.sqrt(groups * owners), groups),
        out_shape=part_shape,
        in_specs=[VMEM] * (groups + 2),
        out_specs=VMEM,
        compiler_params=PARAMS,
        name="gradients",
    )(*parts, near_speed.reshape(rows, depth), near_density.reshape(rows, depth))

    whole = jnp.zeros((2, groups, part, depth), f32)
    for hop in range(groups):
        values = grads
        if hop:
            values = lax.ppermute(grads, "grp", [(g, (g + hop) % groups) for g in range(groups)])
        place = lax.rem(my_group - hop + groups, groups)
        whole = lax.dynamic_update_slice_in_dim(whole, values[:, None], place, axis=1)
    return (whole[0].reshape(speed.shape), whole[1].reshape(speed.shape))


def solution(mesh):
    return jax.shard_map(
        per_device,
        mesh=mesh,
        in_specs=(
            P("tile", None, None, None),
            P("tile", None, None, None),
            P(("grp", "tile"), None, None, None, None),
            P(("grp", "tile"), None, None, None, None),
            P(("grp", "tile"), None),
            P(("grp", "tile"), None),
            P(("grp", "tile"), None),
            P(("grp", "tile"), None, None),
            P(("grp", "tile"), None, None),
        ),
        out_specs=(P("tile", None, None, None), P("tile", None, None, None)),
        check_vma=False,
    )
```

```python
import functools
import math

import jax
import jax.numpy as jnp
from jax import lax
from jax.experimental import pallas as pl
from jax.experimental.pallas import tpu as pltpu
from jax.sharding import PartitionSpec as P

COEF = (1225.0 / 1024.0, -245.0 / 3072.0, 49.0 / 5120.0, -5.0 / 7168.0)
REACH = 4
EDGE = 8
ROWS = 8
SPAN = 8

SMEM = pl.BlockSpec(memory_space=pltpu.SMEM)
VMEM = pl.BlockSpec(memory_space=pltpu.VMEM)
PARAMS = pltpu.CompilerParams(vmem_limit_bytes=36 * 1024 * 1024)


def entry_of(list_ref):
    return jnp.max(list_ref[0:1, 0:1].astype(jnp.float32)).astype(jnp.int32)


def combine(ahead, behind):
    total = None
    for order in range(1, 5):
        upper, lower = ahead(order), behind(order)
        if upper is None and lower is None:
            continue
        if lower is None:
            term = upper
        elif upper is None:
            term = -lower
        else:
            term = upper - lower
        if order > 1:
            term = (COEF[order - 1] / COEF[0]) * term
        total = term if total is None else total + term
    return total


def band(first, depth):
    source = lax.broadcasted_iota(jnp.int32, (depth, depth), 0)
    target = lax.broadcasted_iota(jnp.int32, (depth, depth), 1)
    total = jnp.zeros((depth, depth), jnp.float32)
    for order in range(1, 5):
        weight = COEF[order - 1] / COEF[0]
        total = total + jnp.where(source == target + (first + order - 1), weight, 0.0)
        total = total - jnp.where(source == target + (first - order), weight, 0.0)
    return jnp.concatenate(halves(total), axis=1)


def halves(values):
    high = values.astype(jnp.bfloat16)
    return high, (values - high.astype(jnp.float32)).astype(jnp.bfloat16)


def along_z(values, matrix):
    xs, ys, zs = values.shape
    pair = jnp.concatenate(halves(values.reshape(xs * ys, zs)), axis=1)
    parts = jnp.dot(pair, matrix, preferred_element_type=jnp.float32)
    return (parts[:, :zs] + parts[:, zs:]).reshape(xs, ys, zs)


def blocks(xs, ys, body):
    if xs <= SPAN:
        for y0 in range(0, ys, ROWS):
            body(0, xs, y0)
        return

    def span(index, _):
        for y0 in range(0, ys, ROWS):
            body(index * SPAN, SPAN, y0)
        return 0

    lax.fori_loop(0, xs // SPAN, span, 0)


def window(xs, x0, load):
    kept = {}

    def at(offset):
        if xs <= SPAN and not 0 <= offset < xs:
            return None
        if offset not in kept:
            kept[offset] = load(x0 + offset)
        return kept[offset]

    return at


def slopes(xs, p, x0, y0, plane, offset):
    centre = plane(offset)
    here = x0 + offset + REACH
    return (
        combine(lambda k: plane(offset + k), lambda k: plane(offset + 1 - k)),
        combine(
            lambda k: p[here, pl.ds(EDGE + y0 + k, ROWS)],
            lambda k: centre if k == 1 else p[here, pl.ds(EDGE + y0 + 1 - k, ROWS)],
        ),
    )


def prepare_kernel(
    steps, fwd, adj, src, wave, rec, res, _piece,
    fwd_slope, adj_slope, fwd_source, adj_source, ahead, behind, *fields,
):
    xs, ys, zs = fwd_slope.shape[1:]
    for ref, first in ((ahead, 1), (behind, 0)):
        one = band(first, zs)
        ref[:zs] = one
        ref[zs:] = one

    def clear(ref):
        ref[...] = jnp.zeros(ref.shape, jnp.float32)

    for state, (p, v0, v1, v2), slope in (
        (fwd, fields[:4], fwd_slope),
        (adj, fields[4:], adj_slope),
    ):
        for ref in (p, v0):
            clear(ref.at[:REACH])
            clear(ref.at[REACH + xs :])
        for ref in (p.at[pl.ds(REACH, xs)], v1):
            clear(ref.at[:, :EDGE])
            clear(ref.at[:, EDGE + ys :])
        for x in range(xs):
            p[REACH + x, EDGE : EDGE + ys] = state[0, 0, x].astype(jnp.float32)
            v0[REACH + x] = state[0, 1, x].astype(jnp.float32)
            v1[x, EDGE : EDGE + ys] = state[0, 2, x].astype(jnp.float32)
            v2[x] = state[0, 3, x].astype(jnp.float32)

        def block(x0, count, y0, p=p, slope=slope):
            plane = window(xs, x0, lambda x: p[REACH + x, pl.ds(EDGE + y0, ROWS)])
            for offset in range(count):
                for d, values in enumerate(slopes(xs, p, x0, y0, plane, offset)):
                    slope[d, x0 + offset, pl.ds(y0, ROWS)] = values

        blocks(xs, ys, block)
        slope[2] = along_z(p[REACH : REACH + xs, EDGE : EDGE + ys], ahead[...])

    row = lax.broadcasted_iota(jnp.int32, (ys, zs), 0)
    lane = lax.broadcasted_iota(jnp.int32, (ys, zs), 1)
    src_mark = (row == src[0, 1]) & (lane == src[0, 2])
    for x in range(xs):
        rec_mark = (row == rec[0, 0, x]) & (lane == rec[0, 1, x])
        for step in range(steps):
            amplitude = jnp.where(x == src[0, 0], wave[0, step], 0.0)
            fwd_source[step, x] = jnp.where(src_mark, amplitude, 0.0)
            adj_source[step, x] = jnp.where(rec_mark, res[0, step, x], 0.0)


def near_kernel(speed, density, aperture, near_speed, near_density, entry):
    near_speed[...] = speed[...]
    near_density[...] = density[...]
    entry[...] = jnp.full(entry.shape, entry_of(aperture), jnp.int32)


def pick_kernel(chips, near_speed, near_density, far_speed, far_density, *refs):
    stripes = 2 * chips
    lists, outs = refs[:stripes], refs[stripes:]
    held = near_speed.shape[0]
    me = lax.axis_index("tile")
    residue, half = lax.rem(me, stripes), lax.div(me, stripes)
    entries = [entry_of(ref) for ref in lists]
    for hop in range(stripes):
        entry = entries[hop]
        corner, column = lax.div(entry, held), lax.rem(entry, held)
        here = (residue >= corner) == (half == 0)
        piece = outs[hop]

        @pl.when(here)
        def _():
            piece[0] = near_speed[column]
            piece[1] = near_density[column]

        @pl.when(jnp.logical_not(here))
        def _():
            piece[0] = far_speed[column]
            piece[1] = far_density[column]


def gather_order(stripes):
    return [0] + list(range(2, stripes, 2)) + list(range(1, stripes, 2))


def wave_kernel(chips, steps, held, *refs):
    stripes = 2 * chips
    pieces, refs = refs[:stripes], refs[stripes:]
    fwd_slope, adj_slope, fwd_source, adj_source, ahead, behind, entry_ref = refs[:7]
    kept, traded, p, v0, v1, v2, q, w0, w1, w2 = refs[15:25]
    bulk, buoy, dp, dv, bulk_img, buoy_img, across_z, flat = refs[25:]
    tile_x, tile_y = pieces[0].shape[1:3]
    xs, ys, zs = bulk.shape
    residue = lax.rem(lax.axis_index("tile"), stripes)
    entry = entry_of(entry_ref)
    corner = lax.div(entry, held)

    def place_of(hop):
        return lax.rem((residue ^ hop) - corner + stripes, stripes) * tile_x

    for hop, piece in zip(gather_order(stripes), pieces):
        cells = pl.ds(place_of(hop), tile_x)
        speed, density = piece[0], piece[1]
        bulk[cells] = COEF[0] * (density * speed * speed)
        buoy[cells] = COEF[0] / density

    def push(fields, first, note):
        p, v0, v1, v2 = fields
        if first is None:
            across_z[...] = along_z(p[REACH : REACH + xs, EDGE : EDGE + ys], ahead[...])

        def block(x0, count, y0):
            rows, inner = pl.ds(y0, ROWS), pl.ds(EDGE + y0, ROWS)
            plane = window(xs, x0, lambda x: p[REACH + x, inner])
            for offset in range(count):
                x = x0 + offset
                if first is None:
                    two = slopes(xs, p, x0, y0, plane, offset)
                else:
                    two = (first[0, x, rows], first[1, x, rows])
                light = buoy[x, rows]
                changes = (light * two[0], light * two[1])
                moved = (v0[REACH + x, rows] + changes[0], v1[x, inner] + changes[1])
                v0[REACH + x, rows] = moved[0]
                v1[x, inner] = moved[1]
                note(0, x, rows, changes, moved)

        def block_z(x0, count, y0):
            rows = pl.ds(y0, ROWS)
            for x in range(count):
                x = x0 + x
                slope = across_z[x, rows] if first is None else first[2, x, rows]
                change = buoy[x, rows] * slope
                moved = v2[x, rows] + change
                v2[x, rows] = moved
                note(2, x, rows, (change,), (moved,))

        blocks(xs, ys, block)
        blocks(xs, ys, block_z)

    def spread(fields, source, step, note):
        p, v0, v1, v2 = fields
        across_z[...] = along_z(v2[...], behind[...])

        def block(x0, count, y0):
            rows = pl.ds(y0, ROWS)
            plane = window(xs, x0, lambda x: v0[REACH + x, rows])
            for offset in range(count):
                x = x0 + offset
                along_x = combine(lambda k: plane(offset + k - 1), lambda k: plane(offset - k))
                along_y = combine(
                    lambda k: v1[x, pl.ds(EDGE + y0 + k - 1, ROWS)],
                    lambda k: v1[x, pl.ds(EDGE + y0 - k, ROWS)],
                )
                flat[x, rows] = along_x + along_y

        def block_z(x0, count, y0):
            rows, inner = pl.ds(y0, ROWS), pl.ds(EDGE + y0, ROWS)
            for x in range(count):
                x = x0 + x
                change = bulk[x, rows] * (flat[x, rows] + across_z[x, rows])
                change = change + source[step, x, rows]
                moved = p[REACH + x, inner] + change
                p[REACH + x, inner] = moved
                note(x, rows, change, moved)

        blocks(xs, ys, block)
        blocks(xs, ys, block_z)

    fields = (p, v0, v1, v2)
    for step in range(steps):

        def keep_dv(first, x, rows, changes, moved, step=step):
            for d, change in enumerate(changes, first):
                dv[step, d, x, rows] = change

        def keep_dp(x, rows, change, moved, step=step):
            dp[step, x, rows] = change

        push(fields, fwd_slope if step == 0 else None, keep_dv)
        spread(fields, fwd_source, step, keep_dp)

    fields = (q, w0, w1, w2)
    for step in reversed(range(steps)):
        last = step == steps - 1

        def add_buoy(first, x, rows, changes, moved, step=step, last=last):
            image = None if last and first == 0 else buoy_img[x, rows]
            for d, values in enumerate(moved, first):
                product = dv[step, d, x, rows] * values
                image = product if image is None else image + product
            buoy_img[x, rows] = image

        def add_bulk(x, rows, change, moved, step=step, last=last):
            image = dp[step, x, rows] * moved
            bulk_img[x, rows] = image if last else bulk_img[x, rows] + image

        push(fields, adj_slope if last else None, add_buoy)
        spread(fields, adj_source, step, add_bulk)

    tile_rows = tile_x * tile_y
    for chip in range(chips):
        for ref, hop in ((kept, 2 * chip), (traded, 2 * chip + 1)):
            cells = pl.ds(place_of(hop), tile_x)
            ref[chip, :tile_rows] = bulk_img[cells].reshape(tile_rows, zs)
            ref[chip, tile_rows : 2 * tile_rows] = buoy_img[cells].reshape(tile_rows, zs)
            ref[chip, 2 * tile_rows :] = jnp.full((8, zs), entry).astype(jnp.float32)


def return_order(chips):
    even = [chips] + list(range(1, chips)) + list(range(chips + 1, 2 * chips))
    return list(zip(even, reversed(even)))


def merge_kernel(chips, kept, came, *outs):
    rows = kept.shape[1] - 8
    odd = lax.rem(lax.axis_index("tile"), 2) == 1
    for out, (even_hop, odd_hop) in zip(outs, [(0, 0)] + return_order(chips)):
        chip = jnp.where(odd, odd_hop % chips, even_hop % chips)
        for shot, source in enumerate((kept, came)):
            out[shot * rows : (shot + 1) * rows] = source[chip, :rows]
            first = 2 * rows + 4 * shot
            out[first : first + 4] = source[chip, rows : rows + 4]


def add_kernel(chips, groups, held, *refs):
    came, parts, total = refs[: 2 * chips], refs[2 * chips : 2 * chips + groups], refs[-1]
    stripes = 2 * chips
    me, group = lax.axis_index("tile"), lax.axis_index("grp")
    tile_rows = total.shape[1] // (held + 1)
    part = parts[0].shape[1]
    slots = []
    for pair in came:
        for shot in range(2):
            first = 4 * tile_rows + 4 * shot
            entry = jnp.max(pair[first : first + 1, :1]).astype(jnp.int32)
            corner, column = lax.div(entry, held), lax.rem(entry, held)
            mine = (corner <= me) & (me < corner + stripes)
            slots.append(jnp.where(mine, column, held))
    total[...] = jnp.zeros_like(total)
    for index, pair in enumerate(came):
        for shot in range(2):
            slot = slots[2 * index + shot]
            rows = pl.ds(pl.multiple_of(slot * tile_rows, tile_rows), tile_rows)
            for field in range(2):
                first = (2 * shot + field) * tile_rows
                total[field, rows] = total[field, rows] + pair[first : first + tile_rows]
    for index, hop in enumerate([0] + far_first(groups)):
        first = pl.multiple_of((group ^ hop) * part, part)
        for field in range(2):
            parts[index][field] = total[field, pl.ds(first, part)]


def far_first(groups):
    return list(range(groups - 1, 0, -1))


def grads_kernel(scale, groups, *refs):
    parts, speed_ref, density_ref, grads = refs[:groups], *refs[groups:]
    part = parts[0].shape[1]
    rows = pl.ds(pl.multiple_of(lax.axis_index("grp") * part, part), part)
    speed, density = speed_ref[rows], density_ref[rows]
    bulk_sum, buoy_sum = parts[0][0], parts[0][1]
    for other in parts[1:]:
        bulk_sum = bulk_sum + other[0]
        buoy_sum = buoy_sum + other[1]
    grads[0] = scale * (bulk_sum * (2.0 * density * speed))
    grads[1] = scale * (bulk_sum * (speed * speed) - buoy_sum / (density * density))


def per_device(speed, density, fwd_state, adj_state, aperture, src_pos, wavelet, rec_pos, residual):
    owners = lax.axis_size("tile")
    groups = lax.axis_size("grp")
    my_group = lax.axis_index("grp")
    held, tile_x, tile_y, depth = speed.shape
    stripes = aperture.shape[1]
    chips = stripes // 2
    steps = wavelet.shape[1]
    xs = stripes * tile_x
    f32 = jnp.float32
    cells = (xs, tile_y, depth)

    def shape(*dims):
        return jax.ShapeDtypeStruct(dims, f32)

    def across(values, hop):
        return lax.ppermute(values, "tile", [(t, t ^ hop) for t in range(owners)])

    far_speed = across(speed, stripes)
    far_density = across(density, stripes)
    lists = {hop: across(aperture, hop) for hop in range(stripes - 1, 0, -1)}
    four = [
        (xs + 2 * REACH, tile_y + 2 * EDGE, depth),
        (xs + 2 * REACH, tile_y, depth),
        (xs, tile_y + 2 * EDGE, depth),
        cells,
    ]
    near_speed, near_density, entry = pl.pallas_call(
        near_kernel,
        out_shape=[
            shape(*speed.shape),
            shape(*speed.shape),
            jax.ShapeDtypeStruct((8, depth), jnp.int32),
        ],
        in_specs=[VMEM] * 3,
        out_specs=[VMEM] * 3,
        compiler_params=PARAMS,
        cost_estimate=pl.CostEstimate(flops=4_000_000, bytes_accessed=6_000_000, transcendentals=0),
        name="hold_near_tiles",
    )(speed, density, aperture)
    pieces = pl.pallas_call(
        functools.partial(pick_kernel, chips),
        out_shape=[shape(2, tile_x, tile_y, depth)] * stripes,
        in_specs=[VMEM] * (4 + stripes),
        out_specs=[VMEM] * stripes,
        compiler_params=PARAMS,
        name="pick_tiles",
    )(near_speed, near_density, far_speed, far_density, entry, *[lists[h] for h in range(1, stripes)])

    prepared = pl.pallas_call(
        functools.partial(prepare_kernel, steps),
        out_shape=[shape(3, *cells)] * 2
        + [shape(steps, *cells)] * 2
        + [jax.ShapeDtypeStruct((2 * depth, 2 * depth), jnp.bfloat16)] * 2
        + [shape(*dims) for dims in four + four],
        in_specs=[VMEM] * 2 + [SMEM] * 4 + [VMEM],
        out_specs=[VMEM] * 14,
        compiler_params=PARAMS,
        cost_estimate=pl.CostEstimate(flops=4_000_000, bytes_accessed=6_000_000, transcendentals=0),
        name="prepare",
    )(fwd_state, adj_state, src_pos, wavelet, jnp.swapaxes(rec_pos, 1, 2), residual, pieces[0])
    prepared, fields = prepared[:6], prepared[6:]
    pieces = [across(pieces[hop], hop) if hop else pieces[0] for hop in gather_order(stripes)]

    tile_rows = tile_x * tile_y
    sent = shape(chips, 2 * tile_rows + 8, depth)
    kept, traded, *_ = pl.pallas_call(
        functools.partial(wave_kernel, chips, steps, held),
        out_shape=[sent, sent] + [shape(*dims) for dims in four + four],
        in_specs=[VMEM] * (stripes + 15),
        out_specs=[VMEM] * 10,
        scratch_shapes=[
            pltpu.VMEM(cells, f32),
            pltpu.VMEM(cells, f32),
            pltpu.VMEM((steps,) + cells, f32),
            pltpu.VMEM((steps, 3) + cells, f32),
        ]
        + [pltpu.VMEM(cells, f32)] * 4
        + [
        ],
        input_output_aliases={stripes + 7 + index: 2 + index for index in range(8)},
        compiler_params=PARAMS,
        name="replay_and_adjoint",
    )(*pieces, *prepared, entry, *fields)

    both = shape(4 * tile_rows + 8, depth)
    stacks = pl.pallas_call(
        functools.partial(merge_kernel, chips),
        out_shape=[both] * stripes,
        in_specs=[VMEM] * 2,
        out_specs=[VMEM] * stripes,
        compiler_params=PARAMS,
        name="merge_pair",
    )(kept, across(traded, 1))
    came = [
        lax.ppermute(values, "tile", [(t, t ^ (2 * hops[t % 2])) for t in range(owners)])
        for values, hops in zip(stacks[1:], return_order(chips))
    ]
    came = came[-1:] + came[:-1]

    rows = held * tile_rows
    part = rows // groups
    part_shape = shape(2, part, depth)
    parts = pl.pallas_call(
        functools.partial(add_kernel, chips, groups, held),
        out_shape=[part_shape] * groups,
        in_specs=[VMEM] * stripes,
        out_specs=[VMEM] * groups,
        scratch_shapes=[pltpu.VMEM((2, rows + tile_rows, depth), f32)],
        compiler_params=PARAMS,
        name="add_stripes",
    )(stacks[0], *came)

    def along(values, hop):
        return lax.ppermute(values, "grp", [(g, g ^ hop) for g in range(groups)])

    parts = [parts[0]] + [along(values, hop) for values, hop in zip(parts[1:], far_first(groups))]
    grads = pl.pallas_call(
        functools.partial(grads_kernel, 1.0 / math.sqrt(groups * owners), groups),
        out_shape=part_shape,
        in_specs=[VMEM] * (groups + 2),
        out_specs=VMEM,
        compiler_params=PARAMS,
        name="gradients",
    )(*parts, near_speed.reshape(rows, depth), near_density.reshape(rows, depth))

    whole = jnp.zeros((2, groups, part, depth), f32)
    for hop in range(groups):
        values = grads
        if hop:
            values = lax.ppermute(grads, "grp", [(g, (g + hop) % groups) for g in range(groups)])
        place = lax.rem(my_group - hop + groups, groups)
        whole = lax.dynamic_update_slice_in_dim(whole, values[:, None], place, axis=1)
    return (whole[0].reshape(speed.shape), whole[1].reshape(speed.shape))


def solution(mesh):
    return jax.shard_map(
        per_device,
        mesh=mesh,
        in_specs=(
            P("tile", None, None, None),
            P("tile", None, None, None),
            P(("grp", "tile"), None, None, None, None),
            P(("grp", "tile"), None, None, None, None),
            P(("grp", "tile"), None),
            P(("grp", "tile"), None),
            P(("grp", "tile"), None),
            P(("grp", "tile"), None, None),
            P(("grp", "tile"), None, None),
        ),
        out_specs=(P("tile", None, None, None), P("tile", None, None, None)),
        check_vma=False,
    )
```
